32 devices in a mesh: seq: 2 (over y), seg: 16 (over z, x, core).
Axes of the slice: x: 2, y: 2, z: 4, core: 2. Of those that a mesh axis runs over, the one named last changes fastest.
Arguments:
- tokens: bfloat16 [32, 512, 512], P('seg', 'seq'), may hold values from -6 to 6
- memory: bfloat16 [32, 64, 512], P('seg', 'seq'), may hold values from -6 to 6
- lengths: int32 [32, 8], P('seg'), may hold values from 1 to 384, 512 in all within a row
- attn_gain: float32 [512], replicated, may hold values from 0.25 to 1.75
- query_weight: bfloat16 [512, 512], replicated, may hold values from -0.25 to 0.25
- pair_weight: bfloat16 [512, 1024], replicated, may hold values from -0.25 to 0.25
- out_weight: bfloat16 [512, 512], replicated, may hold values from -0.75 to 0.75
- ffn_gain: float32 [512], replicated, may hold values from 0.25 to 1.75
- ffn_in: bfloat16 [512, 2048], replicated, may hold values from -0.25 to 0.25
- ffn_out: bfloat16 [2048, 512], replicated, may hold values from -0.125 to 0.125
- write_query: bfloat16 [512, 512], replicated, may hold values from -0.25 to 0.25
- write_pair: bfloat16 [512, 1024], replicated, may hold values from -0.25 to 0.25
- write_out: bfloat16 [512, 512], replicated, may hold values from -1 to 1
- write_gate: bfloat16 [512, 512], replicated, may hold values from -0.25 to 0.25
- write_gain: float32 [512], replicated, may hold values from 0.25 to 1.75
- out_cotangent: bfloat16 [32, 512, 512], P('seg', 'seq'), may hold values from -6 to 6
- memory_cotangent: bfloat16 [32, 64, 512], P('seg', 'seq'), may hold values from -6 to 6
Outputs:
- out: bfloat16 [32, 512, 512], P('seg', 'seq')
- new_memory: bfloat16 [32, 64, 512], P('seg', 'seq')
- grad_tokens: float32 [32, 512, 512], P('seg', 'seq')
- grad_memory: float32 [32, 64, 512], P('seg', 'seq')
- grad_attn_gain: float32 [512], P('seg')
- grad_query_weight: float32 [512, 512], P('seg')
- grad_pair_weight: float32 [512, 1024], P('seg')
- grad_out_weight: float32 [512, 512], P('seg')
- grad_ffn_gain: float32 [512], P('seg')
- grad_ffn_in: float32 [512, 2048], P('seg')
- grad_ffn_out: float32 [2048, 512], P('seg')
- grad_write_query: float32 [512, 512], P('seg')
- grad_write_pair: float32 [512, 1024], P('seg')
- grad_write_out: float32 [512, 512], P('seg')
- grad_write_gate: float32 [512, 512], P('seg')
- grad_write_gain: float32 [512], P('seg')
The draws below stay inside these ranges and needn't reach their ends.
Inputs may be any that keep to these rules, and one draw needn't show every extreme that they name: Each segment's 8 lengths sum to 512, and its longest document has exactly 384 tokens.
All inputs are finite; a program needn't handle non-finite values.
Results may differ from the reference program's by a relative error of at most 0.03.
Values may be sent and summed in bfloat16 or wider, within the bound.
No kernel may reach another device: no remote copies, remote signals or barrier semaphores. Data moves between devices by JAX's collectives and lax.ppermute only.
A program may use at most 128 MiB of HBM per device.

```python
import math
import jax
import jax.numpy as jnp
import numpy as np
from jax import lax

D = 512
H = 8
HD = 64
FF = 2048
M = 64
SEG = 512
DOCS = 8
SEGS = 32


def levels(rng, extent, pieces, least, top_value):
    level, own = 1.0, jax.random.fold_in(rng, 6)
    for dim, parts in pieces:
        heights = jnp.exp(jax.random.uniform(jax.random.fold_in(own, dim), (parts,), jnp.float32, least / len(pieces), top_value / len(pieces)))
        level = level * jnp.repeat(heights, extent[dim] // parts).reshape([-1 if axis == dim else 1 for axis in range(len(extent))])
    return level


def length_profile(number_of, total, limit, slope):
    loads = [(1 << 20) // math.isqrt(rank ** slope) + 1 for rank in range(2, number_of + 1)]
    spare, holding = total - limit - (number_of - 1), [1] * (number_of - 1)
    while spare > 0:
        free = [i for i in range(number_of - 1) if holding[i] < limit]
        whole, left = sum([loads[i] for i in free]), spare
        for i in free:
            extra = min(limit - holding[i], max(1, left * loads[i] // whole), spare)
            holding[i] = holding[i] + extra
            spare = spare - extra
    return np.array([limit] + holding)


def uneven(stream_key, amount, total, most, slope):
    if amount == 2:
        one = jax.random.randint(stream_key, (), max(1, total - most), min(most, total - 1) + 1)
        return jnp.stack([one, total - one])
    tallies = jnp.asarray(length_profile(amount, total, most, slope), jnp.int32)
    pairs = (amount - 1) // 2
    giver, receiver = tallies[1:1 + 2 * pairs:2], tallies[2:2 + 2 * pairs:2]
    margin = jnp.minimum(giver - 1, most - receiver)
    passed = jax.random.randint(jax.random.fold_in(stream_key, 1), (pairs,), 0, 1 << 20) % (margin + 1)
    tallies = tallies.at[1:1 + 2 * pairs:2].set(giver - passed).at[2:2 + 2 * pairs:2].set(receiver + passed)
    return tallies[jax.random.permutation(jax.random.fold_in(stream_key, 2), amount)]


def normal_values(own_key, extent, deviation, reach, pieces=(), kind=jnp.bfloat16):
    factor_of = levels(own_key, extent, pieces, -0.22, 0.18) if pieces else 1.0
    array = jax.random.normal(own_key, extent, jnp.float32) * deviation * factor_of
    return jnp.minimum(jnp.maximum(array, -reach), reach).astype(kind)


def setup_inputs(seed: int = 0) -> dict:
    streams_of = jax.random.split(jax.random.key(seed), 18)
    return {
        "tokens": normal_values(streams_of[0], (SEGS, SEG, D), 1.0, 6.0, ((0, 16), (1, 2))),
        "memory": normal_values(streams_of[1], (SEGS, M, D), 1.0, 6.0, ((0, 16), (1, 2))),
        "lengths": jax.vmap(lambda own: uneven(own, DOCS, SEG, 3 * SEG // 4, 2))(jax.random.split(streams_of[2], SEGS)).reshape((SEGS, DOCS)).astype(jnp.int32),
        "attn_gain": jnp.clip(1.0 + 0.15 * jax.random.normal(streams_of[3], (D,), jnp.float32), 0.25, 1.75),
        "query_weight": normal_values(streams_of[4], (D, D), D ** -0.5, 0.25),
        "pair_weight": normal_values(streams_of[5], (D, 2 * D), D ** -0.5, 0.25),
        "out_weight": normal_values(streams_of[6], (D, D), (D // 8) ** -0.5, 0.75),
        "ffn_gain": jnp.clip(1.0 + 0.15 * jax.random.normal(streams_of[7], (D,), jnp.float32), 0.25, 1.75),
        "ffn_in": normal_values(streams_of[8], (D, FF), D ** -0.5, 0.25),
        "ffn_out": normal_values(streams_of[9], (FF, D), FF ** -0.5, 0.125),
        "write_query": normal_values(streams_of[10], (D, D), D ** -0.5, 0.25),
        "write_pair": normal_values(streams_of[11], (D, 2 * D), D ** -0.5, 0.25),
        "write_out": normal_values(streams_of[12], (D, D), (D // 16) ** -0.5, 1.0),
        "write_gate": normal_values(streams_of[13], (D, D), D ** -0.5, 0.25),
        "write_gain": jnp.clip(1.0 + 0.15 * jax.random.normal(streams_of[14], (D,), jnp.float32), 0.25, 1.75),
        "out_cotangent": normal_values(streams_of[15], (SEGS, SEG, D), 1.0, 6.0, ((0, 16), (1, 2))),
        "memory_cotangent": normal_values(streams_of[16], (SEGS, M, D), 1.0, 6.0, ((0, 16), (1, 2))),
    }


@jax.custom_vjp
def low(v):
    return lax.optimization_barrier(v.astype(jnp.bfloat16)).astype(jnp.float32)

@jax.custom_vjp
def reduced_backward(v):
    return v

def low_keep(v):
    return (low(v), None)

def low_pass(kept, grad):
    return (grad,)

def back_keep(v):
    return (v, None)

def back_low(kept, grad):
    return (low(grad),)
low.defvjp(low_keep, low_pass)
reduced_backward.defvjp(back_keep, back_low)
EPSILON = 1e-05
MASKED_SCORE = -1e+30
FULL_PRECISION = lax.Precision.HIGHEST

def norm_rows(values, scales):
    average = lax.optimization_barrier(jnp.mean(values, -1, keepdims=True))
    centred = values - average
    spread = lax.optimization_barrier(jnp.mean(centred * centred, -1, keepdims=True))
    return centred * lax.rsqrt(spread + EPSILON) * scales

def product(left, right):
    return jnp.dot(left, right, precision=FULL_PRECISION)

def divide_into_heads(values):
    return values.reshape(values.shape[0], H, values.shape[1] // H)

def segment(seg_tokens, seg_memory, seg_docs, attn_gain, query_weight, pair_weight, out_weight, ffn_gain, ffn_in, ffn_out, write_query, write_pair, write_out, write_gate, write_gain):
    seg_len = seg_tokens.shape[0]
    memory_entries = seg_memory.shape[0]
    hidden_width = seg_tokens.shape[1]
    score_scale = HD ** (-0.5)
    normed_x = low(norm_rows(seg_tokens, attn_gain))
    normed_m = low(norm_rows(seg_memory, attn_gain))
    query = reduced_backward(low(product(normed_x, query_weight)))
    pair_x = reduced_backward(low(product(normed_x, pair_weight)))
    pair_m = reduced_backward(low(product(normed_m, pair_weight)))
    pairs = jnp.concatenate([pair_m, pair_x], 0)
    keys = divide_into_heads(pairs[:, :hidden_width])
    values = divide_into_heads(pairs[:, hidden_width:])
    scores = reduced_backward(jnp.einsum('ihd,jhd->hij', divide_into_heads(query), keys, precision=FULL_PRECISION) * score_scale)
    positions = jnp.arange(seg_len, dtype=jnp.int32)
    token_ok = (positions[None, :] <= positions[:, None]) & (seg_docs[None, :] == seg_docs[:, None])
    allowed = jnp.concatenate([jnp.ones((seg_len, memory_entries), dtype=bool), token_ok], 1)
    masked = jnp.where(allowed[None], scores, MASKED_SCORE)
    probs = low(jax.nn.softmax(masked, -1))
    mixed = jnp.einsum('hij,jhd->ihd', probs, values, precision=FULL_PRECISION).reshape(seg_len, hidden_width)
    mixed = reduced_backward(low(mixed))
    resid = seg_tokens + reduced_backward(product(mixed, out_weight))
    normed2 = low(norm_rows(resid, ffn_gain))
    inner = reduced_backward(product(normed2, ffn_in))
    act = reduced_backward(low(jax.nn.gelu(inner)))
    result = resid + reduced_backward(product(act, ffn_out))
    out_low = low(result)
    writer_query_weight = reduced_backward(low(product(normed_m, write_query)))
    writer_pair_weight = reduced_backward(low(product(out_low, write_pair)))
    writer_score_matrix = reduced_backward(jnp.einsum('tyi,qyi->ytq', divide_into_heads(writer_query_weight), divide_into_heads(writer_pair_weight[:, :hidden_width]), precision=FULL_PRECISION) * score_scale)
    writer_probabilities = low(jax.nn.softmax(writer_score_matrix, -1))
    writer_mixed_heads = jnp.einsum('ucb,buq->cuq', writer_probabilities, divide_into_heads(writer_pair_weight[:, hidden_width:]), precision=FULL_PRECISION).reshape(memory_entries, hidden_width)
    writer_mixed_heads = reduced_backward(low(writer_mixed_heads))
    update = reduced_backward(product(writer_mixed_heads, write_out))
    gate = jax.nn.sigmoid(reduced_backward(product(low(update), write_gate)))
    written = norm_rows(seg_memory + gate * update, write_gain)
    return (out_low, written)

def reference(tokens, memory, lengths, attn_gain, query_weight, pair_weight, out_weight, ffn_gain, ffn_in, ffn_out, write_query, write_pair, write_out, write_gate, write_gain, out_cotangent, memory_cotangent):
    bounds = jnp.cumsum(lengths, axis=1).astype(jnp.int32)
    positions = jnp.arange(SEG, dtype=jnp.int32)
    seg_docs = lax.optimization_barrier(jnp.sum((positions[None, :, None] >= bounds[:, None, :]).astype(jnp.int32), -1)).astype(jnp.int32)
    weights = (attn_gain, query_weight, pair_weight, out_weight, ffn_gain, ffn_in, ffn_out, write_query, write_pair, write_out, write_gate, write_gain)
    weights = tuple((w.astype(jnp.float32) for w in weights))

    def forward(tok_float, mem_float, *params):
        step = jax.checkpoint(lambda items: segment(items[0], items[1], items[2], *params))
        return lax.map(step, (tok_float, mem_float, seg_docs))
    outputs, pull = jax.vjp(forward, tokens.astype(jnp.float32), memory.astype(jnp.float32), *weights)
    grads = pull((out_cotangent.astype(jnp.float32), memory_cotangent.astype(jnp.float32)))
    return (outputs[0].astype(jnp.bfloat16), outputs[1].astype(jnp.bfloat16), grads[0], grads[1], grads[2], grads[3], grads[4], grads[5], grads[6], grads[7], grads[8], grads[9], grads[10], grads[11], grads[12], grads[13])
```

```python
import functools

import jax
import jax.numpy as jnp
from jax import lax
from jax.experimental import pallas as pl
from jax.experimental.pallas import tpu as pltpu
from jax.sharding import PartitionSpec as P

H = 8
GROUPS = 16
EPSILON = 1e-05
MASKED = -1e30
F32 = jnp.float32
BF16 = jnp.bfloat16
VMEM_LIMIT = 56 * 1024 * 1024


def dot(a, b, ca=1, cb=0):
    return lax.dot_general(a, b, (((ca,), (cb,)), ((), ())), preferred_element_type=F32)


def norm_parts(v):
    centred = v - jnp.mean(v, -1, keepdims=True)
    r = lax.rsqrt(jnp.mean(centred * centred, -1, keepdims=True) + EPSILON)
    return centred * r, r


def norm_back(dy, xhat, r, gain):
    dx = dy * gain
    m1 = jnp.mean(dx, -1, keepdims=True)
    m2 = jnp.mean(dx * xhat, -1, keepdims=True)
    return r * (dx - m1 - xhat * m2), jnp.sum(dy * xhat, 0, keepdims=True)


def whole_rows(pair_ref, recv_ref, start, half, y, dst_ref):
    own = pl.multiple_of(y * half, half)
    other = pl.multiple_of((1 - y) * half, half)
    dst_ref[pl.ds(own, half), :] = pair_ref[y].astype(dst_ref.dtype)
    dst_ref[pl.ds(other, half), :] = recv_ref[start : start + half, :].astype(dst_ref.dtype)


def emit(grad, keep_ref, send_ref, offset, c):
    rows = grad.shape[0] // GROUPS
    g = grad.reshape(GROUPS // 2, 2, rows, grad.shape[1])
    zero, one = g[:, 0], g[:, 1]
    first = c == 0
    keep_ref[:, offset : offset + rows, :] = jnp.where(first, zero, one).astype(BF16)
    send_ref[:, offset : offset + rows, :] = jnp.where(first, one, zero).astype(BF16)


def lane_low(shape):
    return lax.broadcasted_iota(jnp.int32, shape, 1) < 64


def stacked_heads(block):
    low = lane_low(block.shape)
    zero = jnp.zeros_like(block)
    return jnp.concatenate([jnp.where(low, block, zero), jnp.where(low, zero, block)], 0)


def unstacked_heads(block):
    rows = block.shape[0] // 2
    top, bottom = block[:rows], block[rows:]
    return jnp.where(lane_low(top.shape), top, bottom)


def forward_kernel(
    place, lengths, tokens, memory, recv, attn_gain, query_weight, pair_weight, out_weight,
    ffn_gain, ffn_in, ffn_out, write_query,
    x_ref, mem_ref, nall_ref, qs_ref, kall_ref, vall_ref, p0, p1, p2, p3,
    mixed_ref, resid_ref, n2_ref, act_ref, dg_ref, out_ref, send_ref, wqs_ref,
):
    y = place[0]
    half, width = tokens.shape[1], tokens.shape[2]
    mhalf = memory.shape[1]
    slots = 2 * mhalf
    whole_rows(tokens, recv, 0, half, y, x_ref)
    whole_rows(memory, recv, half, mhalf, y, mem_ref)
    gain = attn_gain[...]
    xhat, _ = norm_parts(x_ref[...])
    nx = (xhat * gain).astype(BF16)
    mhat, _ = norm_parts(mem_ref[...])
    nm = (mhat * gain).astype(BF16)
    nall_ref[0:slots, :] = nm
    nall_ref[slots:128, :] = jnp.zeros((128 - slots, width), BF16)
    nall_ref[128:, :] = nx
    qs_ref[...] = (dot(nx, query_weight[...]) * 0.125).astype(BF16)
    nall = nall_ref[...]
    kall_ref[...] = dot(nall, pair_weight[:, :width]).astype(BF16)
    vall_ref[...] = dot(nall, pair_weight[:, width:]).astype(BF16)
    wqs_ref[...] = (dot(nm, write_query[...]) * 0.125).astype(BF16)
    bounds = []
    total = 0
    for k in range(lengths.shape[1]):
        total = total + lengths[y, k]
        bounds.append(total)
    rows = 2 * half
    pos_c = lax.broadcasted_iota(jnp.int32, (1, rows), 1)
    doc_c = sum([(pos_c >= b).astype(jnp.int32) for b in bounds])
    mem_bias = jnp.where(
        lax.broadcasted_iota(jnp.int32, (128, 128), 1) < slots, 0.0, MASKED
    ).astype(F32)
    for i, p_ref in enumerate((p0, p1, p2, p3)):
        w = 128 * (i + 2)
        cols = w - 128
        pos_r = lax.broadcasted_iota(jnp.int32, (128, 1), 0) + 128 * i
        doc_r = sum([(pos_r >= b).astype(jnp.int32) for b in bounds])
        ok = (doc_r == doc_c[:, :cols]) & (pos_c[:, :cols] <= pos_r)
        bias = jnp.concatenate([mem_bias, jnp.where(ok, 0.0, MASKED).astype(F32)], 1)
        for p in range(H // 2):
            lanes = slice(128 * p, 128 * p + 128)
            q01 = stacked_heads(qs_ref[128 * i : 128 * i + 128, lanes])
            s = dot(q01, kall_ref[0:w, lanes], 1, 1)
            s = (s.reshape(2, 128, w) + bias[None]).reshape(256, w)
            e = jnp.exp(s - jnp.max(s, -1, keepdims=True))
            pr = (e * (1.0 / jnp.sum(e, -1, keepdims=True))).astype(BF16)
            p_ref[p] = pr
            o = dot(pr, vall_ref[0:w, lanes])
            mixed_ref[128 * i : 128 * i + 128, lanes] = unstacked_heads(o).astype(BF16)
    resid = x_ref[...] + dot(mixed_ref[...], out_weight[...])
    resid_ref[...] = resid
    rhat, _ = norm_parts(resid)
    n2 = (rhat * ffn_gain[...]).astype(BF16)
    n2_ref[...] = n2
    ff = ffn_in.shape[1]
    k0 = 0.7978845608028654
    for j in range(ff // 512):
        cols = slice(512 * j, 512 * j + 512)
        v = dot(n2, ffn_in[:, cols])
        v2 = v * v
        t = jnp.tanh(k0 * (v + 0.044715 * (v2 * v)))
        h = 0.5 * (1.0 + t)
        act_ref[:, cols] = (v * h).astype(BF16)
        dg = h + (0.5 * v) * (1.0 - t * t) * (k0 + (3.0 * 0.044715 * k0) * v2)
        dg_ref[:, cols] = dg.astype(BF16)
    out = (resid_ref[...] + dot(act_ref[...], ffn_out[...])).astype(BF16)
    out_ref[...] = out
    send_ref[...] = out_ref[pl.ds(pl.multiple_of((1 - y) * half, half), half), :]


def head_mask(rows_per, width):
    shape = (H * rows_per, width)
    row_head = lax.broadcasted_iota(jnp.int32, shape, 0) // rows_per
    col_head = lax.broadcasted_iota(jnp.int32, shape, 1) // (width // H)
    return row_head == col_head


def block_diagonal(v, mask):
    return jnp.where(mask, jnp.concatenate([v] * H, 0), jnp.zeros((), v.dtype))


def diagonal_blocks(v, mask):
    rows = v.shape[0] // H
    v = jnp.where(mask, v, 0.0)
    return jnp.sum(v.reshape(H, rows, v.shape[1]), 0)


def write_kernel(
    place, out, wqs, mem, nall, memory_cotangent, recv, write_pair, write_out, write_gate,
    write_gain,
    keep_ref, send_ref, dwpair_ref, dwquery_ref, dblend_ref, newmem_ref, gain_ref, mc_ref,
):
    y, c = place[0], place[1]
    slots, width = wqs.shape
    mhalf = slots // 2
    whole_rows(memory_cotangent, recv, recv.shape[0] - mhalf, mhalf, y, mc_ref)
    o = out[...]
    wk = dot(o, write_pair[:, :width]).astype(BF16)
    wv = dot(o, write_pair[:, width:]).astype(BF16)
    mask = head_mask(slots, width)
    qbd = block_diagonal(wqs[...], mask)
    s = dot(qbd, wk, 1, 1)
    e = jnp.exp(s - jnp.max(s, -1, keepdims=True))
    pf = e * (1.0 / jnp.sum(e, -1, keepdims=True))
    pb = pf.astype(BF16)
    wmixed = diagonal_blocks(dot(pb, wv), mask).astype(BF16)
    update = dot(wmixed, write_out[...])
    update_low = update.astype(BF16)
    gate = jax.nn.sigmoid(dot(update_low, write_gate[...]))
    blended = mem[...] + gate * update
    bhat, br = norm_parts(blended)
    newmem_ref[...] = (bhat * write_gain[...]).astype(BF16)
    d_blend, d_gain = norm_back(mc_ref[...], bhat, br, write_gain[...])
    gain_ref[...] = d_gain
    dblend_ref[...] = d_blend
    d_gate_pre = (d_blend * update * gate * (1.0 - gate)).astype(BF16)
    d_update = (d_blend * gate + dot(d_gate_pre, write_gate[...], 1, 1)).astype(BF16)
    d_wmixed = dot(d_update, write_out[...], 1, 1).astype(BF16)
    emit(dot(update_low, d_gate_pre, 0, 0), keep_ref, send_ref, 128, c)
    emit(dot(wmixed, d_update, 0, 0), keep_ref, send_ref, 96, c)
    dbd = block_diagonal(d_wmixed, mask)
    dp = dot(dbd, wv, 1, 1)
    row = jnp.sum(pf * dp, -1, keepdims=True)
    ds = (pf * (dp - row)).astype(BF16)
    d_wquery = (diagonal_blocks(dot(ds, wk), mask) * 0.125).astype(BF16)
    dwquery_ref[...] = d_wquery
    dwk = dot(ds, qbd, 0, 0).astype(BF16)
    dwv = dot(pb, dbd, 0, 0).astype(BF16)
    dwpair_ref[:, :width] = dwk
    dwpair_ref[:, width:] = dwv
    emit(dot(nall[0:slots, :], d_wquery, 0, 0), keep_ref, send_ref, 0, c)
    emit(dot(o, dwk, 0, 0), keep_ref, send_ref, 32, c)
    emit(dot(o, dwv, 0, 0), keep_ref, send_ref, 64, c)


def ffn_back_kernel(
    place, dwpair, out_cotangent, recv, write_pair, act, dg, n2, resid, ffn_in, ffn_out, ffn_gain,
    keep_ref, send_ref, dresid_ref, gain_ref, dout_ref,
):
    y, c = place[0], place[1]
    half, width = out_cotangent.shape[1:]
    ff = ffn_in.shape[1]
    whole_rows(out_cotangent, recv, 0, half, y, dout_ref)
    d_out = dout_ref[...] + dot(dwpair[...], write_pair[...], 1, 1)
    dout_ref[...] = d_out
    d_branch = d_out.astype(BF16)
    rows = width // GROUPS
    deep = ff // GROUPS
    base = (ff // 512) * rows
    n2v = n2[...]
    total = None
    for j in range(ff // 512):
        cols = slice(512 * j, 512 * j + 512)
        d_act = dot(d_branch, ffn_out[cols, :], 1, 1).astype(BF16)
        d_inner = (d_act.astype(F32) * dg[:, cols].astype(F32)).astype(BF16)
        term = dot(d_inner, ffn_in[:, cols], 1, 1)
        total = term if total is None else total + term
        emit(dot(n2v, d_inner, 0, 0), keep_ref, send_ref, rows * j, c)
        grad = dot(act[:, cols], d_branch, 0, 0)
        g = grad.reshape(512 // (2 * deep), 2, deep, width)
        first = c == 0
        per = 512 // (2 * deep)
        keep_ref[per * j : per * (j + 1), base : base + deep, :] = jnp.where(
            first, g[:, 0], g[:, 1]
        ).astype(BF16)
        send_ref[per * j : per * (j + 1), base : base + deep, :] = jnp.where(
            first, g[:, 1], g[:, 0]
        ).astype(BF16)
    rhat, rr = norm_parts(resid[...])
    d_norm, d_gain = norm_back(total, rhat, rr, ffn_gain[...])
    gain_ref[...] = d_gain
    dresid_ref[...] = dout_ref[...] + d_norm


def attn_back_kernel(
    place, dresid, mixed, out_weight, qs, kall, vall, p0, p1, p2, p3, nall, x, mem, attn_gain,
    query_weight, pair_weight, write_query, dwquery, dblend, newmem, gain2, gain3,
    keep_ref, send_ref, own_tok_ref, own_mem_ref, own_new_ref, swap_ref,
    dk_ref, dv_ref, dm_ref, dq_ref, tok_ref, gmem_ref,
):
    y, c = place[0], place[1]
    width = dresid.shape[1]
    slots = mem.shape[0]
    half, mhalf = dresid.shape[0] // 2, slots // 2
    d_attn = dresid[...].astype(BF16)
    emit(dot(mixed[...], d_attn, 0, 0), keep_ref, send_ref, 96, c)
    dm_ref[...] = dot(d_attn, out_weight[...], 1, 1).astype(BF16)
    for p in range(H // 2):
        lanes = slice(128 * p, 128 * p + 128)
        for i, p_ref in reversed(list(enumerate((p0, p1, p2, p3)))):
            w = 128 * (i + 2)
            rows = slice(128 * i, 128 * i + 128)
            q01 = stacked_heads(qs[rows, lanes])
            dm01 = stacked_heads(dm_ref[rows, lanes])
            pb = p_ref[p]
            pf = pb.astype(F32)
            dp = dot(dm01, vall[0:w, lanes], 1, 1)
            t = pf * dp
            ds = (t - pf * jnp.sum(t, -1, keepdims=True)).astype(BF16)
            dq = unstacked_heads(dot(ds, kall[0:w, lanes])) * 0.125
            dq_ref[rows, lanes] = dq.astype(BF16)
            dk = dot(ds, q01, 0, 0)
            dv = dot(pb, dm01, 0, 0)
            if i == 3:
                dk_ref[0:w, lanes] = dk
                dv_ref[0:w, lanes] = dv
            else:
                dk_ref[0:w, lanes] += dk
                dv_ref[0:w, lanes] += dv
    dk = dk_ref[...].astype(BF16)
    dv = dv_ref[...].astype(BF16)
    dq = dq_ref[...]
    na = nall[...]
    emit(dot(na[128:], dq, 0, 0), keep_ref, send_ref, 0, c)
    emit(dot(na, dk, 0, 0), keep_ref, send_ref, 32, c)
    emit(dot(na, dv, 0, 0), keep_ref, send_ref, 64, c)
    d_all = dot(dk, pair_weight[:, :width], 1, 1) + dot(dv, pair_weight[:, width:], 1, 1)
    d_nx = d_all[128:] + dot(dq, query_weight[...], 1, 1)
    d_nm = d_all[:slots] + dot(dwquery[...], write_query[...], 1, 1)
    gain = attn_gain[...]
    xhat, xr = norm_parts(x[...])
    d_x, g_x = norm_back(d_nx, xhat, xr, gain)
    mhat, mr = norm_parts(mem[...])
    d_m, g_m = norm_back(d_nm, mhat, mr, gain)
    tok_ref[...] = dresid[...] + d_x
    gmem_ref[...] = dblend[...] + d_m
    own = pl.multiple_of(y * half, half)
    other = pl.multiple_of((1 - y) * half, half)
    mown = pl.multiple_of(y * mhalf, mhalf)
    mother = pl.multiple_of((1 - y) * mhalf, mhalf)
    own_tok_ref[...] = tok_ref[pl.ds(own, half), :]
    own_mem_ref[...] = gmem_ref[pl.ds(mown, mhalf), :]
    own_new_ref[...] = newmem[pl.ds(mown, mhalf), :]
    swap_ref[0:half, :] = tok_ref[pl.ds(other, half), :].astype(BF16)
    swap_ref[half : half + mhalf, :] = newmem[pl.ds(mother, mhalf), :]
    swap_ref[half + mhalf :, :] = gmem_ref[pl.ds(mother, mhalf), :].astype(BF16)
    gains = jnp.concatenate([g_x + g_m, gain2[...], gain3[...], jnp.zeros((29, width), F32)], 0)
    gains = jnp.broadcast_to(gains[None].astype(BF16), (GROUPS // 2, 32, width))
    keep_ref[:, 128:160, :] = gains
    send_ref[:, 128:160, :] = gains


def call(kernel, outs, scratch=(), smem=1, flops=0, nbytes=0):
    def run(*args):
        specs = [
            pl.BlockSpec(memory_space=pltpu.SMEM if i < smem else pltpu.VMEM)
            for i in range(len(args))
        ]
        return pl.pallas_call(
            kernel,
            out_shape=[jax.ShapeDtypeStruct(s, d) for s, d in outs],
            in_specs=specs,
            out_specs=[pl.BlockSpec(memory_space=pltpu.VMEM)] * len(outs),
            scratch_shapes=[pltpu.VMEM(s, d) for s, d in scratch],
            compiler_params=pltpu.CompilerParams(vmem_limit_bytes=VMEM_LIMIT),
            cost_estimate=pl.CostEstimate(flops=flops, bytes_accessed=nbytes, transcendentals=0),
        )(*args)

    return run


def other_of(axis, bit):
    size = lax.axis_size(axis)
    return [(i, i ^ bit) for i in range(size)]


def halves(total, axis, bit_value):
    size = total.shape[axis] // 2
    keep = lax.dynamic_slice_in_dim(total, bit_value * size, size, axis)
    send = lax.dynamic_slice_in_dim(total, (1 - bit_value) * size, size, axis)
    return keep, send


def added(keep, recv):
    return (keep.astype(F32) + recv.astype(F32)).astype(BF16)


def reduced_small(keep, send, rows_a):
    seg = lax.axis_index("seg")
    y = lax.axis_index("seq")
    x, z = (seg // 2) % 2, seg // 4
    total = added(keep, lax.ppermute(send, "seg", other_of("seg", 1)))
    r, w = total.shape[1:]
    a = total[:, :rows_a].reshape(4, 2, rows_a, w)
    b = total[:, rows_a:]
    take = lambda v, i, ax: lax.dynamic_index_in_dim(v, i, ax, keepdims=False)
    ra = lax.ppermute(take(a, 1 - x, 1), "seg", other_of("seg", 2))
    kb, sb = halves(b, 1, y)
    rb = lax.ppermute(sb, "seq", other_of("seq", 1))
    a = added(take(a, x, 1), ra)
    b = added(kb, rb).reshape(4, 2, (r - rows_a) // 2, w)
    ka, sa = halves(a, 1, y)
    ra = lax.ppermute(sa, "seq", other_of("seq", 1))
    rb = lax.ppermute(take(b, 1 - x, 1), "seg", other_of("seg", 2))
    t = jnp.concatenate([added(ka, ra), added(take(b, x, 1), rb)], 1)
    t = t.reshape(2, 2, r // 2, w)
    t = added(take(t, z % 2, 1), lax.ppermute(take(t, 1 - z % 2, 1), "seg", other_of("seg", 4)))
    t = added(take(t, z // 2, 0), lax.ppermute(take(t, 1 - z // 2, 0), "seg", other_of("seg", 8)))
    o = lax.ppermute(t, "seq", other_of("seq", 1))
    first = jnp.where(y == 0, t, o).astype(F32)
    second = jnp.where(y == 0, o, t).astype(F32)
    ha = rows_a // 2
    return jnp.concatenate([first[:ha], second[:ha], first[ha:], second[ha:]], 0)


def reduced_any(keep, send, pieces):
    groups = lax.axis_size("seg")
    c = lax.axis_index("seg") % 2
    first = jnp.where(c == 0, keep, send)
    second = jnp.where(c == 0, send, keep)
    total = jnp.stack([first, second], 1)
    total = total.reshape((GROUPS,) + keep.shape[1:])
    fine = groups // GROUPS
    parts = []
    at = 0
    for rows, shared in pieces:
        part = total[:, at : at + rows]
        if shared:
            part = jnp.broadcast_to(part[:, None], (GROUPS, fine) + part.shape[1:])
        else:
            part = part.reshape(GROUPS, fine, rows // fine, part.shape[2])
        parts.append(part.reshape(groups, -1, part.shape[-1]))
        at += rows
    total = jnp.concatenate(parts, 1)
    total = lax.psum_scatter(total.astype(F32), "seg", scatter_dimension=0, tiled=True)[0]
    return lax.psum(total, "seq")


def shards(
    tokens, memory, lengths, attn_gain, query_weight, pair_weight, out_weight, ffn_gain, ffn_in,
    ffn_out, write_query, write_pair, write_out, write_gate, write_gain, out_cotangent,
    memory_cotangent,
):
    half, width = tokens.shape[1:]
    mhalf = memory.shape[1]
    rows, slots, ff = 2 * half, 2 * mhalf, ffn_in.shape[1]
    padded = rows + 128
    groups = lax.axis_size("seg")
    y = lax.axis_index("seq")
    seg = lax.axis_index("seg")
    place = jnp.stack([y, seg % 2]).astype(jnp.int32)
    swap = other_of("seq", 1)
    pick = lambda v: lax.dynamic_index_in_dim(v, 1 - y, 0, keepdims=False)
    recv_a = lax.ppermute(jnp.concatenate([pick(tokens), pick(memory)], 0), "seq", swap)
    recv_b = lax.ppermute(
        jnp.concatenate([pick(out_cotangent), pick(memory_cotangent)], 0), "seq", swap
    )
    ag, fg, wg = attn_gain[None], ffn_gain[None], write_gain[None]
    big = ((rows, width), BF16)
    (
        x, mem, nall, qs, kall, vall, p0, p1, p2, p3, mixed, resid, n2, act, dg, out, out_send, wqs
    ) = call(
        forward_kernel,
        [
            ((rows, width), F32), ((slots, width), F32), ((padded, width), BF16), big,
            ((padded, width), BF16), ((padded, width), BF16),
            *[((H // 2, 256, 128 * (i + 2)), BF16) for i in range(4)],
            big, ((rows, width), F32), big, ((rows, ff), BF16), ((rows, ff), BF16), big,
            ((half, width), BF16), ((slots, width), BF16),
        ],
        smem=2, flops=2 * 3 * 10**9, nbytes=20 * 10**6,
    )(
        place, lengths, tokens, memory, recv_a, ag, query_weight, pair_weight, out_weight, fg,
        ffn_in, ffn_out, write_query,
    )
    out_recv = lax.ppermute(out_send, "seq", swap)
    keep1, send1, dwpair, dwquery, dblend, newmem, gain3 = call(
        write_kernel,
        [
            ((GROUPS // 2, 160, width), BF16), ((GROUPS // 2, 160, width), BF16),
            ((rows, 2 * width), BF16), ((slots, width), BF16), ((slots, width), F32),
            ((slots, width), BF16), ((1, width), F32),
        ],
        scratch=[((slots, width), F32)], flops=2 * 15 * 10**8, nbytes=10 * 10**6,
    )(
        place, out, wqs, mem, nall, memory_cotangent, recv_b, write_pair, write_out, write_gate, wg
    )
    keep2, send2, dresid, gain2 = call(
        ffn_back_kernel,
        [
            ((GROUPS // 2, 256, width), BF16), ((GROUPS // 2, 256, width), BF16),
            ((rows, width), F32), ((1, width), F32),
        ],
        scratch=[((rows, width), F32)], flops=2 * 25 * 10**8, nbytes=20 * 10**6,
    )(
        place, dwpair, out_cotangent, recv_b, write_pair, act, dg, n2, resid, ffn_in, ffn_out, fg
    )
    keep3, send3, own_tok, own_mem, own_new, swap_out = call(
        attn_back_kernel,
        [
            ((GROUPS // 2, 160, width), BF16), ((GROUPS // 2, 160, width), BF16),
            ((half, width), F32), ((mhalf, width), F32), ((mhalf, width), BF16),
            ((half + 2 * mhalf, width), BF16),
        ],
        scratch=[
            ((padded, width), F32), ((padded, width), F32), big, big, ((rows, width), F32),
            ((slots, width), F32),
        ],
        flops=2 * 3 * 10**9, nbytes=20 * 10**6,
    )(
        place, dresid, mixed, out_weight, qs, kall, vall, p0, p1, p2, p3, nall, x, mem, ag,
        query_weight, pair_weight, write_query, dwquery, dblend, newmem, gain2, gain3,
    )
    swapped = lax.ppermute(swap_out, "seq", swap)
    if groups == GROUPS:
        w1 = reduced_small(keep1, send1, 96)
        w2 = reduced_small(keep2, send2, 160)
        w3 = reduced_small(keep3, send3, 96)
    else:
        r = width // GROUPS
        w1 = reduced_any(keep1, send1, [(r, False)] * 5)
        w2 = reduced_any(keep2, send2, [(r, False)] * (ff // 512) + [(ff // GROUPS, False)])
        w3 = reduced_any(keep3, send3, [(r, False)] * 4 + [(32, True)])
    r = width // groups
    cut = lambda w, at, n: jnp.concatenate([w[(at + i) * r : (at + i + 1) * r] for i in range(n)], 1)
    gains = w3[4 * r :]
    gain_of = lambda i: lax.dynamic_slice_in_dim(gains[i], seg * r, r, 0)

    def both(own, recv):
        recv = recv.astype(own.dtype)
        return jnp.where(
            jnp.arange(2)[:, None, None] == y, own[None], recv[None]
        )

    own_out = lax.dynamic_slice_in_dim(out, y * half, half, 0)
    return (
        both(own_out, out_recv),
        both(own_new, swapped[half : half + mhalf]),
        both(own_tok, swapped[:half]),
        both(own_mem, swapped[half + mhalf :]),
        gain_of(0),
        w3[:r],
        cut(w3, 1, 2),
        w3[3 * r : 4 * r],
        gain_of(1),
        cut(w2, 0, ff // 512),
        w2[(ff // 512) * r :],
        w1[:r],
        cut(w1, 1, 2),
        w1[3 * r : 4 * r],
        w1[4 * r : 5 * r],
        gain_of(2),
    )


def solution(mesh):
    row = P("seg", "seq", None)
    grad = P("seg", None)
    in_specs = (row, row, P("seg", None)) + (P(),) * 12 + (row, row)
    out_specs = (row, row, row, row, P("seg"), grad, grad, grad, P("seg")) + (grad,) * 6 + (P("seg"),)
    return jax.shard_map(shards, mesh=mesh, in_specs=in_specs, out_specs=out_specs, check_vma=False)
```

```python
import jax
import jax.numpy as jnp
from jax import lax
from jax.experimental import pallas as pl
from jax.experimental.pallas import tpu as pltpu
from jax.sharding import PartitionSpec as P

H = 8
GROUPS = 16
EPSILON = 1e-05
MASKED = -1e30
F32 = jnp.float32
BF16 = jnp.bfloat16
VMEM_LIMIT = 56 * 1024 * 1024


def part(place, half, own):
    index = place[0] if own else 1 - place[0]
    return pl.ds(pl.multiple_of(index * half, half), half)


def call(body, ins, outs, scratch=(), flops=0, nbytes=0, limit=16, home=True):
    kinds = [kind for kind, _ in ins]
    arrays = [
        pltpu.with_memory_space_constraint(a, pltpu.VMEM) if kind == "v" else a for kind, a in ins
    ]
    spaces = {"s": pltpu.SMEM, "v": pltpu.VMEM, "d": pl.ANY}

    def kernel(*refs):
        given = [r for kind, r in zip(kinds, refs) if kind != "d"]
        body(*given, *refs[len(ins) :])

    shape = (lambda s, d: pltpu.VMEM(s, d)) if home else jax.ShapeDtypeStruct
    return pl.pallas_call(
        kernel,
        out_shape=[shape(s, d) for s, d in outs],
        in_specs=[pl.BlockSpec(memory_space=spaces[kind]) for kind in kinds],
        out_specs=[pl.BlockSpec(memory_space=pltpu.VMEM)] * len(outs),
        scratch_shapes=[pltpu.VMEM(s, d) for s, d in scratch],
        compiler_params=pltpu.CompilerParams(vmem_limit_bytes=limit * 1024 * 1024),
        cost_estimate=pl.CostEstimate(flops=flops, bytes_accessed=nbytes, transcendentals=0),
    )(*arrays)


def dot(a, b, ca=1, cb=0):
    return lax.dot_general(a, b, (((ca,), (cb,)), ((), ())), preferred_element_type=F32)


def norm_parts(v):
    centred = v - jnp.mean(v, -1, keepdims=True)
    r = lax.rsqrt(jnp.mean(centred * centred, -1, keepdims=True) + EPSILON)
    return centred * r, r


def norm_back(dy, xhat, r, gain):
    dx = dy * gain
    m1 = jnp.mean(dx, -1, keepdims=True)
    m2 = jnp.mean(dx * xhat, -1, keepdims=True)
    return r * (dx - m1 - xhat * m2), jnp.sum(dy * xhat, 0, keepdims=True)


def emit_rows(grad, rows, ks_ref, offset, c, first=0):
    pairs = grad.shape[0] // (2 * rows)
    g = grad.astype(BF16).reshape(pairs, 2, rows, grad.shape[1])
    where = (slice(first, first + pairs), slice(offset, offset + rows), slice(None))
    even, odd = g[:, 0], g[:, 1]
    send_ref, keep_ref = ks_ref
    keep_ref[where] = jnp.where(c == 0, even, odd)
    send_ref[where] = jnp.where(c == 0, odd, even)


def whole_rows(place, pair_ref, recv_ref, start, half):
    own, other = pair_ref[place[0]], recv_ref[start : start + half, :]
    first = place[0] == 0
    return jnp.concatenate([jnp.where(first, own, other), jnp.where(first, other, own)], 0)


def lane_low(shape):
    return lax.broadcasted_iota(jnp.int32, shape, 1) < 64


def stacked_heads(block):
    low = lane_low(block.shape)
    zero = jnp.zeros_like(block)
    return jnp.concatenate([jnp.where(low, block, zero), jnp.where(low, zero, block)], 0)


def unstacked_heads(block):
    rows = block.shape[0] // 2
    top, bottom = block[:rows], block[rows:]
    return jnp.where(lane_low(top.shape), top, bottom)


def head_mask(rows_per, width):
    shape = (H * rows_per, width)
    row_head = lax.broadcasted_iota(jnp.int32, shape, 0) // rows_per
    col_head = lax.broadcasted_iota(jnp.int32, shape, 1) // (width // H)
    return row_head == col_head


def block_diagonal(v, mask):
    return jnp.where(mask, jnp.concatenate([v] * H, 0), jnp.zeros((), v.dtype))


def diagonal_blocks(v, mask):
    rows = v.shape[0] // H
    v = jnp.where(mask, v, 0.0)
    return jnp.sum(v.reshape(H, rows, v.shape[1]), 0)


def forward_body(
    place, lengths, tokens, memory, recv, attn_gain, query_weight, pair_weight, write_query, out_weight,
    ffn_gain, ffn_in, ffn_out,
    x, mem, nall, qs, kall, vall, p0, p1, p2, p3, mixed, resid, n2, act, dg,
    out_send, out_own, out, wqs,
):
    y = place[0]
    width = pair_weight.shape[0]
    rows = x.shape[0]
    slots = mem.shape[0]
    half = rows // 2
    x[...] = whole_rows(place, tokens, recv, 0, half)
    mem[...] = whole_rows(place, memory, recv, half, slots // 2)
    gain = attn_gain[...]
    xhat, _ = norm_parts(x[...].astype(F32))
    nx = (xhat * gain).astype(BF16)
    mhat, _ = norm_parts(mem[...].astype(F32))
    nm = (mhat * gain).astype(BF16)
    nall[0:slots, :] = nm
    nall[slots:128, :] = jnp.zeros((128 - slots, width), BF16)
    nall[128:, :] = nx
    qs[...] = (dot(nx, query_weight[...]) * 0.125).astype(BF16)
    na = nall[...]
    kall[...] = dot(na, pair_weight[:, :width]).astype(BF16)
    vall[...] = dot(na, pair_weight[:, width:]).astype(BF16)
    wqs[...] = (dot(nm, write_query[...]) * 0.125).astype(BF16)
    bounds = []
    total = 0
    for k in range(lengths.shape[1]):
        total = total + lengths[y, k]
        bounds.append(total)
    pos_c = lax.broadcasted_iota(jnp.int32, (1, rows), 1)
    doc_c = sum([(pos_c >= b).astype(jnp.int32) for b in bounds])
    mem_bias = jnp.where(
        lax.broadcasted_iota(jnp.int32, (128, 128), 1) < slots, 0.0, MASKED
    ).astype(F32)
    for i, p_out in enumerate((p0, p1, p2, p3)):
        w = 128 * (i + 2)
        cols = w - 128
        pos_r = lax.broadcasted_iota(jnp.int32, (128, 1), 0) + 128 * i
        doc_r = sum([(pos_r >= b).astype(jnp.int32) for b in bounds])
        ok = (doc_r == doc_c[:, :cols]) & (pos_c[:, :cols] <= pos_r)
        bias = jnp.concatenate([mem_bias, jnp.where(ok, 0.0, MASKED).astype(F32)], 1)
        for p in range(H // 2):
            lanes = slice(128 * p, 128 * p + 128)
            q01 = stacked_heads(qs[128 * i : 128 * i + 128, lanes])
            s = dot(q01, kall[0:w, lanes], 1, 1)
            s = (s.reshape(2, 128, w) + bias[None]).reshape(256, w)
            e = jnp.exp(s - jnp.max(s, -1, keepdims=True))
            pr = (e * (1.0 / jnp.sum(e, -1, keepdims=True))).astype(BF16)
            p_out[p] = pr
            o = dot(pr, vall[0:w, lanes])
            mixed[128 * i : 128 * i + 128, lanes] = unstacked_heads(o).astype(BF16)
    r = x[...].astype(F32) + dot(mixed[...], out_weight[...])
    resid[...] = r
    rhat, _ = norm_parts(r)
    n2v = (rhat * ffn_gain[...]).astype(BF16)
    n2[...] = n2v
    ff = ffn_in.shape[1]
    k0 = 0.7978845608028654
    for j in range(ff // 512):
        cols = slice(512 * j, 512 * j + 512)
        v = dot(n2v, ffn_in[:, cols])
        v2 = v * v
        t = jnp.tanh(k0 * (v + 0.044715 * (v2 * v)))
        h = 0.5 * (1.0 + t)
        act[:, cols] = (v * h).astype(BF16)
        d = h + (0.5 * v) * (1.0 - t * t) * (k0 + (3.0 * 0.044715 * k0) * v2)
        dg[:, cols] = d.astype(BF16)
    out[...] = (resid[...] + dot(act[...], ffn_out[...])).astype(BF16)
    out_own[...] = out[part(place, half, True), :]
    out_send[...] = out[part(place, half, False), :]


def write_body(
    place, out, wqs, mem, memory_cotangent, recv, write_pair, write_out, write_gate, write_gain, nall,
    send, keep, dwpair, dwquery, dblend, own_new, newmem, gain_out,
):
    c, ks = place[1], (send, keep)
    slots, width = wqs.shape
    o = out[...]
    wk = dot(o, write_pair[:, :width]).astype(BF16)
    wv = dot(o, write_pair[:, width:]).astype(BF16)
    mask = head_mask(slots, width)
    qbd = block_diagonal(wqs[...], mask)
    s = dot(qbd, wk, 1, 1)
    e = jnp.exp(s - jnp.max(s, -1, keepdims=True))
    pf = e * (1.0 / jnp.sum(e, -1, keepdims=True))
    pb = pf.astype(BF16)
    wmixed = diagonal_blocks(dot(pb, wv), mask).astype(BF16)
    update = dot(wmixed, write_out[...])
    update_low = update.astype(BF16)
    gate = jax.nn.sigmoid(dot(update_low, write_gate[...]))
    blended = mem[...].astype(F32) + gate * update
    bhat, br = norm_parts(blended)
    gain = write_gain[...]
    newmem[...] = (bhat * gain).astype(BF16)
    mhalf = slots // 2
    own_new[...] = newmem[part(place, mhalf, True), :]
    mc = whole_rows(place, memory_cotangent, recv, recv.shape[0] - mhalf, mhalf).astype(F32)
    d_blend, d_gain = norm_back(mc, bhat, br, gain)
    gain_out[...] = d_gain
    dblend[...] = d_blend
    d_gate_pre = (d_blend * update * gate * (1.0 - gate)).astype(BF16)
    d_update = (d_blend * gate + dot(d_gate_pre, write_gate[...], 1, 1)).astype(BF16)
    d_wmixed = dot(d_update, write_out[...], 1, 1).astype(BF16)
    emit_rows(dot(update_low, d_gate_pre, 0, 0), 32, ks, 128, c)
    emit_rows(dot(wmixed, d_update, 0, 0), 32, ks, 96, c)
    dbd = block_diagonal(d_wmixed, mask)
    dp = dot(dbd, wv, 1, 1)
    row = jnp.sum(pf * dp, -1, keepdims=True)
    ds = (pf * (dp - row)).astype(BF16)
    d_wquery = (diagonal_blocks(dot(ds, wk), mask) * 0.125).astype(BF16)
    dwquery[...] = d_wquery
    dwk = dot(ds, qbd, 0, 0).astype(BF16)
    dwv = dot(pb, dbd, 0, 0).astype(BF16)
    dwpair[:, :width] = dwk
    dwpair[:, width:] = dwv
    emit_rows(dot(nall[0:slots, :], d_wquery, 0, 0), 32, ks, 0, c)
    emit_rows(dot(o, dwk, 0, 0), 32, ks, 32, c)
    emit_rows(dot(o, dwv, 0, 0), 32, ks, 64, c)


def ffn_back_body(
    place, dwpair, write_pair, out_cotangent, recv, ffn_out, dg, ffn_in, act, n2,
    send, keep, total_out, dout_out,
):
    c, ks = place[1], (send, keep)
    width, ff = ffn_in.shape
    rows, deep = width // GROUPS, ff // GROUPS
    cot = whole_rows(place, out_cotangent, recv, 0, out_cotangent.shape[1])
    d_out = cot.astype(F32) + dot(dwpair[...], write_pair[...], 1, 1)
    dout_out[...] = d_out
    d_branch = d_out.astype(BF16)
    total = None
    for j in range(ff // 512):
        cols = slice(512 * j, 512 * j + 512)
        d_act = dot(d_branch, ffn_out[cols, :], 1, 1).astype(BF16)
        d_inner = (d_act.astype(F32) * dg[:, cols].astype(F32)).astype(BF16)
        term = dot(d_inner, ffn_in[:, cols], 1, 1)
        total = term if total is None else total + term
        emit_rows(dot(n2[...], d_inner, 0, 0), rows, ks, rows * j, c)
        emit_rows(
            dot(act[:, cols], d_branch, 0, 0),
            deep, ks, rows * (ff // 512), c, 512 // (2 * deep) * j,
        )
    total_out[...] = total


def resid_back_body(
    place, total, dout, resid, ffn_gain, out_weight,
    dresid, dmixed, gain_out,
):
    rhat, rr = norm_parts(resid[...])
    d_norm, d_gain = norm_back(total[...], rhat, rr, ffn_gain[...])
    gain_out[...] = d_gain
    d = dout[...] + d_norm
    dresid[...] = d
    dmixed[...] = dot(d.astype(BF16), out_weight[...], 1, 1).astype(BF16)


def attn_back_body(
    place, qs, dm, vall, p3, kall, p2, p1, p0,
    dq_out, dk_out, dv_out, dk_ref, dv_ref,
):
    for p in range(H // 2):
        lanes = slice(128 * p, 128 * p + 128)
        for i, p_in in reversed(list(enumerate((p0, p1, p2, p3)))):
            w = 128 * (i + 2)
            rows = slice(128 * i, 128 * i + 128)
            q01 = stacked_heads(qs[rows, lanes])
            dm01 = stacked_heads(dm[rows, lanes])
            dp = dot(dm01, vall[0:w, lanes], 1, 1)
            pb = p_in[p]
            pf = pb.astype(F32)
            t = pf * dp
            ds = (t - pf * jnp.sum(t, -1, keepdims=True)).astype(BF16)
            dq = unstacked_heads(dot(ds, kall[0:w, lanes])) * 0.125
            dq_out[rows, lanes] = dq.astype(BF16)
            dk = dot(ds, q01, 0, 0)
            dv = dot(pb, dm01, 0, 0)
            if i == 3:
                dk_ref[0:w, lanes] = dk
                dv_ref[0:w, lanes] = dv
            else:
                dk_ref[0:w, lanes] += dk
                dv_ref[0:w, lanes] += dv
    dk_out[...] = dk_ref[...].astype(BF16)
    dv_out[...] = dv_ref[...].astype(BF16)


def input_back_body(
    place, nall, dq, dk, dv, pair_weight, query_weight, dwquery, write_query, x, mem, attn_gain,
    dresid, dblend, mixed, gain2, gain3, newmem,
    send, keep, own_tok, own_mem, swap, gtok, gmem,
):
    c, ks = place[1], (send, keep)
    rows, width = x.shape
    slots = mem.shape[0]
    half, mhalf = rows // 2, slots // 2
    na = nall[...]
    dqv = dq[...]
    emit_rows(dot(na[128:], dqv, 0, 0), 32, ks, 0, c)
    emit_rows(dot(na, dk[...], 0, 0), 32, ks, 32, c)
    emit_rows(dot(na, dv[...], 0, 0), 32, ks, 64, c)
    emit_rows(dot(mixed[...], dresid[...].astype(BF16), 0, 0), 32, ks, 96, c)
    d_all = dot(dk[...], pair_weight[:, :width], 1, 1)
    d_all = d_all + dot(dv[...], pair_weight[:, width:], 1, 1)
    d_nx = d_all[128:] + dot(dqv, query_weight[...], 1, 1)
    d_nm = d_all[:slots] + dot(dwquery[...], write_query[...], 1, 1)
    gain = attn_gain[...]
    xhat, xr = norm_parts(x[...].astype(F32))
    d_x, g_x = norm_back(d_nx, xhat, xr, gain)
    mhat, mr = norm_parts(mem[...].astype(F32))
    d_m, g_m = norm_back(d_nm, mhat, mr, gain)
    gains = jnp.concatenate(
        [g_x + g_m, gain2[...], gain3[...], jnp.zeros((29, width), F32)], 0
    ).astype(BF16)
    for one in ks:
        one[:, 128:160, :] = jnp.broadcast_to(gains, (GROUPS // 2, 32, width))
    gtok[...] = dresid[...] + d_x
    gmem[...] = dblend[...] + d_m
    own_tok[...] = gtok[part(place, half, True), :]
    own_mem[...] = gmem[part(place, mhalf, True), :]
    other = part(place, half, False)
    mother = part(place, mhalf, False)
    swap[0:half, :] = gtok[other, :].astype(BF16)
    swap[half : half + mhalf, :] = newmem[mother, :]
    swap[half + mhalf :, :] = gmem[mother, :].astype(BF16)


BIT = {"y": 0, "x": 2, "z": 3, "h": 4}


def other_of(axis, bit):
    return [(i, i ^ bit) for i in range(lax.axis_size(axis))]


def exchanged(send, label):
    if label == "y":
        return lax.ppermute(send, "seq", other_of("seq", 1))
    return lax.ppermute(send, "seg", other_of("seg", {"x": 2, "z": 4, "h": 8, "c": 1}[label]))


class Stream:
    def __init__(self, keep, recv, dims, start, rows):
        self.keep, self.recv, self.dims, self.start, self.rows = keep, recv, dims, start, rows


def stage(place, streams, labels, joined=False, deps=()):
    ins = [("s", place)]
    index = {}
    for s in streams:
        for arr in (s.keep, s.recv):
            if id(arr) not in index:
                index[id(arr)] = len(ins)
                ins.append(("v", arr))
    n_arrays = len(ins)
    ins += [("d", d) for d in deps]
    width = streams[0].keep.shape[-1]
    shapes, new_dims, new_rows = [], [], []
    for s, label in zip(streams, labels):
        rows = s.rows // 2 if label == "y" else s.rows
        dims = s.dims.replace(label, "")
        new_dims.append(dims)
        new_rows.append(rows)
        shapes.append((2,) * len(dims) + (rows, width))
    if joined:
        shapes = [(sum(new_rows), width)]
    outs = []
    for shape in shapes:
        outs += [(shape, BF16)] * 2

    def body(place, *refs):
        given, made = refs[: n_arrays - 1], refs[n_arrays - 1 :]

        def value(s, label, own, arr):
            bit = place[BIT[label]]
            bit = bit if own else 1 - bit
            where = []
            for d in s.dims:
                where.append(bit if d == label else slice(None))
            if label == "y":
                half = s.rows // 2
                where.append(pl.ds(pl.multiple_of(s.start + bit * half, 16), half))
            else:
                where.append(slice(s.start, s.start + s.rows))
            return given[index[id(arr)] - 1][tuple(where) + (slice(None),)].astype(F32)

        for own in (False, True):
            at = 0
            for k, (s, label) in enumerate(zip(streams, labels)):
                total = (value(s, label, own, s.keep) + value(s, label, own, s.recv)).astype(BF16)
                target = made[(0 if joined else 2 * k) + (0 if own else 1)]
                if joined:
                    target[at : at + new_rows[k], :] = total
                    at += new_rows[k]
                else:
                    target[...] = total

    results = call(body, ins, outs, flops=10**6, nbytes=10**6)
    if joined:
        return results[0], results[1]
    return [
        (results[2 * k], results[2 * k + 1], new_dims[k], new_rows[k]) for k in range(len(streams))
    ]


def added(place, keep, recv):
    def body(place, keep, recv, total):
        total[...] = (keep[...].astype(F32) + recv[...].astype(F32)).astype(BF16)

    (total,) = call(
        body,
        [("s", place), ("v", keep), ("v", recv)],
        [(keep.shape, BF16)],
        flops=10**6, nbytes=10**6,
    )
    return total


def reduced_any(keep, send, pieces):
    groups = lax.axis_size("seg")
    c = lax.axis_index("seg") % 2
    first = jnp.where(c == 0, keep, send)
    second = jnp.where(c == 0, send, keep)
    total = jnp.stack([first, second], 1)
    total = total.reshape((GROUPS,) + keep.shape[1:])
    fine = groups // GROUPS
    parts = []
    at = 0
    for rows, shared in pieces:
        piece = total[:, at : at + rows]
        if shared:
            piece = jnp.broadcast_to(piece[:, None], (GROUPS, fine) + piece.shape[1:])
        else:
            piece = piece.reshape(GROUPS, fine, rows // fine, piece.shape[2])
        parts.append(piece.reshape(groups, -1, piece.shape[-1]))
        at += rows
    total = jnp.concatenate(parts, 1)
    total = lax.psum_scatter(total.astype(F32), "seg", scatter_dimension=0, tiled=True)[0]
    return lax.psum(total, "seq")


def final_parts(place, one, two, ff):
    width = one[0].shape[-1]
    r = width // GROUPS
    n = ff // 512
    shapes = [
        (r, width), (r, 2 * width), (r, width), (r, ff), (ff // GROUPS, width),
        (r, width), (r, 2 * width), (r, width), (r, width), (8, width),
    ]

    def body(place, t1, o1, t2, o2, gq, gp, go, gfi, gfo, gwq, gwp, gwo, gwg, gains, full1, full2):
        y = place[0]
        for t, o, full, streams in ((t1, o1, full1, one[2]), (t2, o2, full2, two[2])):
            at = start = 0
            for rows in streams:
                half = rows // 2
                for ref, own in ((t, True), (o, False)):
                    index = y if own else 1 - y
                    full[pl.ds(pl.multiple_of(start + index * half, 16), half), :] = ref[
                        at : at + half, :
                    ].astype(F32)
                at += half
                start += rows
        gq[...] = full2[0:r, :]
        gp[:, :width] = full2[r : 2 * r, :]
        gp[:, width:] = full2[2 * r : 3 * r, :]
        go[...] = full2[3 * r : 4 * r, :]
        gains[...] = full2[4 * r : 4 * r + 8, :]
        gwq[...] = full1[0:r, :]
        gwp[:, :width] = full1[r : 2 * r, :]
        gwp[:, width:] = full1[2 * r : 3 * r, :]
        gwo[...] = full1[3 * r : 4 * r, :]
        gwg[...] = full1[4 * r : 5 * r, :]
        for j in range(n):
            gfi[:, 512 * j : 512 * j + 512] = full1[(5 + j) * r : (6 + j) * r, :]
        gfo[...] = full1[(5 + n) * r :, :]

    ins = [("s", place)] + [("v", a) for a in (one[0], one[1], two[0], two[1])]
    return call(
        body, ins, [(s, F32) for s in shapes],
        scratch=[((sum(one[2]), width), F32), ((sum(two[2]), width), F32)],
        flops=10**6, nbytes=10**6, home=False,
    )


def shards(
    tokens, memory, lengths, attn_gain, query_weight, pair_weight, out_weight, ffn_gain, ffn_in,
    ffn_out, write_query, write_pair, write_out, write_gate, write_gain, out_cotangent,
    memory_cotangent,
):
    half, width = tokens.shape[1:]
    mhalf = memory.shape[1]
    rows, slots, ff = 2 * half, 2 * mhalf, ffn_in.shape[1]
    padded = rows + 128
    groups = lax.axis_size("seg")
    y = lax.axis_index("seq")
    seg = lax.axis_index("seg")
    place = jnp.stack([y, seg % 2, (seg // 2) % 2, (seg // 4) % 2, (seg // 8) % 2])
    place = place.astype(jnp.int32)
    sc = ("s", place)
    pick = lambda v: lax.dynamic_index_in_dim(v, 1 - y, 0, keepdims=False)
    recv_a = exchanged(jnp.concatenate([pick(tokens), pick(memory)], 0), "y")
    recv_b = exchanged(jnp.concatenate([pick(out_cotangent), pick(memory_cotangent)], 0), "y")
    ag, fg, wg = attn_gain[None], ffn_gain[None], write_gain[None]
    v = lambda *arrs: [("v", a) for a in arrs]
    big = ((rows, width), BF16)
    wide = ((padded, width), BF16)
    deep = ((rows, ff), BF16)
    half_b = ((half, width), BF16)
    keep_send = lambda n: [((GROUPS // 2, n, width), BF16)] * 2
    small = ((slots, width), BF16)
    full_f = ((rows, width), F32)
    gain_row = ((1, width), F32)
    (
        x, mem, nall, qs, kall, vall, p0, p1, p2, p3, mixed, resid, n2, act, dg,
        out_send, out_own, out, wqs,
    ) = call(
        forward_body,
        [sc, ("s", lengths)] + v(tokens, memory, recv_a, ag, query_weight, pair_weight, write_query, out_weight, fg, ffn_in, ffn_out),
        [big, small, wide, big, wide, wide]
        + [((H // 2, 256, 128 * (i + 2)), BF16) for i in range(4)]
        + [big, full_f, big, deep, deep, half_b, half_b, big, small],
        flops=2 * 6 * 10**9, nbytes=20 * 10**6,
    )
    out_recv = exchanged(out_send, "y")
    send0, keep0, dwpair, dwquery, dblend, own_new, newmem, gain3 = call(
        write_body,
        [sc] + v(out, wqs, mem, memory_cotangent, recv_b, write_pair, write_out, write_gate, wg, nall),
        [
            *keep_send(160), ((rows, 2 * width), BF16), small,
            ((slots, width), F32), ((mhalf, width), BF16), small, gain_row,
        ],
        flops=2 * 3 * 10**9, nbytes=10 * 10**6,
    )
    small_mesh = groups == GROUPS
    send1, keep1, total, dout = call(
        ffn_back_body,
        [sc] + v(dwpair, write_pair, out_cotangent, recv_b, ffn_out, dg, ffn_in, act, n2),
        [*keep_send(256), full_f, full_f],
        flops=2 * 5 * 10**9, nbytes=20 * 10**6,
    )
    dresid, dmixed, gain2 = call(
        resid_back_body, [sc] + v(total, dout, resid, fg, out_weight), [full_f, big, gain_row],
        flops=2 * 10**9, nbytes=5 * 10**6,
    )
    deps1, deps2 = [], []
    if small_mesh:
        cube = lambda a: a.reshape((2, 2, 2) + a.shape[1:])
        recv0, recv1 = exchanged(send0, "c"), exchanged(send1, "c")
        k0, r0, k1, r1 = cube(keep0), cube(recv0), cube(keep1), cube(recv1)
        streams = [
            Stream(k0, r0, "hzx", 0, 160), Stream(k1, r1, "hzx", 0, 128),
            Stream(k1, r1, "hzx", 128, 128),
        ]
        orders = ("xyz", "yzx", "zxy")

        def moved(parts, step):
            return [
                Stream(keep, exchanged(send, orders[k][step]), dims, 0, r)
                for k, (keep, send, dims, r) in enumerate(parts)
            ]

        labels = lambda step: [o[step] for o in orders]
        parts = stage(place, streams, labels(0), deps=[dresid])
        deps1 = [("d", p[0]) for p in parts]
        streams = moved(parts, 0)
    dq, dk, dv = call(
        attn_back_body,
        [sc] + v(qs, dmixed, vall, p3, kall, p2, p1, p0) + deps1,
        [big, wide, wide],
        scratch=[((padded, width), F32)] * 2,
        flops=2 * 6 * 10**9, nbytes=20 * 10**6,
    )
    if small_mesh:
        parts = stage(place, streams, labels(1), deps=[dq])
        deps2 = [("d", p[0]) for p in parts]
        streams = moved(parts, 1)
    send2, keep2, own_tok, own_mem, swap = call(
        input_back_body,
        [sc]
        + v(
            nall, dq, dk, dv, pair_weight, query_weight, dwquery, write_query, x, mem, ag, dresid,
            dblend, mixed, gain2, gain3, newmem,
        )
        + deps2,
        [
            *keep_send(160), ((half, width), F32), ((mhalf, width), F32),
            ((half + 2 * mhalf, width), BF16),
        ],
        scratch=[((rows, width), F32), ((slots, width), F32)],
        flops=2 * 3 * 10**9, nbytes=20 * 10**6,
    )
    swapped = exchanged(swap, "y")
    r = width // groups
    if small_mesh:
        recv2 = exchanged(send2, "c")
        k2, r2 = cube(keep2), cube(recv2)
        keep, send = stage_three(place, streams, labels(2), swap)
        t1 = added(place, keep, exchanged(send, "h"))
        o1 = exchanged(t1, "y")
        late = [
            Stream(k2, r2, "hzx", 0, 64), Stream(k2, r2, "hzx", 64, 32),
            Stream(k2, r2, "hzx", 96, 64),
        ]
        late = moved(stage(place, late, labels(0)), 0)
        late = moved(stage(place, late, labels(1)), 1)
        late = moved(stage(place, late, labels(2)), 2)
        keep, send = stage(place, late, "hhh", joined=True)
        t2 = added(place, keep, exchanged(send, "h"))
        o2 = exchanged(t2, "y")
        gq, gp, go, gfi, gfo, gwq, gwp, gwo, gwg, gains = final_parts(
            place, (t1, o1, (160, 128, 128)), (t2, o2, (64, 32, 64)), ff
        )
    else:
        w = width // GROUPS
        w0 = reduced_any(keep0, send0, [(w, False)] * 5)
        w1 = reduced_any(keep1, send1, [(w, False)] * (ff // 512) + [(ff // GROUPS, False)])
        w2 = reduced_any(keep2, send2, [(w, False)] * 4 + [(32, True)])
        cut = lambda a, at, n: jnp.concatenate(
            [a[(at + i) * r : (at + i + 1) * r] for i in range(n)], 1
        )
        gq, gp, go, gains = cut(w2, 0, 1), cut(w2, 1, 2), cut(w2, 3, 1), w2[4 * r :]
        gfi, gfo = cut(w1, 0, ff // 512), w1[(ff // 512) * r :]
        gwq, gwp, gwo, gwg = cut(w0, 0, 1), cut(w0, 1, 2), cut(w0, 3, 1), cut(w0, 4, 1)
    gain_of = lambda i: lax.dynamic_slice_in_dim(gains[i], seg * r, r, 0)

    def both(own, recv):
        recv = recv.astype(own.dtype)
        return jnp.where(jnp.arange(2)[:, None, None] == y, own[None], recv[None])

    return (
        both(out_own, out_recv),
        both(own_new, swapped[half : half + mhalf]),
        both(own_tok, swapped[:half]),
        both(own_mem, swapped[half + mhalf :]),
        gain_of(0), gq, gp, go, gain_of(1), gfi, gfo, gwq, gwp, gwo, gwg, gain_of(2),
    )


def stage_three(place, streams, labels, dep):
    parts = stage(place, streams, labels, deps=[dep])
    moved = [
        Stream(keep, exchanged(send, label), dims, 0, r)
        for label, (keep, send, dims, r) in zip(labels, parts)
    ]
    return stage(place, moved, "hhh", joined=True)


def solution(mesh):
    row = P("seg", "seq", None)
    grad = P("seg", None)
    in_specs = (row, row, P("seg", None)) + (P(),) * 12 + (row, row)
    out_specs = (row, row, row, row, P("seg"), grad, grad, grad, P("seg")) + (grad,) * 6 + (P("seg"),)
    return jax.shard_map(shards, mesh=mesh, in_specs=in_specs, out_specs=out_specs, check_vma=False)
```

```python
import jax
import jax.numpy as jnp
from jax import lax
from jax.experimental import pallas as pl
from jax.experimental.pallas import tpu as pltpu
from jax.sharding import PartitionSpec as P

H = 8
GROUPS = 16
EPSILON = 1e-05
MASKED = -1e30
F32 = jnp.float32
BF16 = jnp.bfloat16
VMEM_LIMIT = 56 * 1024 * 1024


def part(place, half, own):
    index = place[0] if own else 1 - place[0]
    return pl.ds(pl.multiple_of(index * half, half), half)


class Fetched:
    def __init__(self, source, ref, sem):
        self.ref, self.copy, self.waited = ref, pltpu.make_async_copy(source, ref, sem), False

    def __call__(self):
        if not self.waited:
            self.copy.wait()
            self.waited = True
        return self.ref


def position():
    seg = lax.axis_index("seg")
    return [lax.axis_index("seq")] + [(seg >> k) & 1 for k in range(4)]


def call(body, ins, outs, scratch=(), flops=0, nbytes=0, limit=16, home=True):
    kinds = [kind for kind, _ in ins]
    arrays = [
        pltpu.with_memory_space_constraint(a, pltpu.VMEM) if kind == "v" else a for kind, a in ins
    ]
    spaces = {"s": pltpu.SMEM, "v": pltpu.VMEM, "d": pl.ANY, "h": pl.ANY}
    fetched = [pltpu.VMEM(a.shape, a.dtype) for kind, a in ins if kind == "h"]
    n_io = len(ins) + len(outs)

    def kernel(*refs):
        given, at = [], 0
        for kind, r in zip(kinds, refs):
            if kind == "h":
                r = Fetched(r, refs[n_io + at], refs[-1].at[at])
                r.copy.start()
                at += 1
            if kind != "d":
                given.append(r)
        end = -1 if fetched else len(refs)
        body(position(), *given, *refs[len(ins) : n_io], *refs[n_io + at : end])
        for r in given:
            if isinstance(r, Fetched):
                r()

    shape = (lambda s, d: pltpu.VMEM(s, d)) if home else jax.ShapeDtypeStruct
    sems = [pltpu.SemaphoreType.DMA((len(fetched),))] if fetched else []
    return pl.pallas_call(
        kernel,
        out_shape=[shape(s, d) for s, d in outs],
        in_specs=[pl.BlockSpec(memory_space=spaces[kind]) for kind in kinds],
        out_specs=[pl.BlockSpec(memory_space=pltpu.VMEM)] * len(outs),
        scratch_shapes=fetched + [pltpu.VMEM(s, d) for s, d in scratch] + sems,
        compiler_params=pltpu.CompilerParams(vmem_limit_bytes=limit * 1024 * 1024),
        cost_estimate=pl.CostEstimate(flops=flops, bytes_accessed=nbytes, transcendentals=0),
    )(*arrays)


def dot(a, b, ca=1, cb=0):
    return lax.dot_general(a, b, (((ca,), (cb,)), ((), ())), preferred_element_type=F32)


def norm_parts(v):
    centred = v - jnp.mean(v, -1, keepdims=True)
    r = lax.rsqrt(jnp.mean(centred * centred, -1, keepdims=True) + EPSILON)
    return centred * r, r


def norm_back(dy, xhat, r, gain):
    dx = dy * gain
    m1 = jnp.mean(dx, -1, keepdims=True)
    m2 = jnp.mean(dx * xhat, -1, keepdims=True)
    return r * (dx - m1 - xhat * m2), jnp.sum(dy * xhat, 0, keepdims=True)


def emit_rows(grad, rows, ks_ref, offset, c, first=0):
    pairs = grad.shape[0] // (2 * rows)
    g = grad.astype(BF16).reshape(pairs, 2, rows, grad.shape[1])
    where = (slice(first, first + pairs), slice(offset, offset + rows), slice(None))
    even, odd = g[:, 0], g[:, 1]
    send_ref, keep_ref = ks_ref
    keep_ref[where] = jnp.where(c == 0, even, odd)
    send_ref[where] = jnp.where(c == 0, odd, even)


def whole_rows(place, pair_ref, recv_ref, start, half):
    own, other = pair_ref[place[0]], recv_ref[start : start + half, :]
    first = place[0] == 0
    return jnp.concatenate([jnp.where(first, own, other), jnp.where(first, other, own)], 0)


def lane_low(shape):
    return lax.broadcasted_iota(jnp.int32, shape, 1) < 64


def stacked_heads(block):
    low = lane_low(block.shape)
    zero = jnp.zeros_like(block)
    return jnp.concatenate([jnp.where(low, block, zero), jnp.where(low, zero, block)], 0)


def unstacked_heads(block):
    rows = block.shape[0] // 2
    top, bottom = block[:rows], block[rows:]
    return jnp.where(lane_low(top.shape), top, bottom)


def head_mask(rows_per, width):
    shape = (H * rows_per, width)
    row_head = lax.broadcasted_iota(jnp.int32, shape, 0) // rows_per
    col_head = lax.broadcasted_iota(jnp.int32, shape, 1) // (width // H)
    return row_head == col_head


def block_diagonal(v, mask):
    return jnp.where(mask, jnp.concatenate([v] * H, 0), jnp.zeros((), v.dtype))


def diagonal_blocks(v, mask):
    rows = v.shape[0] // H
    v = jnp.where(mask, v, 0.0)
    return jnp.sum(v.reshape(H, rows, v.shape[1]), 0)


def forward_body(
    place, lengths, tokens, memory, recv, attn_gain, query_weight, pair_weight, write_query, out_weight,
    ffn_gain, ffn_in, ffn_out,
    x, mem, nall, qs, kall, vall, p0, p1, p2, p3, mixed, resid, n2, act, dg,
    out_send, out_own, out, wqs,
):
    y = place[0]
    width = pair_weight.shape[0]
    rows = x.shape[0]
    slots = mem.shape[0]
    half = rows // 2
    x[...] = whole_rows(place, tokens, recv, 0, half)
    mem[...] = whole_rows(place, memory, recv, half, slots // 2)
    gain = attn_gain[...]
    xhat, _ = norm_parts(x[...].astype(F32))
    nx = (xhat * gain).astype(BF16)
    mhat, _ = norm_parts(mem[...].astype(F32))
    nm = (mhat * gain).astype(BF16)
    nall[0:slots, :] = nm
    nall[slots:128, :] = jnp.zeros((128 - slots, width), BF16)
    nall[128:, :] = nx
    qs[...] = (dot(nx, query_weight[...]) * 0.125).astype(BF16)
    na = nall[...]
    kall[...] = dot(na, pair_weight[:, :width]).astype(BF16)
    vall[...] = dot(na, pair_weight[:, width:]).astype(BF16)
    wqs[...] = (dot(nm, write_query[...]) * 0.125).astype(BF16)
    bounds = []
    total = 0
    for k in range(lengths.shape[1]):
        total = total + lengths[y, k]
        bounds.append(total)
    pos_c = lax.broadcasted_iota(jnp.int32, (1, rows), 1)
    doc_c = sum([(pos_c >= b).astype(jnp.int32) for b in bounds])
    mem_bias = jnp.where(
        lax.broadcasted_iota(jnp.int32, (128, 128), 1) < slots, 0.0, MASKED
    ).astype(F32)
    for i, p_out in enumerate((p0, p1, p2, p3)):
        w = 128 * (i + 2)
        cols = w - 128
        pos_r = lax.broadcasted_iota(jnp.int32, (128, 1), 0) + 128 * i
        doc_r = sum([(pos_r >= b).astype(jnp.int32) for b in bounds])
        ok = (doc_r == doc_c[:, :cols]) & (pos_c[:, :cols] <= pos_r)
        bias = jnp.concatenate([mem_bias, jnp.where(ok, 0.0, MASKED).astype(F32)], 1)
        for p in range(H // 2):
            lanes = slice(128 * p, 128 * p + 128)
            q01 = stacked_heads(qs[128 * i : 128 * i + 128, lanes])
            s = dot(q01, kall[0:w, lanes], 1, 1)
            s = (s.reshape(2, 128, w) + bias[None]).reshape(256, w)
            e = jnp.exp(s - jnp.max(s, -1, keepdims=True))
            pr = (e * (1.0 / jnp.sum(e, -1, keepdims=True))).astype(BF16)
            p_out[p] = pr
            o = dot(pr, vall[0:w, lanes])
            mixed[128 * i : 128 * i + 128, lanes] = unstacked_heads(o).astype(BF16)
    r = x[...].astype(F32) + dot(mixed[...], out_weight[...])
    resid[...] = r
    rhat, _ = norm_parts(r)
    n2v = (rhat * ffn_gain[...]).astype(BF16)
    n2[...] = n2v
    ff = ffn_in.shape[1]
    k0 = 0.7978845608028654
    for j in range(ff // 512):
        cols = slice(512 * j, 512 * j + 512)
        v = dot(n2v, ffn_in[:, cols])
        v2 = v * v
        t = jnp.tanh(k0 * (v + 0.044715 * (v2 * v)))
        h = 0.5 * (1.0 + t)
        act[:, cols] = (v * h).astype(BF16)
        d = h + (0.5 * v) * (1.0 - t * t) * (k0 + (3.0 * 0.044715 * k0) * v2)
        dg[:, cols] = d.astype(BF16)
    out[...] = (resid[...] + dot(act[...], ffn_out[...])).astype(BF16)
    out_own[...] = out[part(place, half, True), :]
    out_send[...] = out[part(place, half, False), :]


def write_body(
    place, out, wqs, mem, memory_cotangent, recv, write_pair, write_out, write_gate, write_gain, nall,
    send, keep, dwpair, dwquery, dblend, own_new, newmem, gain_out,
):
    c, ks = place[1], (send, keep)
    slots, width = wqs.shape
    o = out[...]
    wk = dot(o, write_pair[:, :width]).astype(BF16)
    wv = dot(o, write_pair[:, width:]).astype(BF16)
    mask = head_mask(slots, width)
    qbd = block_diagonal(wqs[...], mask)
    s = dot(qbd, wk, 1, 1)
    e = jnp.exp(s - jnp.max(s, -1, keepdims=True))
    pf = e * (1.0 / jnp.sum(e, -1, keepdims=True))
    pb = pf.astype(BF16)
    wmixed = diagonal_blocks(dot(pb, wv), mask).astype(BF16)
    update = dot(wmixed, write_out[...])
    update_low = update.astype(BF16)
    gate = jax.nn.sigmoid(dot(update_low, write_gate[...]))
    blended = mem[...].astype(F32) + gate * update
    bhat, br = norm_parts(blended)
    gain = write_gain[...]
    newmem[...] = (bhat * gain).astype(BF16)
    mhalf = slots // 2
    own_new[...] = newmem[part(place, mhalf, True), :]
    mc = whole_rows(place, memory_cotangent, recv, recv.shape[0] - mhalf, mhalf).astype(F32)
    d_blend, d_gain = norm_back(mc, bhat, br, gain)
    gain_out[...] = d_gain
    dblend[...] = d_blend
    d_gate_pre = (d_blend * update * gate * (1.0 - gate)).astype(BF16)
    d_update = (d_blend * gate + dot(d_gate_pre, write_gate[...], 1, 1)).astype(BF16)
    d_wmixed = dot(d_update, write_out[...], 1, 1).astype(BF16)
    emit_rows(dot(update_low, d_gate_pre, 0, 0), 32, ks, 128, c)
    emit_rows(dot(wmixed, d_update, 0, 0), 32, ks, 96, c)
    dbd = block_diagonal(d_wmixed, mask)
    dp = dot(dbd, wv, 1, 1)
    row = jnp.sum(pf * dp, -1, keepdims=True)
    ds = (pf * (dp - row)).astype(BF16)
    d_wquery = (diagonal_blocks(dot(ds, wk), mask) * 0.125).astype(BF16)
    dwquery[...] = d_wquery
    dwk = dot(ds, qbd, 0, 0).astype(BF16)
    dwv = dot(pb, dbd, 0, 0).astype(BF16)
    dwpair[:, :width] = dwk
    dwpair[:, width:] = dwv
    emit_rows(dot(nall[0:slots, :], d_wquery, 0, 0), 32, ks, 0, c)
    emit_rows(dot(o, dwk, 0, 0), 32, ks, 32, c)
    emit_rows(dot(o, dwv, 0, 0), 32, ks, 64, c)


def ffn_back_body(
    place, dwpair, write_pair, out_cotangent, recv, ffn_out, dg, act,
    send, keep, dout_out, dinner,
):
    c, ks = place[1], (send, keep)
    ff, width = ffn_out.shape
    deep = ff // GROUPS
    cot = whole_rows(place, out_cotangent, recv, 0, out_cotangent.shape[1])
    d_out = cot.astype(F32) + dot(dwpair[...], write_pair[...], 1, 1)
    dout_out[...] = d_out
    d_branch = d_out.astype(BF16)
    for j in range(ff // 512):
        cols = slice(512 * j, 512 * j + 512)
        d_act = dot(d_branch, ffn_out[cols, :], 1, 1).astype(BF16)
        dinner[:, cols] = (d_act.astype(F32) * dg[:, cols].astype(F32)).astype(BF16)
        emit_rows(
            dot(act[:, cols], d_branch, 0, 0), deep, ks, 0, c, 512 // (2 * deep) * j,
        )


def inner_back_body(
    place, dinner, n2, ffn_in,
    send, keep, total,
):
    rows = ffn_in.shape[0] // GROUPS
    for j in range(ffn_in.shape[1] // 512):
        cols = slice(512 * j, 512 * j + 512)
        emit_rows(dot(n2[...], dinner[:, cols], 0, 0), rows, (send, keep), rows * j, place[1])
    total[...] = dot(dinner[...], ffn_in[...], 1, 1)


def resid_back_body(
    place, total, dout, resid, ffn_gain, out_weight, mixed,
    send, keep, dresid, dmixed, gain_out,
):
    rhat, rr = norm_parts(resid[...])
    d_norm, d_gain = norm_back(total[...], rhat, rr, ffn_gain[...])
    gain_out[...] = d_gain
    d = dout[...] + d_norm
    dresid[...] = d
    d_attn = d.astype(BF16)
    emit_rows(dot(mixed[...], d_attn, 0, 0), 32, (send, keep), 0, place[1])
    dmixed[...] = dot(d_attn, out_weight[...], 1, 1).astype(BF16)


def attn_back_body(
    place, qs, dm, vall, p3, kall, p2, p1, p0,
    dq_out, dk_out, dv_out, dk_ref, dv_ref,
):
    for p in range(H // 2):
        lanes = slice(128 * p, 128 * p + 128)
        for i, p_in in reversed(list(enumerate((p0, p1, p2, p3)))):
            w = 128 * (i + 2)
            rows = slice(128 * i, 128 * i + 128)
            q01 = stacked_heads(qs[rows, lanes])
            dm01 = stacked_heads(dm[rows, lanes])
            dp = dot(dm01, vall[0:w, lanes], 1, 1)
            pb = p_in[p]
            pf = pb.astype(F32)
            t = pf * dp
            ds = (t - pf * jnp.sum(t, -1, keepdims=True)).astype(BF16)
            dq = unstacked_heads(dot(ds, kall[0:w, lanes])) * 0.125
            dq_out[rows, lanes] = dq.astype(BF16)
            dk = dot(ds, q01, 0, 0)
            dv = dot(pb, dm01, 0, 0)
            if i == 3:
                dk_ref[0:w, lanes] = dk
                dv_ref[0:w, lanes] = dv
            else:
                dk_ref[0:w, lanes] += dk
                dv_ref[0:w, lanes] += dv
    dk_out[...] = dk_ref[...].astype(BF16)
    dv_out[...] = dv_ref[...].astype(BF16)


def input_back_body(
    place, nall, dq, dk, dv, pair_weight, query_weight, dwquery, write_query, x, mem, attn_gain,
    dresid, dblend, gain2, gain3, newmem,
    send, keep, own_tok, own_mem, swap, gtok, gmem,
):
    c, ks = place[1], (send, keep)
    rows, width = x.shape
    slots = mem.shape[0]
    half, mhalf = rows // 2, slots // 2
    na = nall[...]
    dqv = dq[...]
    emit_rows(dot(na[128:], dqv, 0, 0), 32, ks, 0, c)
    emit_rows(dot(na, dk[...], 0, 0), 32, ks, 32, c)
    emit_rows(dot(na, dv[...], 0, 0), 32, ks, 64, c)
    d_all = dot(dk[...], pair_weight[:, :width], 1, 1)
    d_all = d_all + dot(dv[...], pair_weight[:, width:], 1, 1)
    d_nx = d_all[128:] + dot(dqv, query_weight[...], 1, 1)
    d_nm = d_all[:slots] + dot(dwquery[...], write_query[...], 1, 1)
    gain = attn_gain[...]
    xhat, xr = norm_parts(x[...].astype(F32))
    d_x, g_x = norm_back(d_nx, xhat, xr, gain)
    mhat, mr = norm_parts(mem[...].astype(F32))
    d_m, g_m = norm_back(d_nm, mhat, mr, gain)
    gains = jnp.concatenate(
        [g_x + g_m, gain2[...], gain3[...], jnp.zeros((13, width), F32)], 0
    ).astype(BF16)
    for one in ks:
        one[:, 96:112, :] = jnp.broadcast_to(gains, (GROUPS // 2, 16, width))
    gtok[...] = dresid[...] + d_x
    gmem[...] = dblend[...] + d_m
    own_tok[...] = gtok[part(place, half, True), :]
    own_mem[...] = gmem[part(place, mhalf, True), :]
    other = part(place, half, False)
    mother = part(place, mhalf, False)
    swap[0:half, :] = gtok[other, :].astype(BF16)
    swap[half : half + mhalf, :] = newmem[mother, :]
    swap[half + mhalf :, :] = gmem[mother, :].astype(BF16)


BIT = {"y": 0, "x": 2, "z": 3, "h": 4}


def other_of(axis, bit):
    return [(i, i ^ bit) for i in range(lax.axis_size(axis))]


def exchanged(send, label):
    if label == "y":
        return lax.ppermute(send, "seq", other_of("seq", 1))
    return lax.ppermute(send, "seg", other_of("seg", {"x": 2, "z": 4, "h": 8, "c": 1}[label]))


class Stream:
    def __init__(self, keep, recv, dims, start, rows):
        self.keep, self.recv, self.dims, self.start, self.rows = keep, recv, dims, start, rows


def stage(streams, labels, joined=False, deps=(), tail=False):
    ins = []
    index = {}
    for s in streams:
        for arr in (s.keep, s.recv):
            if id(arr) not in index:
                index[id(arr)] = len(ins)
                ins.append(("v", arr))
    n_arrays = len(ins)
    ins += [("d", d) for d in deps]
    width = streams[0].keep.shape[-1]
    shapes, new_dims, new_rows = [], [], []
    for s, label in zip(streams, labels):
        rows = s.rows // 2 if label == "y" else s.rows
        dims = s.dims.replace(label, "")
        new_dims.append(dims)
        new_rows.append(rows)
        shapes.append((2,) * len(dims) + (rows, width))
    if joined:
        shapes = [(sum(new_rows), width)]
    if tail:
        shapes = shapes[:-2] + [shapes[-2][:-2] + (new_rows[-2] + new_rows[-1], width)]
    outs = []
    for shape in shapes:
        outs += [(shape, BF16)] * 2

    def body(place, *refs):
        given, made = refs[:n_arrays], refs[n_arrays:]

        def value(s, label, own, arr):
            bit = place[BIT[label]]
            bit = bit if own else 1 - bit
            where = []
            for d in s.dims:
                where.append(bit if d == label else slice(None))
            if label == "y":
                half = s.rows // 2
                where.append(pl.ds(pl.multiple_of(s.start + bit * half, 16), half))
            else:
                where.append(slice(s.start, s.start + s.rows))
            return given[index[id(arr)]][tuple(where) + (slice(None),)].astype(F32)

        for own in (False, True):
            at = 0
            for k, (s, label) in enumerate(zip(streams, labels)):
                total = (value(s, label, own, s.keep) + value(s, label, own, s.recv)).astype(BF16)
                last = tail and k == len(streams) - 1
                target = made[(0 if joined else 2 * (k - last)) + (0 if own else 1)]
                if joined:
                    target[at : at + new_rows[k], :] = total
                    at += new_rows[k]
                elif last:
                    target[..., new_rows[k - 1] :, :] = total
                elif tail and k == len(streams) - 2:
                    target[..., : new_rows[k], :] = total
                else:
                    target[...] = total

    results = call(body, ins, outs, flops=10**6, nbytes=10**6)
    if joined:
        return results[0], results[1]
    if tail:
        new_rows = new_rows[:-2] + [new_rows[-2] + new_rows[-1]]
    return [
        (results[2 * k], results[2 * k + 1], new_dims[k], n) for k, n in enumerate(new_rows)
    ]


def added(keep, recv, deps=()):
    def body(place, keep, recv, total):
        total[...] = (keep[...].astype(F32) + recv[...].astype(F32)).astype(BF16)

    (total,) = call(
        body,
        [("v", keep), ("v", recv)] + [("d", d) for d in deps],
        [(keep.shape, BF16)],
        flops=10**6, nbytes=10**6,
    )
    return total


def in_hbm(a):
    return pltpu.with_memory_space_constraint(a, pltpu.HBM)


def packed(body_rows, extra_rows):
    half, width = body_rows.shape[1:]
    extra = extra_rows.shape[1]

    def kernel(a, b, o, sem):
        other = 1 - lax.axis_index("seq")
        copies = [
            pltpu.make_async_copy(a.at[other], o.at[0:half], sem.at[0]),
            pltpu.make_async_copy(b.at[other], o.at[half:], sem.at[1]),
        ]
        for copy in copies:
            copy.start()
        for copy in copies:
            copy.wait()

    return pl.pallas_call(
        kernel,
        out_shape=pltpu.VMEM((half + extra, width), body_rows.dtype),
        in_specs=[pl.BlockSpec(memory_space=pltpu.HBM)] * 2,
        out_specs=pl.BlockSpec(memory_space=pltpu.VMEM),
        scratch_shapes=[pltpu.SemaphoreType.DMA((2,))],
        compiler_params=pltpu.CompilerParams(vmem_limit_bytes=4 * 1024 * 1024),
    )(in_hbm(body_rows), in_hbm(extra_rows))


def assembled(own, recv, dtypes, deps=()):
    width = own[0].shape[1]

    def body(place, *refs):
        n = len(own)
        start = 0
        for mine, out in zip(refs[:n], refs[n + 1 :]):
            rows = mine.shape[0]
            out[place[0]] = mine[...].astype(out.dtype)
            out[1 - place[0]] = refs[n][start : start + rows, :].astype(out.dtype)
            start += rows

    return call(
        body,
        [("v", a) for a in own] + [("v", recv)] + [("d", d) for d in deps],
        [((2,) + a.shape, d) for a, d in zip(own, dtypes)],
        flops=10**6, nbytes=10**6, home=False,
    )


def fetched_weights(weights):
    def kernel(*refs):
        n = len(weights)
        copies = [
            pltpu.make_async_copy(refs[k], refs[n + k], refs[-1].at[k]) for k in range(n)
        ]
        for copy in copies:
            copy.start()
        for copy in copies:
            copy.wait()

    return pl.pallas_call(
        kernel,
        out_shape=[pltpu.VMEM(a.shape, a.dtype) for a in weights],
        in_specs=[pl.BlockSpec(memory_space=pltpu.HBM)] * len(weights),
        out_specs=[pl.BlockSpec(memory_space=pltpu.VMEM)] * len(weights),
        scratch_shapes=[pltpu.SemaphoreType.DMA((len(weights),))],
        compiler_params=pltpu.CompilerParams(vmem_limit_bytes=4 * 1024 * 1024),
        cost_estimate=pl.CostEstimate(flops=10**9, bytes_accessed=10**7, transcendentals=0),
    )(*[in_hbm(a) for a in weights])


def reduced_any(keep, send, pieces):
    groups = lax.axis_size("seg")
    c = lax.axis_index("seg") % 2
    first = jnp.where(c == 0, keep, send)
    second = jnp.where(c == 0, send, keep)
    total = jnp.stack([first, second], 1)
    total = total.reshape((GROUPS,) + keep.shape[1:])
    fine = groups // GROUPS
    parts = []
    at = 0
    for rows, shared in pieces:
        piece = total[:, at : at + rows]
        if shared:
            piece = jnp.broadcast_to(piece[:, None], (GROUPS, fine) + piece.shape[1:])
        else:
            piece = piece.reshape(GROUPS, fine, rows // fine, piece.shape[2])
        parts.append(piece.reshape(groups, -1, piece.shape[-1]))
        at += rows
    total = jnp.concatenate(parts, 1)
    total = lax.psum_scatter(total.astype(F32), "seg", scatter_dimension=0, tiled=True)[0]
    return lax.psum(total, "seq")


def final_parts(one, two, ff):
    t1, o1, split = one
    t2, o2 = two
    width = t1.shape[-1]
    r = width // GROUPS
    n = ff // 512
    shapes = [
        (r, width), (r, 2 * width), (r, width), (r, ff), (ff // GROUPS, width),
        (r, width), (r, 2 * width), (r, width), (r, width), (r,), (r,), (r,),
    ]

    def body(place, t1, o1, t2, o2, gq, gp, go, gfi, gfo, gwq, gwp, gwo, gwg, g0, g1, g2, full):
        y = place[0]
        at = start = 0
        for rows in split:
            half = rows // 2
            for ref, index in ((t1, y), (o1, 1 - y)):
                full[pl.ds(pl.multiple_of(start + index * half, 16), half), :] = ref[
                    at : at + half, :
                ].astype(F32)
            at += half
            start += rows
        total = (t2[...].astype(F32) + o2[...].astype(F32))
        gq[...] = total[0:r, :]
        gp[:, :width] = total[r : 2 * r, :]
        gp[:, width:] = total[2 * r : 3 * r, :]
        seg = lax.axis_index("seg")
        gains = pltpu.roll(total[3 * r : 3 * r + 8, :], (width - seg * r) % width, 1)
        for k, ref in enumerate((g0, g1, g2)):
            ref[...] = gains[k, :r]
        gwq[...] = full[0:r, :]
        gwp[:, :width] = full[r : 2 * r, :]
        gwp[:, width:] = full[2 * r : 3 * r, :]
        gwo[...] = full[3 * r : 4 * r, :]
        gwg[...] = full[4 * r : 5 * r, :]
        for j in range(n):
            gfi[:, 512 * j : 512 * j + 512] = full[(5 + j) * r : (6 + j) * r, :]
        gfo[...] = full[(5 + n) * r : (5 + n) * r + ff // GROUPS, :]
        go[...] = full[(5 + n) * r + ff // GROUPS :, :]

    return call(
        body, [("v", a) for a in (t1, o1, t2, o2)], [(s, F32) for s in shapes],
        scratch=[((sum(split), width), F32)], flops=10**6, nbytes=10**6, home=False,
    )


def shards(
    tokens, memory, lengths, attn_gain, query_weight, pair_weight, out_weight, ffn_gain, ffn_in,
    ffn_out, write_query, write_pair, write_out, write_gate, write_gain, out_cotangent,
    memory_cotangent,
):
    half, width = tokens.shape[1:]
    mhalf = memory.shape[1]
    rows, slots, ff = 2 * half, 2 * mhalf, ffn_in.shape[1]
    padded = rows + 128
    groups = lax.axis_size("seg")
    recv_a = exchanged(packed(tokens, memory), "y")
    recv_b = exchanged(packed(out_cotangent, memory_cotangent), "y")
    (
        tokens, memory, out_cotangent, memory_cotangent, query_weight, pair_weight, out_weight,
        ffn_in, ffn_out, write_query, write_pair, write_out, write_gate,
    ) = fetched_weights(
        (
            tokens, memory, out_cotangent, memory_cotangent, query_weight, pair_weight, out_weight,
            ffn_in, ffn_out, write_query, write_pair, write_out, write_gate,
        )
    )
    ag, fg, wg = attn_gain[None], ffn_gain[None], write_gain[None]
    v = lambda *arrs: [("v", a) for a in arrs]
    h = lambda *arrs: [("h", a) for a in arrs]
    deps = lambda *arrs: [("d", a) for a in arrs]
    big = ((rows, width), BF16)
    wide = ((padded, width), BF16)
    deep = ((rows, ff), BF16)
    half_b = ((half, width), BF16)
    keep_send = lambda n: [((GROUPS // 2, n, width), BF16)] * 2
    small = ((slots, width), BF16)
    full_f = ((rows, width), F32)
    gain_row = ((1, width), F32)
    (
        x, mem, nall, qs, kall, vall, p0, p1, p2, p3, mixed, resid, n2, act, dg,
        out_send, out_own, out, wqs,
    ) = call(
        forward_body,
        [("s", lengths)] + v(tokens, memory, recv_a, ag, query_weight, pair_weight)
        + v(write_query, out_weight, fg, ffn_in, ffn_out),
        [big, small, wide, big, wide, wide]
        + [((H // 2, 256, 128 * (i + 2)), BF16) for i in range(4)]
        + [big, full_f, big, deep, deep, half_b, half_b, big, small],
        flops=2 * 6 * 10**9, nbytes=20 * 10**6, limit=16,
    )
    out_recv = exchanged(out_send, "y")
    send0, keep0, dwpair, dwquery, dblend, own_new, newmem, gain3 = call(
        write_body,
        v(out, wqs, mem, memory_cotangent, recv_b, write_pair, write_out, write_gate, wg, nall),
        [
            *keep_send(160), ((rows, 2 * width), BF16), small,
            ((slots, width), F32), ((mhalf, width), BF16), small, gain_row,
        ],
        flops=2 * 3 * 10**9, nbytes=10 * 10**6,
    )
    small_mesh = groups == GROUPS
    cube = lambda a: a.reshape((2, 2, 2) + a.shape[1:])
    pair = lambda keep, send: (cube(keep), cube(exchanged(send, "c")))
    deps0 = deps1 = []
    send1, keep1, dout, dinner = call(
        ffn_back_body,
        v(dwpair, write_pair, out_cotangent, recv_b, ffn_out, dg, act) + deps(out_recv),
        [*keep_send(128), full_f, deep],
        flops=2 * 5 * 10**9, nbytes=20 * 10**6,
    )
    if small_mesh:
        send0, _ = lax.optimization_barrier((send0, out_recv))
        k0, r0 = pair(keep0, send0)
        deps0 = deps(r0)
    send4, keep4, total = call(
        inner_back_body, v(dinner, n2, ffn_in) + deps0, [*keep_send(128), full_f],
        flops=10**9, nbytes=20 * 10**6,
    )
    if small_mesh:
        k1, r1 = pair(keep1, send1)
        deps0 = deps(r1)
    send3, keep3, dresid, dmixed, gain2 = call(
        resid_back_body, v(total, dout, resid, fg, out_weight, mixed) + deps0,
        [*keep_send(32), full_f, big, gain_row],
        flops=10**8, nbytes=10**6,
    )
    orders = ("xyz", "yzx", "zxy")
    late_orders = ("xz", "zx")

    def moved(parts, labels):
        return [
            Stream(keep, exchanged(send, label), dims, 0, r)
            for label, (keep, send, dims, r) in zip(labels, parts)
        ]

    nth = lambda these, step: [o[step] for o in these]
    if small_mesh:
        k4, r4 = pair(keep4, send4)
        k3, r3 = pair(keep3, send3)
        streams = [
            Stream(k0, r0, "hzx", 0, 160), Stream(k4, r4, "hzx", 0, 128),
            Stream(k1, r1, "hzx", 0, 128), Stream(k3, r3, "hzx", 0, 32),
        ]
        parts = stage_joined(streams, nth(orders, 0), [])
        deps1 = deps(parts[0][0])
        first = moved(parts, nth(orders, 0))
    dq, dk, dv = call(
        attn_back_body,
        v(qs, dmixed, vall, p3, kall, p2, p1, p0) + deps1,
        [big, wide, wide],
        scratch=[((padded, width), F32)] * 2,
        flops=2 * 6 * 10**9, nbytes=20 * 10**6,
    )
    send2, keep2, own_tok, own_mem, swap = call(
        input_back_body,
        v(
            nall, dq, dk, dv, pair_weight, query_weight, dwquery, write_query, x, mem, ag, dresid,
            dblend, gain2, gain3, newmem,
        ),
        [
            *keep_send(112), ((half, width), F32), ((mhalf, width), F32),
            ((half + 2 * mhalf, width), BF16),
        ],
        scratch=[((rows, width), F32), ((slots, width), F32)],
        flops=2 * 3 * 10**9, nbytes=20 * 10**6,
    )
    r = width // groups
    (out_both,) = assembled([out_own], out_recv, [BF16])
    if small_mesh:
        chain = [send2]

        def each(streams, labels):
            results = []
            for stream, label in zip(streams, labels):
                ((keep, send, dims, n),) = stage([stream], [label], deps=chain[-1:])
                results.append((keep, send, dims, n))
                chain.append(keep)
            return moved(results, labels)

        second = each(first, nth(orders, 1))
        send2, swap, _ = lax.optimization_barrier((send2, swap, chain[-1]))
        k2, r2 = pair(keep2, send2)
        late = [Stream(k2, r2, "hzx", 0, 64), Stream(k2, r2, "hzx", 64, 48)]
        late = each(late, nth(late_orders, 0))
        third = each(second, nth(orders, 2))
        late = late_second = each(late, nth(late_orders, 1))
        late = [chain[-1:]]
        keep, send = stage(third, "hhh", joined=True, deps=[late[0][0]])
        recv = exchanged(send, "h")
        late_keep, late_send = stage(late_second, "hh", joined=True, deps=[keep])
        late_recv = exchanged(late_send, "h")
        t1 = added(keep, recv, deps=[late_keep])
        o1 = exchanged(t1, "y")
        t2 = added(late_keep, late_recv, deps=[t1])
        o2 = exchanged(t2, "y")
        gq, gp, go, gfi, gfo, gwq, gwp, gwo, gwg, *gains = final_parts(
            (t1, o1, (160, 128, 160)), (t2, o2), ff
        )
    else:
        w = width // GROUPS
        w0 = reduced_any(keep0, send0, [(w, False)] * 5)
        gfo = reduced_any(keep1, send1, [(ff // GROUPS, False)])
        w1 = reduced_any(keep4, send4, [(w, False)] * (ff // 512))
        w2 = reduced_any(keep2, send2, [(w, False)] * 3 + [(16, True)])
        go = reduced_any(keep3, send3, [(w, False)])
        cut = lambda a, at, n: jnp.concatenate(
            [a[(at + i) * r : (at + i + 1) * r] for i in range(n)], 1
        )
        gq, gp = cut(w2, 0, 1), cut(w2, 1, 2)
        gfi = cut(w1, 0, ff // 512)
        gwq, gwp, gwo, gwg = cut(w0, 0, 1), cut(w0, 1, 2), cut(w0, 3, 1), cut(w0, 4, 1)
        at = lax.axis_index("seg") * r
        gains = [lax.dynamic_slice_in_dim(w2[3 * r + i], at, r, 0) for i in range(3)]
    swapped = exchanged(swap, "y")
    tok_both, new_both, mem_both = assembled([own_tok, own_new, own_mem], swapped, [F32, BF16, F32])
    return (
        out_both, new_both, tok_both, mem_both,
        gains[0], gq, gp, go, gains[1], gfi, gfo, gwq, gwp, gwo, gwg, gains[2],
    )


def stage_joined(streams, labels, deps):
    return stage(streams, list(labels) + [labels[-1]], tail=True, deps=deps)


def solution(mesh):
    row = P("seg", "seq", None)
    grad = P("seg", None)
    in_specs = (row, row, P("seg", None)) + (P(),) * 12 + (row, row)
    out_specs = (row, row, row, row, P("seg"), grad, grad, grad, P("seg")) + (grad,) * 6 + (P("seg"),)
    return jax.shard_map(shards, mesh=mesh, in_specs=in_specs, out_specs=out_specs, check_vma=False)
```

```python
import jax
import jax.numpy as jnp
from jax import lax
from jax.experimental import pallas as pl
from jax.experimental.pallas import tpu as pltpu
from jax.sharding import PartitionSpec as P

H = 8
GROUPS = 16
EPSILON = 1e-05
MASKED = -1e30
F32 = jnp.float32
BF16 = jnp.bfloat16
VMEM_LIMIT = 56 * 1024 * 1024


def part(place, half, own):
    index = place[0] if own else 1 - place[0]
    return pl.ds(pl.multiple_of(index * half, half), half)


class Fetched:
    def __init__(self, source, ref, sem):
        self.ref, self.copy, self.waited = ref, pltpu.make_async_copy(source, ref, sem), False

    def __call__(self):
        if not self.waited:
            self.copy.wait()
            self.waited = True
        return self.ref


def position():
    seg = lax.axis_index("seg")
    return [lax.axis_index("seq")] + [(seg >> k) & 1 for k in range(4)]


def call(body, ins, outs, scratch=(), flops=0, nbytes=0, limit=16, home=True):
    kinds = [kind for kind, _ in ins]
    arrays = [
        pltpu.with_memory_space_constraint(a, pltpu.VMEM) if kind == "v" else a for kind, a in ins
    ]
    spaces = {"s": pltpu.SMEM, "v": pltpu.VMEM, "d": pl.ANY, "h": pl.ANY}
    fetched = [pltpu.VMEM(a.shape, a.dtype) for kind, a in ins if kind == "h"]
    n_io = len(ins) + len(outs)

    def kernel(*refs):
        given, at = [], 0
        for kind, r in zip(kinds, refs):
            if kind == "h":
                r = Fetched(r, refs[n_io + at], refs[-1].at[at])
                r.copy.start()
                at += 1
            if kind != "d":
                given.append(r)
        end = -1 if fetched else len(refs)
        body(position(), *given, *refs[len(ins) : n_io], *refs[n_io + at : end])
        for r in given:
            if isinstance(r, Fetched):
                r()

    shape = (lambda s, d: pltpu.VMEM(s, d)) if home else jax.ShapeDtypeStruct
    sems = [pltpu.SemaphoreType.DMA((len(fetched),))] if fetched else []
    return pl.pallas_call(
        kernel,
        out_shape=[shape(s, d) for s, d in outs],
        in_specs=[pl.BlockSpec(memory_space=spaces[kind]) for kind in kinds],
        out_specs=[pl.BlockSpec(memory_space=pltpu.VMEM)] * len(outs),
        scratch_shapes=fetched + [pltpu.VMEM(s, d) for s, d in scratch] + sems,
        compiler_params=pltpu.CompilerParams(vmem_limit_bytes=limit * 1024 * 1024),
        cost_estimate=pl.CostEstimate(flops=flops, bytes_accessed=nbytes, transcendentals=0),
    )(*arrays)


def dot(a, b, ca=1, cb=0):
    return lax.dot_general(a, b, (((ca,), (cb,)), ((), ())), preferred_element_type=F32)


def norm_parts(v):
    centred = v - jnp.mean(v, -1, keepdims=True)
    r = lax.rsqrt(jnp.mean(centred * centred, -1, keepdims=True) + EPSILON)
    return centred * r, r


def norm_back(dy, xhat, r, gain):
    dx = dy * gain
    m1 = jnp.mean(dx, -1, keepdims=True)
    m2 = jnp.mean(dx * xhat, -1, keepdims=True)
    return r * (dx - m1 - xhat * m2), jnp.sum(dy * xhat, 0, keepdims=True)


def emit_rows(grad, rows, ks_ref, offset, c, first=0):
    pairs = grad.shape[0] // (2 * rows)
    g = grad.astype(BF16).reshape(pairs, 2, rows, grad.shape[1])
    where = (slice(first, first + pairs), slice(offset, offset + rows), slice(None))
    even, odd = g[:, 0], g[:, 1]
    send_ref, keep_ref = ks_ref
    keep_ref[where] = jnp.where(c == 0, even, odd)
    send_ref[where] = jnp.where(c == 0, odd, even)


def whole_rows(place, pair_ref, recv_ref, start, half):
    own, other = pair_ref[place[0]], recv_ref[start : start + half, :]
    first = place[0] == 0
    return jnp.concatenate([jnp.where(first, own, other), jnp.where(first, other, own)], 0)


def lane_low(shape):
    return lax.broadcasted_iota(jnp.int32, shape, 1) < 64


def stacked_heads(block):
    low = lane_low(block.shape)
    zero = jnp.zeros_like(block)
    return jnp.concatenate([jnp.where(low, block, zero), jnp.where(low, zero, block)], 0)


def unstacked_heads(block):
    rows = block.shape[0] // 2
    top, bottom = block[:rows], block[rows:]
    return jnp.where(lane_low(top.shape), top, bottom)


def head_mask(rows_per, width):
    shape = (H * rows_per, width)
    row_head = lax.broadcasted_iota(jnp.int32, shape, 0) // rows_per
    col_head = lax.broadcasted_iota(jnp.int32, shape, 1) // (width // H)
    return row_head == col_head


def block_diagonal(v, mask):
    return jnp.where(mask, jnp.concatenate([v] * H, 0), jnp.zeros((), v.dtype))


def diagonal_blocks(v, mask):
    rows = v.shape[0] // H
    v = jnp.where(mask, v, 0.0)
    return jnp.sum(v.reshape(H, rows, v.shape[1]), 0)


def in_steps(items, stages):
    held = {}
    for step in range(len(items) + len(stages) - 1):
        for k, stage_of in enumerate(stages):
            n = step - k
            if 0 <= n < len(items):
                given = () if k == 0 else (held.pop((n, k - 1)),)
                held[n, k] = stage_of(*items[n], *given)


def forward_body(
    place, lengths, tokens, memory, recv, attn_gain, query_weight, pair_weight, write_query, out_weight,
    ffn_gain, ffn_in, ffn_out,
    x, mem, nall, qs, kall, vall, p0, p1, p2, p3, mixed, resid, n2, act, dg,
    out_send, out_own, out, wqs, kt, vt,
):
    y = place[0]
    width = pair_weight.shape[0]
    rows = x.shape[0]
    slots = mem.shape[0]
    half = rows // 2
    x[...] = whole_rows(place, tokens, recv, 0, half)
    mem[...] = whole_rows(place, memory, recv, half, slots // 2)
    gain = attn_gain[...]
    xhat, _ = norm_parts(x[...].astype(F32))
    nx = (xhat * gain).astype(BF16)
    mhat, _ = norm_parts(mem[...].astype(F32))
    nm = (mhat * gain).astype(BF16)
    nall[0:slots, :] = nm
    nall[slots:128, :] = jnp.zeros((128 - slots, width), BF16)
    nall[128:, :] = nx
    qs[...] = (dot(nx, query_weight[...]) * 0.125).astype(BF16)
    na = nall[...]
    kall[...] = dot(na, pair_weight[:, :width]).astype(BF16)
    vall[...] = dot(na, pair_weight[:, width:]).astype(BF16)
    wqs[...] = (dot(nm, write_query[...]) * 0.125).astype(BF16)
    bounds = []
    total = 0
    for k in range(lengths.shape[1]):
        total = total + lengths[y, k]
        bounds.append(total)
    pos_k = lax.broadcasted_iota(jnp.int32, (rows, 1), 0)
    doc_k = sum([(pos_k >= b).astype(jnp.int32) for b in bounds])
    mem_bias = jnp.where(
        lax.broadcasted_iota(jnp.int32, (128, 128), 0) < slots, 0.0, MASKED
    ).astype(F32)
    kt[...] = kall[...].T
    vt[...] = vall[...].T
    biases = []
    for i in range(4):
        cols = 128 * (i + 1)
        pos_q = lax.broadcasted_iota(jnp.int32, (1, 128), 1) + 128 * i
        doc_q = sum([(pos_q >= b).astype(jnp.int32) for b in bounds])
        ok = (doc_k[:cols] == doc_q) & (pos_k[:cols] <= pos_q)
        bias = jnp.concatenate([mem_bias, jnp.where(ok, 0.0, MASKED).astype(F32)], 0)
        biases.append(jnp.concatenate([bias, bias], 1))

    def score(i, p):
        w, lanes = 128 * (i + 2), slice(128 * p, 128 * p + 128)
        q01 = stacked_heads(qs[128 * i : 128 * i + 128, lanes])
        return dot(kall[0:w, lanes], q01, 1, 1)

    def soften(i, p, s):
        s = s + biases[i]
        e = jnp.exp(s - jnp.max(s, 0, keepdims=True))
        pr = (e * (1.0 / jnp.sum(e, 0, keepdims=True))).astype(BF16)
        (p0, p1, p2, p3)[i][p] = pr
        return pr

    def mix(i, p, pr):
        w, lanes = 128 * (i + 2), slice(128 * p, 128 * p + 128)
        queries = slice(128 * i, 128 * i + 128)
        o = dot(vt[lanes, 0:w], pr).astype(BF16)
        mixed[128 * p : 128 * p + 64, queries] = o[:64, :128]
        mixed[128 * p + 64 : 128 * p + 128, queries] = o[64:, 128:]

    in_steps(
        [(i, p) for i in range(4) for p in range(H // 2)], (score, soften, mix)
    )
    ff = ffn_in.shape[1]
    k0 = 0.7978845608028654
    step = 512
    chunks = ff // step

    def top(block):
        at = slice(half * block, half * block + half)
        r = x[at, :].astype(F32) + dot(mixed[:, at], out_weight[...], 0, 0)
        resid[at, :] = r
        rhat, _ = norm_parts(r)
        n2[at, :] = (rhat * ffn_gain[...]).astype(BF16)

    def inner(block, j):
        if block == 0 and j == 1:
            top(1)
        return dot(n2[half * block : half * block + half, :], ffn_in[:, step * j : step * j + step])

    def gelu(block, j, v):
        at = (slice(half * block, half * block + half), slice(step * j, step * j + step))
        v2 = v * v
        h = 0.5 * jnp.tanh(v * (k0 + (0.044715 * k0) * v2)) + 0.5
        act[at] = (v * h).astype(BF16)
        w = v * (2.0 * k0 + (6.0 * 0.044715 * k0) * v2)
        dg[at] = (h + h * (1.0 - h) * w).astype(BF16)

    def bottom(block):
        at = slice(half * block, half * block + half)
        out[at, :] = (resid[at, :] + dot(act[at, :], ffn_out[...])).astype(BF16)

    top(0)
    held = None
    for n in range(2 * chunks + 1):
        now = None
        if n < 2 * chunks:
            now = inner(n // chunks, n % chunks)
        if held is not None:
            gelu(*held)
        if n == chunks + 1:
            bottom(0)
        held = (n // chunks, n % chunks, now)
    bottom(1)
    out_own[...] = out[part(place, half, True), :]
    out_send[...] = out[part(place, half, False), :]


def write_body(
    place, out, wqs, mem, memory_cotangent, recv, write_pair, write_out, write_gate, write_gain, nall,
    send, keep, dwpair, dwquery, dblend, own_new, newmem, gain_out,
):
    c, ks = place[1], (send, keep)
    slots, width = wqs.shape
    o = out[...]
    wk = dot(o, write_pair[:, :width]).astype(BF16)
    wv = dot(o, write_pair[:, width:]).astype(BF16)
    mask = head_mask(slots, width)
    qbd = block_diagonal(wqs[...], mask)
    s = dot(qbd, wk, 1, 1)
    e = jnp.exp(s - jnp.max(s, -1, keepdims=True))
    pf = e * (1.0 / jnp.sum(e, -1, keepdims=True))
    pb = pf.astype(BF16)
    wmixed = diagonal_blocks(dot(pb, wv), mask).astype(BF16)
    update = dot(wmixed, write_out[...])
    update_low = update.astype(BF16)
    gate = jax.nn.sigmoid(dot(update_low, write_gate[...]))
    blended = mem[...].astype(F32) + gate * update
    bhat, br = norm_parts(blended)
    gain = write_gain[...]
    newmem[...] = (bhat * gain).astype(BF16)
    mhalf = slots // 2
    own_new[...] = newmem[part(place, mhalf, True), :]
    mc = whole_rows(place, memory_cotangent, recv, recv.shape[0] - mhalf, mhalf).astype(F32)
    d_blend, d_gain = norm_back(mc, bhat, br, gain)
    gain_out[...] = d_gain
    dblend[...] = d_blend
    d_gate_pre = (d_blend * update * gate * (1.0 - gate)).astype(BF16)
    d_update = (d_blend * gate + dot(d_gate_pre, write_gate[...], 1, 1)).astype(BF16)
    d_wmixed = dot(d_update, write_out[...], 1, 1).astype(BF16)
    emit_rows(dot(update_low, d_gate_pre, 0, 0), 32, ks, 128, c)
    emit_rows(dot(wmixed, d_update, 0, 0), 32, ks, 96, c)
    dbd = block_diagonal(d_wmixed, mask)
    dp = dot(dbd, wv, 1, 1)
    row = jnp.sum(pf * dp, -1, keepdims=True)
    ds = (pf * (dp - row)).astype(BF16)
    d_wquery = (diagonal_blocks(dot(ds, wk), mask) * 0.125).astype(BF16)
    dwquery[...] = d_wquery
    dwk = dot(ds, qbd, 0, 0).astype(BF16)
    dwv = dot(pb, dbd, 0, 0).astype(BF16)
    dwpair[:, :width] = dwk
    dwpair[:, width:] = dwv
    emit_rows(dot(nall[0:slots, :], d_wquery, 0, 0), 32, ks, 0, c)
    emit_rows(dot(o, dwk, 0, 0), 32, ks, 32, c)
    emit_rows(dot(o, dwv, 0, 0), 32, ks, 64, c)


def ffn_back_body(
    place, dwpair, write_pair, out_cotangent, recv, ffn_out, dg, act,
    send, keep, dout_out, dinner,
):
    c, ks = place[1], (send, keep)
    ff, width = ffn_out.shape
    deep = ff // GROUPS
    cot = whole_rows(place, out_cotangent, recv, 0, out_cotangent.shape[1])
    d_out = cot.astype(F32) + dot(dwpair[...], write_pair[...], 1, 1)
    dout_out[...] = d_out
    d_branch = d_out.astype(BF16)
    for j in range(ff // 512):
        cols = slice(512 * j, 512 * j + 512)
        d_act = dot(d_branch, ffn_out[cols, :], 1, 1).astype(BF16)
        dinner[:, cols] = (d_act.astype(F32) * dg[:, cols].astype(F32)).astype(BF16)
        emit_rows(
            dot(act[:, cols], d_branch, 0, 0), deep, ks, 0, c, 512 // (2 * deep) * j,
        )


def inner_back_body(
    place, dinner, n2, ffn_in,
    send, keep, total,
):
    rows = ffn_in.shape[0] // GROUPS
    for j in range(ffn_in.shape[1] // 512):
        cols = slice(512 * j, 512 * j + 512)
        emit_rows(dot(n2[...], dinner[:, cols], 0, 0), rows, (send, keep), rows * j, place[1])
    total[...] = dot(dinner[...], ffn_in[...], 1, 1)


def resid_back_body(
    place, total, dout, resid, ffn_gain, out_weight, mixed,
    send, keep, dresid, dmixed, gain_out,
):
    rhat, rr = norm_parts(resid[...])
    d_norm, d_gain = norm_back(total[...], rhat, rr, ffn_gain[...])
    gain_out[...] = d_gain
    d = dout[...] + d_norm
    dresid[...] = d
    d_attn = d.astype(BF16)
    emit_rows(dot(mixed[...], d_attn), 32, (send, keep), 0, place[1])
    dmixed[...] = dot(d_attn, out_weight[...], 1, 1).astype(BF16)


def attn_back_body(
    place, qs, dm, vall, p3, kt, p2, p1, p0,
    dq_out, dk_out, dv_out, dk_ref, dv_ref, dqt_ref,
):
    probs = (p0, p1, p2, p3)

    def first(i, p):
        w, lanes = 128 * (i + 2), slice(128 * p, 128 * p + 128)
        dm01 = stacked_heads(dm[128 * i : 128 * i + 128, lanes])
        dv = dot(probs[i][p], dm01)
        if i == 3:
            dv_ref[0:w, lanes] = dv
        else:
            dv_ref[0:w, lanes] += dv
        return dot(vall[0:w, lanes], dm01, 1, 1)

    def second(i, p, dp):
        pf = probs[i][p].astype(F32)
        t = pf * dp
        return (t - pf * jnp.sum(t, 0, keepdims=True)).astype(BF16)

    def third(i, p, ds):
        w, lanes = 128 * (i + 2), slice(128 * p, 128 * p + 128)
        rows = slice(128 * i, 128 * i + 128)
        q01 = stacked_heads(qs[rows, lanes])
        dqt = (dot(kt[lanes, 0:w], ds) * 0.125).astype(BF16)
        dqt_ref[128 * p : 128 * p + 64, rows] = dqt[:64, :128]
        dqt_ref[128 * p + 64 : 128 * p + 128, rows] = dqt[64:, 128:]
        dk = dot(ds, q01)
        if i == 3:
            dk_ref[0:w, lanes] = dk
        else:
            dk_ref[0:w, lanes] += dk

    in_steps(
        [(i, p) for p in range(H // 2) for i in (3, 2, 1, 0)], (first, second, third)
    )
    dq_out[...] = dqt_ref[...].T
    dk_out[...] = dk_ref[...].astype(BF16)
    dv_out[...] = dv_ref[...].astype(BF16)


def input_back_body(
    place, nall, dq, dk, dv, pair_weight, query_weight, dwquery, write_query, x, mem, attn_gain,
    dresid, dblend, gain2, gain3, newmem,
    send, keep, own_tok, own_mem, swap, gtok, gmem,
):
    c, ks = place[1], (send, keep)
    rows, width = x.shape
    slots = mem.shape[0]
    half, mhalf = rows // 2, slots // 2
    na = nall[...]
    dqv = dq[...]
    emit_rows(dot(na[128:], dqv, 0, 0), 32, ks, 0, c)
    emit_rows(dot(na, dk[...], 0, 0), 32, ks, 32, c)
    emit_rows(dot(na, dv[...], 0, 0), 32, ks, 64, c)
    d_all = dot(dk[...], pair_weight[:, :width], 1, 1)
    d_all = d_all + dot(dv[...], pair_weight[:, width:], 1, 1)
    d_nx = d_all[128:] + dot(dqv, query_weight[...], 1, 1)
    d_nm = d_all[:slots] + dot(dwquery[...], write_query[...], 1, 1)
    gain = attn_gain[...]
    xhat, xr = norm_parts(x[...].astype(F32))
    d_x, g_x = norm_back(d_nx, xhat, xr, gain)
    mhat, mr = norm_parts(mem[...].astype(F32))
    d_m, g_m = norm_back(d_nm, mhat, mr, gain)
    gains = jnp.concatenate(
        [g_x + g_m, gain2[...], gain3[...], jnp.zeros((13, width), F32)], 0
    ).astype(BF16)
    for one in ks:
        one[:, 96:112, :] = jnp.broadcast_to(gains, (GROUPS // 2, 16, width))
    gtok[...] = dresid[...] + d_x
    gmem[...] = dblend[...] + d_m
    own_tok[...] = gtok[part(place, half, True), :]
    own_mem[...] = gmem[part(place, mhalf, True), :]
    other = part(place, half, False)
    mother = part(place, mhalf, False)
    swap[0:half, :] = gtok[other, :].astype(BF16)
    swap[half : half + mhalf, :] = newmem[mother, :]
    swap[half + mhalf :, :] = gmem[mother, :].astype(BF16)


BIT = {"y": 0, "x": 2, "z": 3, "h": 4}


def other_of(axis, bit):
    return [(i, i ^ bit) for i in range(lax.axis_size(axis))]


def exchanged(send, label):
    if label == "y":
        return lax.ppermute(send, "seq", other_of("seq", 1))
    return lax.ppermute(send, "seg", other_of("seg", {"x": 2, "z": 4, "h": 8, "c": 1}[label]))


class Stream:
    def __init__(self, keep, recv, dims, start, rows):
        self.keep, self.recv, self.dims, self.start, self.rows = keep, recv, dims, start, rows


def stage(streams, labels, joined=False, deps=(), tail=False):
    ins = []
    index = {}
    for s in streams:
        for arr in (s.keep, s.recv):
            if id(arr) not in index:
                index[id(arr)] = len(ins)
                ins.append(("v", arr))
    n_arrays = len(ins)
    ins += [("d", d) for d in deps]
    width = streams[0].keep.shape[-1]
    shapes, new_dims, new_rows = [], [], []
    for s, label in zip(streams, labels):
        rows = s.rows // 2 if label == "y" else s.rows
        dims = s.dims.replace(label, "")
        new_dims.append(dims)
        new_rows.append(rows)
        shapes.append((2,) * len(dims) + (rows, width))
    if joined:
        shapes = [(sum(new_rows), width)]
    if tail:
        shapes = shapes[:-2] + [shapes[-2][:-2] + (new_rows[-2] + new_rows[-1], width)]
    outs = []
    for shape in shapes:
        outs += [(shape, BF16)] * 2

    def body(place, *refs):
        given, made = refs[:n_arrays], refs[n_arrays:]

        def value(s, label, own, arr):
            bit = place[BIT[label]]
            bit = bit if own else 1 - bit
            where = []
            for d in s.dims:
                where.append(bit if d == label else slice(None))
            if label == "y":
                half = s.rows // 2
                where.append(pl.ds(pl.multiple_of(s.start + bit * half, 16), half))
            else:
                where.append(slice(s.start, s.start + s.rows))
            return given[index[id(arr)]][tuple(where) + (slice(None),)].astype(F32)

        for own in (False, True):
            at = 0
            for k, (s, label) in enumerate(zip(streams, labels)):
                total = (value(s, label, own, s.keep) + value(s, label, own, s.recv)).astype(BF16)
                last = tail and k == len(streams) - 1
                target = made[(0 if joined else 2 * (k - last)) + (0 if own else 1)]
                if joined:
                    target[at : at + new_rows[k], :] = total
                    at += new_rows[k]
                elif last:
                    target[..., new_rows[k - 1] :, :] = total
                elif tail and k == len(streams) - 2:
                    target[..., : new_rows[k], :] = total
                else:
                    target[...] = total

    results = call(body, ins, outs, flops=10**6, nbytes=10**6)
    if joined:
        return results[0], results[1]
    if tail:
        new_rows = new_rows[:-2] + [new_rows[-2] + new_rows[-1]]
    return [
        (results[2 * k], results[2 * k + 1], new_dims[k], n) for k, n in enumerate(new_rows)
    ]


def added(keep, recv, deps=()):
    def body(place, keep, recv, total):
        total[...] = (keep[...].astype(F32) + recv[...].astype(F32)).astype(BF16)

    (total,) = call(
        body,
        [("v", keep), ("v", recv)] + [("d", d) for d in deps],
        [(keep.shape, BF16)],
        flops=10**6, nbytes=10**6,
    )
    return total


def in_hbm(a):
    return pltpu.with_memory_space_constraint(a, pltpu.HBM)


def packed(body_rows, extra_rows):
    half, width = body_rows.shape[1:]
    extra = extra_rows.shape[1]

    def kernel(a, b, o, sem):
        other = 1 - lax.axis_index("seq")
        copies = [
            pltpu.make_async_copy(a.at[other], o.at[0:half], sem.at[0]),
            pltpu.make_async_copy(b.at[other], o.at[half:], sem.at[1]),
        ]
        for copy in copies:
            copy.start()
        for copy in copies:
            copy.wait()

    return pl.pallas_call(
        kernel,
        out_shape=pltpu.VMEM((half + extra, width), body_rows.dtype),
        in_specs=[pl.BlockSpec(memory_space=pltpu.HBM)] * 2,
        out_specs=pl.BlockSpec(memory_space=pltpu.VMEM),
        scratch_shapes=[pltpu.SemaphoreType.DMA((2,))],
        compiler_params=pltpu.CompilerParams(vmem_limit_bytes=4 * 1024 * 1024),
    )(in_hbm(body_rows), in_hbm(extra_rows))


def assembled(own, recv, dtypes, deps=()):
    width = own[0].shape[1]

    def body(place, *refs):
        n = len(own)
        start = 0
        for mine, out in zip(refs[:n], refs[n + 1 :]):
            rows = mine.shape[0]
            out[place[0]] = mine[...].astype(out.dtype)
            out[1 - place[0]] = refs[n][start : start + rows, :].astype(out.dtype)
            start += rows

    return call(
        body,
        [("v", a) for a in own] + [("v", recv)] + [("d", d) for d in deps],
        [((2,) + a.shape, d) for a, d in zip(own, dtypes)],
        flops=10**6, nbytes=10**6, home=False,
    )


def fetched_weights(weights):
    def kernel(*refs):
        n = len(weights)
        copies = [
            pltpu.make_async_copy(refs[k], refs[n + k], refs[-1].at[k]) for k in range(n)
        ]
        for copy in copies:
            copy.start()
        for copy in copies:
            copy.wait()

    return pl.pallas_call(
        kernel,
        out_shape=[pltpu.VMEM(a.shape, a.dtype) for a in weights],
        in_specs=[pl.BlockSpec(memory_space=pltpu.HBM)] * len(weights),
        out_specs=[pl.BlockSpec(memory_space=pltpu.VMEM)] * len(weights),
        scratch_shapes=[pltpu.SemaphoreType.DMA((len(weights),))],
        compiler_params=pltpu.CompilerParams(vmem_limit_bytes=4 * 1024 * 1024),
        cost_estimate=pl.CostEstimate(flops=10**9, bytes_accessed=10**7, transcendentals=0),
    )(*[in_hbm(a) for a in weights])


def reduced_any(keep, send, pieces):
    groups = lax.axis_size("seg")
    c = lax.axis_index("seg") % 2
    first = jnp.where(c == 0, keep, send)
    second = jnp.where(c == 0, send, keep)
    total = jnp.stack([first, second], 1)
    total = total.reshape((GROUPS,) + keep.shape[1:])
    fine = groups // GROUPS
    parts = []
    at = 0
    for rows, shared in pieces:
        piece = total[:, at : at + rows]
        if shared:
            piece = jnp.broadcast_to(piece[:, None], (GROUPS, fine) + piece.shape[1:])
        else:
            piece = piece.reshape(GROUPS, fine, rows // fine, piece.shape[2])
        parts.append(piece.reshape(groups, -1, piece.shape[-1]))
        at += rows
    total = jnp.concatenate(parts, 1)
    total = lax.psum_scatter(total.astype(F32), "seg", scatter_dimension=0, tiled=True)[0]
    return lax.psum(total, "seq")


def final_parts(one, two, ff):
    t1, o1, split = one
    t2, o2 = two
    width = t1.shape[-1]
    r = width // GROUPS
    n = ff // 512
    shapes = [
        (r, width), (r, 2 * width), (r, width), (r, ff), (ff // GROUPS, width),
        (r, width), (r, 2 * width), (r, width), (r, width), (r,), (r,), (r,),
    ]

    def body(place, t1, o1, t2, o2, gq, gp, go, gfi, gfo, gwq, gwp, gwo, gwg, g0, g1, g2, full):
        y = place[0]
        at = start = 0
        for rows in split:
            half = rows // 2
            for ref, index in ((t1, y), (o1, 1 - y)):
                full[pl.ds(pl.multiple_of(start + index * half, 16), half), :] = ref[
                    at : at + half, :
                ].astype(F32)
            at += half
            start += rows
        total = (t2[...].astype(F32) + o2[...].astype(F32))
        gq[...] = total[0:r, :]
        gp[:, :width] = total[r : 2 * r, :]
        gp[:, width:] = total[2 * r : 3 * r, :]
        seg = lax.axis_index("seg")
        gains = pltpu.roll(total[3 * r : 3 * r + 8, :], (width - seg * r) % width, 1)
        for k, ref in enumerate((g0, g1, g2)):
            ref[...] = gains[k, :r]
        gwq[...] = full[0:r, :]
        gwp[:, :width] = full[r : 2 * r, :]
        gwp[:, width:] = full[2 * r : 3 * r, :]
        gwo[...] = full[3 * r : 4 * r, :]
        gwg[...] = full[4 * r : 5 * r, :]
        for j in range(n):
            gfi[:, 512 * j : 512 * j + 512] = full[(5 + j) * r : (6 + j) * r, :]
        gfo[...] = full[(5 + n) * r : (5 + n) * r + ff // GROUPS, :]
        go[...] = full[(5 + n) * r + ff // GROUPS :, :]

    return call(
        body, [("v", a) for a in (t1, o1, t2, o2)], [(s, F32) for s in shapes],
        scratch=[((sum(split), width), F32)], flops=10**6, nbytes=10**6, home=False,
    )


def shards(
    tokens, memory, lengths, attn_gain, query_weight, pair_weight, out_weight, ffn_gain, ffn_in,
    ffn_out, write_query, write_pair, write_out, write_gate, write_gain, out_cotangent,
    memory_cotangent,
):
    half, width = tokens.shape[1:]
    mhalf = memory.shape[1]
    rows, slots, ff = 2 * half, 2 * mhalf, ffn_in.shape[1]
    padded = rows + 128
    groups = lax.axis_size("seg")
    recv_a = exchanged(packed(tokens, memory), "y")
    recv_b = exchanged(packed(out_cotangent, memory_cotangent), "y")
    (
        tokens, memory, out_cotangent, memory_cotangent, query_weight, pair_weight, out_weight,
        ffn_in, ffn_out, write_query, write_pair, write_out, write_gate,
    ) = fetched_weights(
        (
            tokens, memory, out_cotangent, memory_cotangent, query_weight, pair_weight, out_weight,
            ffn_in, ffn_out, write_query, write_pair, write_out, write_gate,
        )
    )
    ag, fg, wg = attn_gain[None], ffn_gain[None], write_gain[None]
    v = lambda *arrs: [("v", a) for a in arrs]
    h = lambda *arrs: [("h", a) for a in arrs]
    deps = lambda *arrs: [("d", a) for a in arrs]
    big = ((rows, width), BF16)
    wide = ((padded, width), BF16)
    deep = ((rows, ff), BF16)
    half_b = ((half, width), BF16)
    keep_send = lambda n: [((GROUPS // 2, n, width), BF16)] * 2
    small = ((slots, width), BF16)
    full_f = ((rows, width), F32)
    gain_row = ((1, width), F32)
    (
        x, mem, nall, qs, kall, vall, p0, p1, p2, p3, mixed, resid, n2, act, dg,
        out_send, out_own, out, wqs, kt,
    ) = call(
        forward_body,
        [("s", lengths)] + v(tokens, memory, recv_a, ag, query_weight, pair_weight)
        + v(write_query, out_weight, fg, ffn_in, ffn_out),
        [big, small, wide, big, wide, wide]
        + [((H // 2, 128 * (i + 2), 256), BF16) for i in range(4)]
        + [big, full_f, big, deep, deep, half_b, half_b, big, small, ((width, padded), BF16)],
        scratch=[((width, padded), BF16)],
        flops=2 * 6 * 10**9, nbytes=20 * 10**6, limit=16,
    )
    out_recv = exchanged(out_send, "y")
    send0, keep0, dwpair, dwquery, dblend, own_new, newmem, gain3 = call(
        write_body,
        v(out, wqs, mem, memory_cotangent, recv_b, write_pair, write_out, write_gate, wg, nall),
        [
            *keep_send(160), ((rows, 2 * width), BF16), small,
            ((slots, width), F32), ((mhalf, width), BF16), small, gain_row,
        ],
        flops=2 * 3 * 10**9, nbytes=10 * 10**6,
    )
    small_mesh = groups == GROUPS
    cube = lambda a: a.reshape((2, 2, 2) + a.shape[1:])
    pair = lambda keep, send: (cube(keep), cube(exchanged(send, "c")))
    deps0 = deps1 = []
    send1, keep1, dout, dinner = call(
        ffn_back_body,
        v(dwpair, write_pair, out_cotangent, recv_b, ffn_out, dg, act) + deps(out_recv),
        [*keep_send(128), full_f, deep],
        flops=2 * 5 * 10**9, nbytes=20 * 10**6,
    )
    if small_mesh:
        send0, _ = lax.optimization_barrier((send0, out_recv))
        k0, r0 = pair(keep0, send0)
        deps0 = deps(r0)
    send4, keep4, total = call(
        inner_back_body, v(dinner, n2, ffn_in) + deps0, [*keep_send(128), full_f],
        flops=10**9, nbytes=20 * 10**6,
    )
    if small_mesh:
        k1, r1 = pair(keep1, send1)
        deps0 = deps(r1)
    send3, keep3, dresid, dmixed, gain2 = call(
        resid_back_body, v(total, dout, resid, fg, out_weight, mixed) + deps0,
        [*keep_send(32), full_f, big, gain_row],
        flops=10**8, nbytes=10**6,
    )
    orders = ("xyz", "yzx", "zxy")
    late_orders = ("xz", "zx")

    def moved(parts, labels):
        return [
            Stream(keep, exchanged(send, label), dims, 0, r)
            for label, (keep, send, dims, r) in zip(labels, parts)
        ]

    nth = lambda these, step: [o[step] for o in these]
    if small_mesh:
        k4, r4 = pair(keep4, send4)
        k3, r3 = pair(keep3, send3)
        streams = [
            Stream(k0, r0, "hzx", 0, 160), Stream(k4, r4, "hzx", 0, 128),
            Stream(k1, r1, "hzx", 0, 128), Stream(k3, r3, "hzx", 0, 32),
        ]
        parts = stage_joined(streams, nth(orders, 0), [])
        deps1 = deps(parts[0][0])
        first = moved(parts, nth(orders, 0))
    dq, dk, dv = call(
        attn_back_body,
        v(qs, dmixed, vall, p3, kt, p2, p1, p0) + deps1,
        [big, wide, wide],
        scratch=[((padded, width), F32)] * 2 + [big],
        flops=2 * 6 * 10**9, nbytes=20 * 10**6,
    )
    send2, keep2, own_tok, own_mem, swap = call(
        input_back_body,
        v(
            nall, dq, dk, dv, pair_weight, query_weight, dwquery, write_query, x, mem, ag, dresid,
            dblend, gain2, gain3, newmem,
        ),
        [
            *keep_send(112), ((half, width), F32), ((mhalf, width), F32),
            ((half + 2 * mhalf, width), BF16),
        ],
        scratch=[((rows, width), F32), ((slots, width), F32)],
        flops=2 * 3 * 10**9, nbytes=20 * 10**6,
    )
    r = width // groups
    (out_both,) = assembled([out_own], out_recv, [BF16])
    if small_mesh:
        chain = [send2]

        def each(streams, labels):
            results = []
            for stream, label in zip(streams, labels):
                ((keep, send, dims, n),) = stage([stream], [label], deps=chain[-1:])
                results.append((keep, send, dims, n))
                chain.append(keep)
            return moved(results, labels)

        second = each(first, nth(orders, 1))
        send2, swap, _ = lax.optimization_barrier((send2, swap, chain[-1]))
        k2, r2 = pair(keep2, send2)
        late = [Stream(k2, r2, "hzx", 0, 64), Stream(k2, r2, "hzx", 64, 48)]
        late = each(late, nth(late_orders, 0))
        third = each(second, nth(orders, 2))
        late = late_second = each(late, nth(late_orders, 1))
        late = [chain[-1:]]
        keep, send = stage(third, "hhh", joined=True, deps=[late[0][0]])
        recv = exchanged(send, "h")
        late_keep, late_send = stage(late_second, "hh", joined=True, deps=[keep])
        late_recv = exchanged(late_send, "h")
        t1 = added(keep, recv, deps=[late_keep])
        o1 = exchanged(t1, "y")
        t2 = added(late_keep, late_recv, deps=[t1])
        o2 = exchanged(t2, "y")
        gq, gp, go, gfi, gfo, gwq, gwp, gwo, gwg, *gains = final_parts(
            (t1, o1, (160, 128, 160)), (t2, o2), ff
        )
    else:
        w = width // GROUPS
        w0 = reduced_any(keep0, send0, [(w, False)] * 5)
        gfo = reduced_any(keep1, send1, [(ff // GROUPS, False)])
        w1 = reduced_any(keep4, send4, [(w, False)] * (ff // 512))
        w2 = reduced_any(keep2, send2, [(w, False)] * 3 + [(16, True)])
        go = reduced_any(keep3, send3, [(w, False)])
        cut = lambda a, at, n: jnp.concatenate(
            [a[(at + i) * r : (at + i + 1) * r] for i in range(n)], 1
        )
        gq, gp = cut(w2, 0, 1), cut(w2, 1, 2)
        gfi = cut(w1, 0, ff // 512)
        gwq, gwp, gwo, gwg = cut(w0, 0, 1), cut(w0, 1, 2), cut(w0, 3, 1), cut(w0, 4, 1)
        at = lax.axis_index("seg") * r
        gains = [lax.dynamic_slice_in_dim(w2[3 * r + i], at, r, 0) for i in range(3)]
    swapped = exchanged(swap, "y")
    tok_both, new_both, mem_both = assembled([own_tok, own_new, own_mem], swapped, [F32, BF16, F32])
    return (
        out_both, new_both, tok_both, mem_both,
        gains[0], gq, gp, go, gains[1], gfi, gfo, gwq, gwp, gwo, gwg, gains[2],
    )


def stage_joined(streams, labels, deps):
    return stage(streams, list(labels) + [labels[-1]], tail=True, deps=deps)


def solution(mesh):
    row = P("seg", "seq", None)
    grad = P("seg", None)
    in_specs = (row, row, P("seg", None)) + (P(),) * 12 + (row, row)
    out_specs = (row, row, row, row, P("seg"), grad, grad, grad, P("seg")) + (grad,) * 6 + (P("seg"),)
    return jax.shard_map(shards, mesh=mesh, in_specs=in_specs, out_specs=out_specs, check_vma=False)
```

```python
import jax
import jax.numpy as jnp
from jax import lax
from jax.experimental import pallas as pl
from jax.experimental.pallas import tpu as pltpu
from jax.sharding import PartitionSpec as P

H = 8
GROUPS = 16
EPSILON = 1e-05
MASKED = -1e30
F32 = jnp.float32
BF16 = jnp.bfloat16
VMEM_LIMIT = 56 * 1024 * 1024


def part(place, half, own):
    index = place[0] if own else 1 - place[0]
    return pl.ds(pl.multiple_of(index * half, half), half)


class Fetched:
    def __init__(self, source, ref, sem):
        self.ref, self.copy, self.waited = ref, pltpu.make_async_copy(source, ref, sem), False

    def __call__(self):
        if not self.waited:
            self.copy.wait()
            self.waited = True
        return self.ref


def position():
    seg = lax.axis_index("seg")
    return [lax.axis_index("seq")] + [(seg >> k) & 1 for k in range(4)]


def call(body, ins, outs, scratch=(), flops=0, nbytes=0, limit=16, home=True):
    kinds = [kind for kind, _ in ins]
    arrays = [
        pltpu.with_memory_space_constraint(a, pltpu.VMEM) if kind == "v" else a for kind, a in ins
    ]
    spaces = {"s": pltpu.SMEM, "v": pltpu.VMEM, "d": pl.ANY, "h": pl.ANY}
    fetched = [pltpu.VMEM(a.shape, a.dtype) for kind, a in ins if kind == "h"]
    n_io = len(ins) + len(outs)

    def kernel(*refs):
        given, at = [], 0
        for kind, r in zip(kinds, refs):
            if kind == "h":
                r = Fetched(r, refs[n_io + at], refs[-1].at[at])
                r.copy.start()
                at += 1
            if kind != "d":
                given.append(r)
        end = -1 if fetched else len(refs)
        body(position(), *given, *refs[len(ins) : n_io], *refs[n_io + at : end])
        for r in given:
            if isinstance(r, Fetched):
                r()

    shape = (lambda s, d: pltpu.VMEM(s, d)) if home else jax.ShapeDtypeStruct
    sems = [pltpu.SemaphoreType.DMA((len(fetched),))] if fetched else []
    return pl.pallas_call(
        kernel,
        out_shape=[shape(s, d) for s, d in outs],
        in_specs=[pl.BlockSpec(memory_space=spaces[kind]) for kind in kinds],
        out_specs=[pl.BlockSpec(memory_space=pltpu.VMEM)] * len(outs),
        scratch_shapes=fetched + [pltpu.VMEM(s, d) for s, d in scratch] + sems,
        compiler_params=pltpu.CompilerParams(vmem_limit_bytes=limit * 1024 * 1024),
        cost_estimate=pl.CostEstimate(flops=flops, bytes_accessed=nbytes, transcendentals=0),
    )(*arrays)


def dot(a, b, ca=1, cb=0):
    return lax.dot_general(a, b, (((ca,), (cb,)), ((), ())), preferred_element_type=F32)


def norm_parts(v):
    centred = v - jnp.mean(v, -1, keepdims=True)
    r = lax.rsqrt(jnp.mean(centred * centred, -1, keepdims=True) + EPSILON)
    return centred * r, r


def norm_back(dy, xhat, r, gain):
    dx = dy * gain
    m1 = jnp.mean(dx, -1, keepdims=True)
    m2 = jnp.mean(dx * xhat, -1, keepdims=True)
    return r * (dx - m1 - xhat * m2), jnp.sum(dy * xhat, 0, keepdims=True)


def emit_rows(grad, rows, ks_ref, offset, c, first=0):
    pairs = grad.shape[0] // (2 * rows)
    g = grad.astype(BF16).reshape(pairs, 2, rows, grad.shape[1])
    where = (slice(first, first + pairs), slice(offset, offset + rows), slice(None))
    even, odd = g[:, 0], g[:, 1]
    send_ref, keep_ref = ks_ref
    keep_ref[where] = jnp.where(c == 0, even, odd)
    send_ref[where] = jnp.where(c == 0, odd, even)


def whole_rows(place, pair_ref, recv_ref, start, half):
    own, other = pair_ref[place[0]], recv_ref[start : start + half, :]
    first = place[0] == 0
    return jnp.concatenate([jnp.where(first, own, other), jnp.where(first, other, own)], 0)


def lane_low(shape):
    return lax.broadcasted_iota(jnp.int32, shape, 1) < 64


def stacked_heads(block):
    low = lane_low(block.shape)
    zero = jnp.zeros_like(block)
    return jnp.concatenate([jnp.where(low, block, zero), jnp.where(low, zero, block)], 0)


def unstacked_heads(block):
    rows = block.shape[0] // 2
    top, bottom = block[:rows], block[rows:]
    return jnp.where(lane_low(top.shape), top, bottom)


def head_mask(rows_per, width):
    shape = (H * rows_per, width)
    row_head = lax.broadcasted_iota(jnp.int32, shape, 0) // rows_per
    col_head = lax.broadcasted_iota(jnp.int32, shape, 1) // (width // H)
    return row_head == col_head


def block_diagonal(v, mask):
    return jnp.where(mask, jnp.concatenate([v] * H, 0), jnp.zeros((), v.dtype))


def diagonal_blocks(v, mask):
    rows = v.shape[0] // H
    v = jnp.where(mask, v, 0.0)
    return jnp.sum(v.reshape(H, rows, v.shape[1]), 0)


def in_steps(items, stages):
    held = {}
    for step in range(len(items) + len(stages) - 1):
        for k, stage_of in enumerate(stages):
            n = step - k
            if 0 <= n < len(items):
                given = () if k == 0 else (held.pop((n, k - 1)),)
                held[n, k] = stage_of(*items[n], *given)


def forward_body(
    place, lengths, tokens, memory, recv, attn_gain, query_weight, pair_weight, write_query, out_weight,
    ffn_gain, ffn_in, ffn_out,
    x, mem, nall, qs, kall, vall, p0, p1, p2, p3, mixed, resid, n2, act, dg,
    out_send, out_own, out, wqs, kt, vt,
):
    y = place[0]
    width = pair_weight.shape[0]
    rows = x.shape[0]
    slots = mem.shape[0]
    half = rows // 2
    x[...] = whole_rows(place, tokens, recv, 0, half)
    mem[...] = whole_rows(place, memory, recv, half, slots // 2)
    gain = attn_gain[...]
    xhat, _ = norm_parts(x[...].astype(F32))
    nx = (xhat * gain).astype(BF16)
    mhat, _ = norm_parts(mem[...].astype(F32))
    nm = (mhat * gain).astype(BF16)
    nall[0:slots, :] = nm
    nall[slots:128, :] = jnp.zeros((128 - slots, width), BF16)
    nall[128:, :] = nx
    qs[...] = (dot(nx, query_weight[...]) * 0.125).astype(BF16)
    na = nall[...]
    kall[...] = dot(na, pair_weight[:, :width]).astype(BF16)
    vall[...] = dot(na, pair_weight[:, width:]).astype(BF16)
    wqs[...] = (dot(nm, write_query[...]) * 0.125).astype(BF16)
    bounds = []
    total = 0
    for k in range(lengths.shape[1]):
        total = total + lengths[y, k]
        bounds.append(total)
    pos_k = lax.broadcasted_iota(jnp.int32, (rows, 1), 0)
    doc_k = sum([(pos_k >= b).astype(jnp.int32) for b in bounds])
    mem_bias = jnp.where(
        lax.broadcasted_iota(jnp.int32, (128, 128), 0) < slots, 0.0, MASKED
    ).astype(F32)
    kt[...] = kall[...].T
    vt[...] = vall[...].T
    biases = []
    for i in range(4):
        cols = 128 * (i + 1)
        pos_q = lax.broadcasted_iota(jnp.int32, (1, 128), 1) + 128 * i
        doc_q = sum([(pos_q >= b).astype(jnp.int32) for b in bounds])
        ok = (doc_k[:cols] == doc_q) & (pos_k[:cols] <= pos_q)
        bias = jnp.concatenate([mem_bias, jnp.where(ok, 0.0, MASKED).astype(F32)], 0)
        biases.append(jnp.concatenate([bias, bias], 1))

    def score(i, p):
        w, lanes = 128 * (i + 2), slice(128 * p, 128 * p + 128)
        q01 = stacked_heads(qs[128 * i : 128 * i + 128, lanes])
        return dot(kall[0:w, lanes], q01, 1, 1)

    def soften(i, p, s):
        s = s + biases[i]
        e = jnp.exp(s - jnp.max(s, 0, keepdims=True))
        pr = (e * (1.0 / jnp.sum(e, 0, keepdims=True))).astype(BF16)
        (p0, p1, p2, p3)[i][p] = pr
        return pr

    def mix(i, p, pr):
        w, lanes = 128 * (i + 2), slice(128 * p, 128 * p + 128)
        queries = slice(128 * i, 128 * i + 128)
        o = dot(vt[lanes, 0:w], pr).astype(BF16)
        mixed[128 * p : 128 * p + 64, queries] = o[:64, :128]
        mixed[128 * p + 64 : 128 * p + 128, queries] = o[64:, 128:]

    in_steps(
        [(i, p) for i in range(4) for p in range(H // 2)], (score, soften, mix)
    )
    ff = ffn_in.shape[1]
    k0 = 0.7978845608028654
    step = 512
    chunks = ff // step

    def top(block):
        at = slice(half * block, half * block + half)
        r = x[at, :].astype(F32) + dot(mixed[:, at], out_weight[...], 0, 0)
        resid[at, :] = r
        rhat, _ = norm_parts(r)
        n2[at, :] = (rhat * ffn_gain[...]).astype(BF16)

    def inner(block, j):
        if block == 0 and j == 1:
            top(1)
        return dot(n2[half * block : half * block + half, :], ffn_in[:, step * j : step * j + step])

    def gelu(block, j, v):
        at = (slice(half * block, half * block + half), slice(step * j, step * j + step))
        v2 = v * v
        h = 0.5 * jnp.tanh(v * (k0 + (0.044715 * k0) * v2)) + 0.5
        act[at] = (v * h).astype(BF16)
        w = v * (2.0 * k0 + (6.0 * 0.044715 * k0) * v2)
        dg[at] = (h + h * (1.0 - h) * w).astype(BF16)

    def bottom(block):
        at = slice(half * block, half * block + half)
        out[at, :] = (resid[at, :] + dot(act[at, :], ffn_out[...])).astype(BF16)

    top(0)
    held = None
    for n in range(2 * chunks + 1):
        now = None
        if n < 2 * chunks:
            now = inner(n // chunks, n % chunks)
        if held is not None:
            gelu(*held)
        if n == chunks + 1:
            bottom(0)
        held = (n // chunks, n % chunks, now)
    bottom(1)
    out_own[...] = out[part(place, half, True), :]
    out_send[...] = out[part(place, half, False), :]


def write_body(
    place, out, wqs, mem, memory_cotangent, recv, write_pair, write_out, write_gate, write_gain, nall,
    send, keep, dwpair, dwquery, dblend, own_new, newmem, gain_out,
):
    c, ks = place[1], (send, keep)
    slots, width = wqs.shape
    o = out[...]
    wk = dot(o, write_pair[:, :width]).astype(BF16)
    wv = dot(o, write_pair[:, width:]).astype(BF16)
    mask = head_mask(slots, width)
    qbd = block_diagonal(wqs[...], mask)
    s = dot(qbd, wk, 1, 1)
    e = jnp.exp(s - jnp.max(s, -1, keepdims=True))
    pf = e * (1.0 / jnp.sum(e, -1, keepdims=True))
    pb = pf.astype(BF16)
    wmixed = diagonal_blocks(dot(pb, wv), mask).astype(BF16)
    update = dot(wmixed, write_out[...])
    update_low = update.astype(BF16)
    gate = jax.nn.sigmoid(dot(update_low, write_gate[...]))
    blended = mem[...].astype(F32) + gate * update
    bhat, br = norm_parts(blended)
    gain = write_gain[...]
    newmem[...] = (bhat * gain).astype(BF16)
    mhalf = slots // 2
    own_new[...] = newmem[part(place, mhalf, True), :]
    mc = whole_rows(place, memory_cotangent, recv, recv.shape[0] - mhalf, mhalf).astype(F32)
    d_blend, d_gain = norm_back(mc, bhat, br, gain)
    gain_out[...] = d_gain
    dblend[...] = d_blend
    d_gate_pre = (d_blend * update * gate * (1.0 - gate)).astype(BF16)
    d_update = (d_blend * gate + dot(d_gate_pre, write_gate[...], 1, 1)).astype(BF16)
    d_wmixed = dot(d_update, write_out[...], 1, 1).astype(BF16)
    emit_rows(dot(update_low, d_gate_pre, 0, 0), 32, ks, 128, c)
    emit_rows(dot(wmixed, d_update, 0, 0), 32, ks, 96, c)
    dbd = block_diagonal(d_wmixed, mask)
    dp = dot(dbd, wv, 1, 1)
    row = jnp.sum(pf * dp, -1, keepdims=True)
    ds = (pf * (dp - row)).astype(BF16)
    d_wquery = (diagonal_blocks(dot(ds, wk), mask) * 0.125).astype(BF16)
    dwquery[...] = d_wquery
    dwk = dot(ds, qbd, 0, 0).astype(BF16)
    dwv = dot(pb, dbd, 0, 0).astype(BF16)
    dwpair[:, :width] = dwk
    dwpair[:, width:] = dwv
    emit_rows(dot(nall[0:slots, :], d_wquery, 0, 0), 32, ks, 0, c)
    emit_rows(dot(o, dwk, 0, 0), 32, ks, 32, c)
    emit_rows(dot(o, dwv, 0, 0), 32, ks, 64, c)


def ffn_back_body(
    place, dwpair, write_pair, out_cotangent, recv, ffn_out, dg, act,
    send, keep, dout_out, dinner,
):
    c, ks = place[1], (send, keep)
    ff, width = ffn_out.shape
    deep = ff // GROUPS
    cot = whole_rows(place, out_cotangent, recv, 0, out_cotangent.shape[1])
    d_out = cot.astype(F32) + dot(dwpair[...], write_pair[...], 1, 1)
    dout_out[...] = d_out
    d_branch = d_out.astype(BF16)
    for j in range(ff // 512):
        cols = slice(512 * j, 512 * j + 512)
        d_act = dot(d_branch, ffn_out[cols, :], 1, 1).astype(BF16)
        dinner[:, cols] = (d_act.astype(F32) * dg[:, cols].astype(F32)).astype(BF16)
        emit_rows(
            dot(act[:, cols], d_branch, 0, 0), deep, ks, 0, c, 512 // (2 * deep) * j,
        )


def inner_back_body(
    place, dinner, n2, ffn_in,
    send, keep, total,
):
    rows = ffn_in.shape[0] // GROUPS
    for j in range(ffn_in.shape[1] // 512):
        cols = slice(512 * j, 512 * j + 512)
        emit_rows(dot(n2[...], dinner[:, cols], 0, 0), rows, (send, keep), rows * j, place[1])
    total[...] = dot(dinner[...], ffn_in[...], 1, 1)


def resid_back_body(
    place, total, dout, resid, ffn_gain, out_weight, mixed,
    send, keep, dresid, dmixed, gain_out,
):
    rhat, rr = norm_parts(resid[...])
    d_norm, d_gain = norm_back(total[...], rhat, rr, ffn_gain[...])
    gain_out[...] = d_gain
    d = dout[...] + d_norm
    dresid[...] = d
    d_attn = d.astype(BF16)
    emit_rows(dot(mixed[...], d_attn), 32, (send, keep), 0, place[1])
    dmixed[...] = dot(d_attn, out_weight[...], 1, 1).astype(BF16)


def attn_back_body(
    place, qs, dm, vall, p3, kt, p2, p1, p0,
    dq_out, dk_out, dv_out, dk_ref, dv_ref, dqt_ref,
):
    probs = (p0, p1, p2, p3)

    def first(i, p):
        w, lanes = 128 * (i + 2), slice(128 * p, 128 * p + 128)
        dm01 = stacked_heads(dm[128 * i : 128 * i + 128, lanes])
        dv = dot(probs[i][p], dm01)
        if i == 3:
            dv_ref[0:w, lanes] = dv
        else:
            dv_ref[0:w, lanes] += dv
        return dot(vall[0:w, lanes], dm01, 1, 1)

    def second(i, p, dp):
        pf = probs[i][p].astype(F32)
        t = pf * dp
        return (t - pf * jnp.sum(t, 0, keepdims=True)).astype(BF16)

    def third(i, p, ds):
        w, lanes = 128 * (i + 2), slice(128 * p, 128 * p + 128)
        rows = slice(128 * i, 128 * i + 128)
        q01 = stacked_heads(qs[rows, lanes])
        dqt = (dot(kt[lanes, 0:w], ds) * 0.125).astype(BF16)
        dqt_ref[128 * p : 128 * p + 64, rows] = dqt[:64, :128]
        dqt_ref[128 * p + 64 : 128 * p + 128, rows] = dqt[64:, 128:]
        dk = dot(ds, q01)
        if i == 3:
            dk_ref[0:w, lanes] = dk
        else:
            dk_ref[0:w, lanes] += dk

    in_steps(
        [(i, p) for p in range(H // 2) for i in (3, 2, 1, 0)], (first, second, third)
    )
    dq_out[...] = dqt_ref[...].T
    dk_out[...] = dk_ref[...].astype(BF16)
    dv_out[...] = dv_ref[...].astype(BF16)


def input_back_body(
    place, nall, dq, dk, dv, pair_weight, query_weight, dwquery, write_query, x, mem, attn_gain,
    dresid, dblend, gain2, gain3, newmem,
    qsend, qkeep, ksend, kkeep, vsend, vkeep, gsend, gkeep, own_tok, own_mem, swap, gtok, gmem,
):
    c = place[1]
    rows, width = x.shape
    slots = mem.shape[0]
    half, mhalf = rows // 2, slots // 2
    na = nall[...]
    dqv = dq[...]
    emit_rows(dot(na[128:], dqv, 0, 0), 32, (qsend, qkeep), 0, c)
    emit_rows(dot(na, dk[...], 0, 0), 32, (ksend, kkeep), 0, c)
    emit_rows(dot(na, dv[...], 0, 0), 32, (vsend, vkeep), 0, c)
    d_all = dot(dk[...], pair_weight[:, :width], 1, 1)
    d_all = d_all + dot(dv[...], pair_weight[:, width:], 1, 1)
    d_nx = d_all[128:] + dot(dqv, query_weight[...], 1, 1)
    d_nm = d_all[:slots] + dot(dwquery[...], write_query[...], 1, 1)
    gain = attn_gain[...]
    xhat, xr = norm_parts(x[...].astype(F32))
    d_x, g_x = norm_back(d_nx, xhat, xr, gain)
    mhat, mr = norm_parts(mem[...].astype(F32))
    d_m, g_m = norm_back(d_nm, mhat, mr, gain)
    gains = jnp.concatenate(
        [g_x + g_m, gain2[...], gain3[...], jnp.zeros((13, width), F32)], 0
    ).astype(BF16)
    for one in (gsend, gkeep):
        one[...] = jnp.broadcast_to(gains, (GROUPS // 2, 16, width))
    gtok[...] = dresid[...] + d_x
    gmem[...] = dblend[...] + d_m
    own_tok[...] = gtok[part(place, half, True), :]
    own_mem[...] = gmem[part(place, mhalf, True), :]
    other = part(place, half, False)
    mother = part(place, mhalf, False)
    swap[0:half, :] = gtok[other, :].astype(BF16)
    swap[half : half + mhalf, :] = newmem[mother, :]
    swap[half + mhalf :, :] = gmem[mother, :].astype(BF16)


BIT = {"y": 0, "x": 2, "z": 3, "h": 4}


def other_of(axis, bit):
    return [(i, i ^ bit) for i in range(lax.axis_size(axis))]


def exchanged(send, label):
    if label == "y":
        return lax.ppermute(send, "seq", other_of("seq", 1))
    return lax.ppermute(send, "seg", other_of("seg", {"x": 2, "z": 4, "h": 8, "c": 1}[label]))


class Stream:
    def __init__(self, keep, recv, dims, start, rows):
        self.keep, self.recv, self.dims, self.start, self.rows = keep, recv, dims, start, rows


def stage(streams, labels, joined=False, deps=(), tail=False):
    ins = []
    index = {}
    for s in streams:
        for arr in (s.keep, s.recv):
            if id(arr) not in index:
                index[id(arr)] = len(ins)
                ins.append(("v", arr))
    n_arrays = len(ins)
    ins += [("d", d) for d in deps]
    width = streams[0].keep.shape[-1]
    shapes, new_dims, new_rows = [], [], []
    for s, label in zip(streams, labels):
        rows = s.rows // 2 if label == "y" else s.rows
        dims = s.dims.replace(label, "")
        new_dims.append(dims)
        new_rows.append(rows)
        shapes.append((2,) * len(dims) + (rows, width))
    if joined:
        shapes = [(sum(new_rows), width)]
    if tail:
        shapes = shapes[:-2] + [shapes[-2][:-2] + (new_rows[-2] + new_rows[-1], width)]
    outs = []
    for shape in shapes:
        outs += [(shape, BF16)] * 2

    def body(place, *refs):
        given, made = refs[:n_arrays], refs[n_arrays:]

        def value(s, label, own, arr):
            bit = place[BIT[label]]
            bit = bit if own else 1 - bit
            where = []
            for d in s.dims:
                where.append(bit if d == label else slice(None))
            if label == "y":
                half = s.rows // 2
                where.append(pl.ds(pl.multiple_of(s.start + bit * half, 16), half))
            else:
                where.append(slice(s.start, s.start + s.rows))
            return given[index[id(arr)]][tuple(where) + (slice(None),)].astype(F32)

        for own in (False, True):
            at = 0
            for k, (s, label) in enumerate(zip(streams, labels)):
                total = (value(s, label, own, s.keep) + value(s, label, own, s.recv)).astype(BF16)
                last = tail and k == len(streams) - 1
                target = made[(0 if joined else 2 * (k - last)) + (0 if own else 1)]
                if joined:
                    target[at : at + new_rows[k], :] = total
                    at += new_rows[k]
                elif last:
                    target[..., new_rows[k - 1] :, :] = total
                elif tail and k == len(streams) - 2:
                    target[..., : new_rows[k], :] = total
                else:
                    target[...] = total

    results = call(body, ins, outs, flops=10**6, nbytes=10**6)
    if joined:
        return results[0], results[1]
    if tail:
        new_rows = new_rows[:-2] + [new_rows[-2] + new_rows[-1]]
    return [
        (results[2 * k], results[2 * k + 1], new_dims[k], n) for k, n in enumerate(new_rows)
    ]


def added(keep, recv, deps=()):
    def body(place, keep, recv, total):
        total[...] = (keep[...].astype(F32) + recv[...].astype(F32)).astype(BF16)

    (total,) = call(
        body,
        [("v", keep), ("v", recv)] + [("d", d) for d in deps],
        [(keep.shape, BF16)],
        flops=10**6, nbytes=10**6,
    )
    return total


class Late:
    def __init__(self, pairs, order):
        flat = lambda a: a.reshape(-1, a.shape[2])
        self.arrays = [(flat(keep), flat(recv), [keep.shape[1]]) for keep, recv in pairs]
        self.order, self.dims = order, "hzx"

    def joined(self, other):
        self.arrays = self.arrays + other.arrays
        return self

    def next(self, deps=()):
        label = self.order[3 - len(self.dims)]
        at = self.dims.index(label)
        count = 1 << at
        plan, target = [], 0
        for array, (_, _, pieces) in enumerate(self.arrays):
            source = 0
            for rows in pieces:
                size = rows << (len(self.dims) - 1 - at)
                for b in range(count):
                    plan.append((array, source + 2 * b * size, target + b * size, size))
                source += 2 * count * size
                target += count * size

        def body(place, *refs):
            bit = place[BIT[label]]
            for out, b in ((refs[-1], 1 - bit), (refs[-2], bit)):
                for array, start, to, size in plan:
                    rows = pl.ds(pl.multiple_of(start + b * size, 16), size)
                    out[to : to + size, :] = (
                        refs[2 * array][rows, :].astype(F32)
                        + refs[2 * array + 1][rows, :].astype(F32)
                    ).astype(BF16)

        ins = [("v", a) for keep, recv, _ in self.arrays for a in (keep, recv)]
        ins += [("d", d) for d in deps]
        width = self.arrays[0][0].shape[1]
        keep, send = call(body, ins, [((target, width), BF16)] * 2, flops=10**6, nbytes=10**6)
        pieces = sum([p for _, _, p in self.arrays], [])
        self.arrays = [(keep, exchanged(send, label), pieces)]
        self.dims = self.dims.replace(label, "")


def in_hbm(a):
    return pltpu.with_memory_space_constraint(a, pltpu.HBM)


def packed(body_rows, extra_rows):
    half, width = body_rows.shape[1:]
    extra = extra_rows.shape[1]

    def kernel(a, b, o, sem):
        other = 1 - lax.axis_index("seq")
        copies = [
            pltpu.make_async_copy(a.at[other], o.at[0:half], sem.at[0]),
            pltpu.make_async_copy(b.at[other], o.at[half:], sem.at[1]),
        ]
        for copy in copies:
            copy.start()
        for copy in copies:
            copy.wait()

    return pl.pallas_call(
        kernel,
        out_shape=pltpu.VMEM((half + extra, width), body_rows.dtype),
        in_specs=[pl.BlockSpec(memory_space=pltpu.HBM)] * 2,
        out_specs=pl.BlockSpec(memory_space=pltpu.VMEM),
        scratch_shapes=[pltpu.SemaphoreType.DMA((2,))],
        compiler_params=pltpu.CompilerParams(vmem_limit_bytes=4 * 1024 * 1024),
    )(in_hbm(body_rows), in_hbm(extra_rows))


def assembled(own, recv, dtypes, deps=()):
    width = own[0].shape[1]

    def body(place, *refs):
        n = len(own)
        start = 0
        for mine, out in zip(refs[:n], refs[n + 1 :]):
            rows = mine.shape[0]
            out[place[0]] = mine[...].astype(out.dtype)
            out[1 - place[0]] = refs[n][start : start + rows, :].astype(out.dtype)
            start += rows

    return call(
        body,
        [("v", a) for a in own] + [("v", recv)] + [("d", d) for d in deps],
        [((2,) + a.shape, d) for a, d in zip(own, dtypes)],
        flops=10**6, nbytes=10**6, home=False,
    )


def fetched_weights(weights):
    def kernel(*refs):
        n = len(weights)
        copies = [
            pltpu.make_async_copy(refs[k], refs[n + k], refs[-1].at[k]) for k in range(n)
        ]
        for copy in copies:
            copy.start()
        for copy in copies:
            copy.wait()

    return pl.pallas_call(
        kernel,
        out_shape=[pltpu.VMEM(a.shape, a.dtype) for a in weights],
        in_specs=[pl.BlockSpec(memory_space=pltpu.HBM)] * len(weights),
        out_specs=[pl.BlockSpec(memory_space=pltpu.VMEM)] * len(weights),
        scratch_shapes=[pltpu.SemaphoreType.DMA((len(weights),))],
        compiler_params=pltpu.CompilerParams(vmem_limit_bytes=4 * 1024 * 1024),
        cost_estimate=pl.CostEstimate(flops=10**9, bytes_accessed=10**7, transcendentals=0),
    )(*[in_hbm(a) for a in weights])


def reduced_any(keep, send, pieces):
    groups = lax.axis_size("seg")
    c = lax.axis_index("seg") % 2
    first = jnp.where(c == 0, keep, send)
    second = jnp.where(c == 0, send, keep)
    total = jnp.stack([first, second], 1)
    total = total.reshape((GROUPS,) + keep.shape[1:])
    fine = groups // GROUPS
    parts = []
    at = 0
    for rows, shared in pieces:
        piece = total[:, at : at + rows]
        if shared:
            piece = jnp.broadcast_to(piece[:, None], (GROUPS, fine) + piece.shape[1:])
        else:
            piece = piece.reshape(GROUPS, fine, rows // fine, piece.shape[2])
        parts.append(piece.reshape(groups, -1, piece.shape[-1]))
        at += rows
    total = jnp.concatenate(parts, 1)
    total = lax.psum_scatter(total.astype(F32), "seg", scatter_dimension=0, tiled=True)[0]
    return lax.psum(total, "seq")


def final_parts(one, two, ff):
    ours, theirs, split = one
    t2, o2 = two
    width = t2.shape[-1]
    r = width // GROUPS
    n = ff // 512
    count = len(ours)
    shapes = [
        (r, width), (r, 2 * width), (r, width), (r, ff), (ff // GROUPS, width),
        (r, width), (r, 2 * width), (r, width), (r, width), (r,), (r,), (r,),
    ]

    def body(place, *refs):
        t2, o2, gq, gp, go, gfi, gfo, gwq, gwp, gwo, gwg, g0, g1, g2, full = refs[2 * count :]
        y = place[0]
        at = start = 0
        for rows in split:
            half = rows // 2
            for ref, index in ((refs[0], y), (refs[1], 1 - y)):
                full[pl.ds(pl.multiple_of(start + index * half, 16), half), :] = ref[
                    at : at + half, :
                ].astype(F32)
            at += half
            start += rows
        total = (t2[...].astype(F32) + o2[...].astype(F32))
        gq[...] = total[0:r, :]
        gp[:, :width] = total[r : 2 * r, :]
        gp[:, width:] = total[2 * r : 3 * r, :]
        seg = lax.axis_index("seg")
        gains = pltpu.roll(total[3 * r : 3 * r + 8, :], (width - seg * r) % width, 1)
        for k, ref in enumerate((g0, g1, g2)):
            ref[...] = gains[k, :r]
        gwq[...] = full[0:r, :]
        gwp[:, :width] = full[r : 2 * r, :]
        gwp[:, width:] = full[2 * r : 3 * r, :]
        gwo[...] = full[3 * r : 4 * r, :]
        gwg[...] = full[4 * r : 5 * r, :]
        for j in range(n):
            gfi[:, 512 * j : 512 * j + 512] = full[(5 + j) * r : (6 + j) * r, :]
        gfo[...] = full[(5 + n) * r : (5 + n) * r + ff // GROUPS, :]
        go[...] = full[(5 + n) * r + ff // GROUPS :, :]

    return call(
        body, [("v", a) for a in (*ours, *theirs, t2, o2)], [(s, F32) for s in shapes],
        scratch=[((sum(split), width), F32)], flops=10**6, nbytes=10**6, home=False,
    )


def shards(
    tokens, memory, lengths, attn_gain, query_weight, pair_weight, out_weight, ffn_gain, ffn_in,
    ffn_out, write_query, write_pair, write_out, write_gate, write_gain, out_cotangent,
    memory_cotangent,
):
    half, width = tokens.shape[1:]
    mhalf = memory.shape[1]
    rows, slots, ff = 2 * half, 2 * mhalf, ffn_in.shape[1]
    padded = rows + 128
    groups = lax.axis_size("seg")
    recv_a = exchanged(packed(tokens, memory), "y")
    recv_b = exchanged(packed(out_cotangent, memory_cotangent), "y")
    (
        tokens, memory, out_cotangent, memory_cotangent, query_weight, pair_weight, out_weight,
        ffn_in, ffn_out, write_query, write_pair, write_out, write_gate,
    ) = fetched_weights(
        (
            tokens, memory, out_cotangent, memory_cotangent, query_weight, pair_weight, out_weight,
            ffn_in, ffn_out, write_query, write_pair, write_out, write_gate,
        )
    )
    ag, fg, wg = attn_gain[None], ffn_gain[None], write_gain[None]
    v = lambda *arrs: [("v", a) for a in arrs]
    h = lambda *arrs: [("h", a) for a in arrs]
    deps = lambda *arrs: [("d", a) for a in arrs]
    big = ((rows, width), BF16)
    wide = ((padded, width), BF16)
    deep = ((rows, ff), BF16)
    half_b = ((half, width), BF16)
    keep_send = lambda n: [((GROUPS // 2, n, width), BF16)] * 2
    small = ((slots, width), BF16)
    full_f = ((rows, width), F32)
    gain_row = ((1, width), F32)
    (
        x, mem, nall, qs, kall, vall, p0, p1, p2, p3, mixed, resid, n2, act, dg,
        out_send, out_own, out, wqs, kt,
    ) = call(
        forward_body,
        [("s", lengths)] + v(tokens, memory, recv_a, ag, query_weight, pair_weight)
        + v(write_query, out_weight, fg, ffn_in, ffn_out),
        [big, small, wide, big, wide, wide]
        + [((H // 2, 128 * (i + 2), 256), BF16) for i in range(4)]
        + [big, full_f, big, deep, deep, half_b, half_b, big, small, ((width, padded), BF16)],
        scratch=[((width, padded), BF16)],
        flops=2 * 6 * 10**9, nbytes=20 * 10**6, limit=16,
    )
    out_recv = exchanged(out_send, "y")
    send0, keep0, dwpair, dwquery, dblend, own_new, newmem, gain3 = call(
        write_body,
        v(out, wqs, mem, memory_cotangent, recv_b, write_pair, write_out, write_gate, wg, nall),
        [
            *keep_send(160), ((rows, 2 * width), BF16), small,
            ((slots, width), F32), ((mhalf, width), BF16), small, gain_row,
        ],
        flops=2 * 3 * 10**9, nbytes=10 * 10**6,
    )
    small_mesh = groups == GROUPS
    cube = lambda a: a.reshape((2, 2, 2) + a.shape[1:])
    pair = lambda keep, send: (cube(keep), cube(exchanged(send, "c")))
    deps0 = deps1 = []
    send1, keep1, dout, dinner = call(
        ffn_back_body,
        v(dwpair, write_pair, out_cotangent, recv_b, ffn_out, dg, act) + deps(out_recv),
        [*keep_send(128), full_f, deep],
        flops=2 * 5 * 10**9, nbytes=20 * 10**6,
    )
    if small_mesh:
        send0, _ = lax.optimization_barrier((send0, out_recv))
        k0, r0 = pair(keep0, send0)
        deps0 = deps(r0)
    send4, keep4, total = call(
        inner_back_body, v(dinner, n2, ffn_in) + deps0, [*keep_send(128), full_f],
        flops=10**9, nbytes=20 * 10**6,
    )
    if small_mesh:
        k1, r1 = pair(keep1, send1)
        deps0 = deps(r1)
    send3, keep3, dresid, dmixed, gain2 = call(
        resid_back_body, v(total, dout, resid, fg, out_weight, mixed) + deps0,
        [*keep_send(32), full_f, big, gain_row],
        flops=10**8, nbytes=10**6,
    )
    orders = ("xyz", "yzx", "zxy")
    late_orders = ("xz", "zx")

    def moved(parts, labels):
        return [
            Stream(keep, exchanged(send, label), dims, 0, r)
            for label, (keep, send, dims, r) in zip(labels, parts)
        ]

    nth = lambda these, step: [o[step] for o in these]
    if small_mesh:
        k4, r4 = pair(keep4, send4)
        k3, r3 = pair(keep3, send3)
        streams = [
            Stream(k0, r0, "hzx", 0, 160), Stream(k4, r4, "hzx", 0, 128),
            Stream(k1, r1, "hzx", 0, 128), Stream(k3, r3, "hzx", 0, 32),
        ]
        parts = stage_joined(streams, nth(orders, 0), [])
        deps1 = deps(parts[0][0])
        first = moved(parts, nth(orders, 0))
    dq, dk, dv = call(
        attn_back_body,
        v(qs, dmixed, vall, p3, kt, p2, p1, p0) + deps1,
        [big, wide, wide],
        scratch=[((padded, width), F32)] * 2 + [big],
        flops=2 * 6 * 10**9, nbytes=20 * 10**6,
    )
    *grads2, own_tok, own_mem, swap = call(
        input_back_body,
        v(
            nall, dq, dk, dv, pair_weight, query_weight, dwquery, write_query, x, mem, ag, dresid,
            dblend, gain2, gain3, newmem,
        ),
        [
            *keep_send(32), *keep_send(32), *keep_send(32), *keep_send(16), ((half, width), F32), ((mhalf, width), F32),
            ((half + 2 * mhalf, width), BF16),
        ],
        scratch=[((rows, width), F32), ((slots, width), F32)],
        flops=2 * 3 * 10**9, nbytes=20 * 10**6,
    )
    r = width // groups
    (out_both,) = assembled([out_own], out_recv, [BF16])
    if small_mesh:
        def each(streams, labels, deps=()):
            results = []
            for stream, label in zip(streams, labels):
                results += stage([stream], [label], deps=list(deps))
            return moved(results, labels)

        second = each(first, nth(orders, 1), [swap])
        pieces = [(grads2[k + 1], exchanged(grads2[k], "c")) for k in range(0, 8, 2)]
        by_x, by_z = Late(pieces[:2], "xzh"), Late(pieces[2:], "zxh")
        by_x.next()
        by_z.next()
        third = each(second, nth(orders, 2))
        behind = [stream.keep for stream in third]
        by_x.next(behind)
        by_z.next(behind)
        keep, send = stage(third, "hhh", joined=True)
        by_x.joined(by_z).next([keep])
        t1 = added(keep, exchanged(send, "h"))
        one, two = [t1], [exchanged(t1, "y")]
        t2 = added(*by_x.arrays[0][:2])
        o2 = exchanged(t2, "y")
        gq, gp, go, gfi, gfo, gwq, gwp, gwo, gwg, *gains = final_parts(
            (one, two, (160, 128, 160)), (t2, o2), ff
        )
    else:
        w = width // GROUPS
        w0 = reduced_any(keep0, send0, [(w, False)] * 5)
        gfo = reduced_any(keep1, send1, [(ff // GROUPS, False)])
        w1 = reduced_any(keep4, send4, [(w, False)] * (ff // 512))
        w2 = jnp.concatenate(
            [
                reduced_any(grads2[k + 1], grads2[k], [(w, False)] if k < 6 else [(16, True)])
                for k in range(0, 8, 2)
            ],
            0,
        )
        go = reduced_any(keep3, send3, [(w, False)])
        cut = lambda a, at, n: jnp.concatenate(
            [a[(at + i) * r : (at + i + 1) * r] for i in range(n)], 1
        )
        gq, gp = cut(w2, 0, 1), cut(w2, 1, 2)
        gfi = cut(w1, 0, ff // 512)
        gwq, gwp, gwo, gwg = cut(w0, 0, 1), cut(w0, 1, 2), cut(w0, 3, 1), cut(w0, 4, 1)
        at = lax.axis_index("seg") * r
        gains = [lax.dynamic_slice_in_dim(w2[3 * r + i], at, r, 0) for i in range(3)]
    swapped = exchanged(swap, "y")
    tok_both, new_both, mem_both = assembled([own_tok, own_new, own_mem], swapped, [F32, BF16, F32])
    return (
        out_both, new_both, tok_both, mem_both,
        gains[0], gq, gp, go, gains[1], gfi, gfo, gwq, gwp, gwo, gwg, gains[2],
    )


def stage_joined(streams, labels, deps):
    return stage(streams, list(labels) + [labels[-1]], tail=True, deps=deps)


def solution(mesh):
    row = P("seg", "seq", None)
    grad = P("seg", None)
    in_specs = (row, row, P("seg", None)) + (P(),) * 12 + (row, row)
    out_specs = (row, row, row, row, P("seg"), grad, grad, grad, P("seg")) + (grad,) * 6 + (P("seg"),)
    return jax.shard_map(shards, mesh=mesh, in_specs=in_specs, out_specs=out_specs, check_vma=False)
```

```python
import jax
import jax.numpy as jnp
from jax import lax
from jax.experimental import pallas as pl
from jax.experimental.pallas import tpu as pltpu
from jax.sharding import PartitionSpec as P

H = 8
GROUPS = 16
EPSILON = 1e-05
MASKED = -1e30
F32 = jnp.float32
BF16 = jnp.bfloat16
VMEM_LIMIT = 56 * 1024 * 1024


def part(place, half, own):
    index = place[0] if own else 1 - place[0]
    return pl.ds(pl.multiple_of(index * half, half), half)


class Fetched:
    def __init__(self, source, ref, sem):
        self.ref, self.copy, self.waited = ref, pltpu.make_async_copy(source, ref, sem), False

    def __call__(self):
        if not self.waited:
            self.copy.wait()
            self.waited = True
        return self.ref


def position():
    seg = lax.axis_index("seg")
    return [lax.axis_index("seq")] + [(seg >> k) & 1 for k in range(4)]


def call(body, ins, outs, scratch=(), flops=0, nbytes=0, limit=16, home=True):
    kinds = [kind for kind, _ in ins]
    arrays = [
        pltpu.with_memory_space_constraint(a, pltpu.VMEM) if kind == "v" else a for kind, a in ins
    ]
    spaces = {"s": pltpu.SMEM, "v": pltpu.VMEM, "d": pl.ANY, "h": pl.ANY}
    fetched = [pltpu.VMEM(a.shape, a.dtype) for kind, a in ins if kind == "h"]
    n_io = len(ins) + len(outs)

    def kernel(*refs):
        given, at = [], 0
        for kind, r in zip(kinds, refs):
            if kind == "h":
                r = Fetched(r, refs[n_io + at], refs[-1].at[at])
                r.copy.start()
                at += 1
            if kind != "d":
                given.append(r)
        end = -1 if fetched else len(refs)
        body(position(), *given, *refs[len(ins) : n_io], *refs[n_io + at : end])
        for r in given:
            if isinstance(r, Fetched):
                r()

    shape = (lambda s, d: pltpu.VMEM(s, d)) if home else jax.ShapeDtypeStruct
    sems = [pltpu.SemaphoreType.DMA((len(fetched),))] if fetched else []
    return pl.pallas_call(
        kernel,
        out_shape=[shape(s, d) for s, d in outs],
        in_specs=[pl.BlockSpec(memory_space=spaces[kind]) for kind in kinds],
        out_specs=[pl.BlockSpec(memory_space=pltpu.VMEM)] * len(outs),
        scratch_shapes=fetched + [pltpu.VMEM(s, d) for s, d in scratch] + sems,
        compiler_params=pltpu.CompilerParams(vmem_limit_bytes=limit * 1024 * 1024),
        cost_estimate=pl.CostEstimate(flops=flops, bytes_accessed=nbytes, transcendentals=0),
    )(*arrays)


def dot(a, b, ca=1, cb=0):
    return lax.dot_general(a, b, (((ca,), (cb,)), ((), ())), preferred_element_type=F32)


def norm_parts(v):
    centred = v - jnp.mean(v, -1, keepdims=True)
    r = lax.rsqrt(jnp.mean(centred * centred, -1, keepdims=True) + EPSILON)
    return centred * r, r


def norm_back(dy, xhat, r, gain):
    dx = dy * gain
    m1 = jnp.mean(dx, -1, keepdims=True)
    m2 = jnp.mean(dx * xhat, -1, keepdims=True)
    return r * (dx - m1 - xhat * m2), jnp.sum(dy * xhat, 0, keepdims=True)


def emit_rows(grad, rows, ks_ref, offset, c, first=0):
    pairs = grad.shape[0] // (2 * rows)
    g = grad.astype(BF16).reshape(pairs, 2, rows, grad.shape[1])
    where = (slice(first, first + pairs), slice(offset, offset + rows), slice(None))
    even, odd = g[:, 0], g[:, 1]
    send_ref, keep_ref = ks_ref
    keep_ref[where] = jnp.where(c == 0, even, odd)
    send_ref[where] = jnp.where(c == 0, odd, even)


def whole_rows(place, pair_ref, recv_ref, start, half):
    own, other = pair_ref[place[0]], recv_ref[start : start + half, :]
    first = place[0] == 0
    return jnp.concatenate([jnp.where(first, own, other), jnp.where(first, other, own)], 0)


def lane_low(shape):
    return lax.broadcasted_iota(jnp.int32, shape, 1) < 64


def stacked_heads(block):
    low = lane_low(block.shape)
    zero = jnp.zeros_like(block)
    return jnp.concatenate([jnp.where(low, block, zero), jnp.where(low, zero, block)], 0)


def unstacked_heads(block):
    rows = block.shape[0] // 2
    top, bottom = block[:rows], block[rows:]
    return jnp.where(lane_low(top.shape), top, bottom)


def head_mask(rows_per, width):
    shape = (H * rows_per, width)
    row_head = lax.broadcasted_iota(jnp.int32, shape, 0) // rows_per
    col_head = lax.broadcasted_iota(jnp.int32, shape, 1) // (width // H)
    return row_head == col_head


def block_diagonal(v, mask):
    return jnp.where(mask, jnp.concatenate([v] * H, 0), jnp.zeros((), v.dtype))


def diagonal_blocks(v, mask):
    rows = v.shape[0] // H
    v = jnp.where(mask, v, 0.0)
    return jnp.sum(v.reshape(H, rows, v.shape[1]), 0)


def in_steps(items, stages):
    held = {}
    for step in range(len(items) + len(stages) - 1):
        for k, stage_of in enumerate(stages):
            n = step - k
            if 0 <= n < len(items):
                given = () if k == 0 else (held.pop((n, k - 1)),)
                held[n, k] = stage_of(*items[n], *given)


def forward_body(
    place, lengths, x_own, n_own, q_own, k_own, v_own, memory, recv, attn_gain, query_weight, pair_weight, write_query, out_weight,
    ffn_gain, ffn_in, ffn_out,
    x, mem, nall, qs, kall, vall, p0, p1, p2, p3, mixed, resid, n2, act, dg,
    out_own, out, wqs, vt,
):
    y = place[0]
    width = pair_weight.shape[0]
    rows = x.shape[0]
    slots = mem.shape[0]
    half = rows // 2
    own, other = part(place, half, True), part(place, half, False)
    x[own, :] = x_own[...]
    x_other = recv[0:half, :]
    x[other, :] = x_other
    mem[...] = whole_rows(place, memory, recv, half, slots // 2)
    gain = attn_gain[...]
    xhat, _ = norm_parts(x_other.astype(F32))
    nx = (xhat * gain).astype(BF16)
    mhat, _ = norm_parts(mem[...].astype(F32))
    nm = (mhat * gain).astype(BF16)
    some = jnp.concatenate([nm, jnp.zeros((128 - slots, width), BF16), nx], 0)
    own_at = pl.ds(pl.multiple_of(128 + place[0] * half, 128), half)
    other_at = pl.ds(pl.multiple_of(128 + (1 - place[0]) * half, 128), half)
    qs[own, :] = q_own[...]
    qs[other, :] = (dot(nx, query_weight[...]) * 0.125).astype(BF16)
    for ref, mine, value in (
        (nall, n_own, some),
        (kall, k_own, dot(some, pair_weight[:, :width]).astype(BF16)),
        (vall, v_own, dot(some, pair_weight[:, width:]).astype(BF16)),
    ):
        ref[0:128, :] = value[:128]
        ref[own_at, :] = mine[...]
        ref[other_at, :] = value[128:]
    wqs[...] = (dot(nm, write_query[...]) * 0.125).astype(BF16)
    bounds = []
    total = 0
    for k in range(lengths.shape[1]):
        total = total + lengths[y, k]
        bounds.append(total)
    pos_k = lax.broadcasted_iota(jnp.int32, (rows, 1), 0)
    doc_k = sum([(pos_k >= b).astype(jnp.int32) for b in bounds])
    mem_bias = jnp.where(
        lax.broadcasted_iota(jnp.int32, (128, 128), 0) < slots, 0.0, MASKED
    ).astype(F32)
    vt[...] = vall[...].T
    biases = []
    for i in range(4):
        cols = 128 * (i + 1)
        pos_q = lax.broadcasted_iota(jnp.int32, (1, 128), 1) + 128 * i
        doc_q = sum([(pos_q >= b).astype(jnp.int32) for b in bounds])
        ok = (doc_k[:cols] == doc_q) & (pos_k[:cols] <= pos_q)
        bias = jnp.concatenate([mem_bias, jnp.where(ok, 0.0, MASKED).astype(F32)], 0)
        biases.append(jnp.concatenate([bias, bias], 1))

    def score(i, p):
        w, lanes = 128 * (i + 2), slice(128 * p, 128 * p + 128)
        q01 = stacked_heads(qs[128 * i : 128 * i + 128, lanes])
        return dot(kall[0:w, lanes], q01, 1, 1)

    def soften(i, p, s):
        s = s + biases[i]
        e = jnp.exp(s - jnp.max(s, 0, keepdims=True))
        pr = (e * (1.0 / jnp.sum(e, 0, keepdims=True))).astype(BF16)
        (p0, p1, p2, p3)[i][p] = pr
        return pr

    def mix(i, p, pr):
        w, lanes = 128 * (i + 2), slice(128 * p, 128 * p + 128)
        queries = slice(128 * i, 128 * i + 128)
        o = dot(vt[lanes, 0:w], pr).astype(BF16)
        mixed[128 * p : 128 * p + 64, queries] = o[:64, :128]
        mixed[128 * p + 64 : 128 * p + 128, queries] = o[64:, 128:]

    in_steps(
        [(i, p) for i in range(4) for p in range(H // 2)], (score, soften, mix)
    )
    ff = ffn_in.shape[1]
    k0 = 0.7978845608028654
    step = 512
    chunks = ff // step

    def top(block):
        at = slice(half * block, half * block + half)
        r = x[at, :].astype(F32) + dot(mixed[:, at], out_weight[...], 0, 0)
        resid[at, :] = r
        rhat, _ = norm_parts(r)
        n2[at, :] = (rhat * ffn_gain[...]).astype(BF16)

    def inner(block, j):
        if block == 0 and j == 1:
            top(1)
        return dot(n2[half * block : half * block + half, :], ffn_in[:, step * j : step * j + step])

    def gelu(block, j, v):
        at = (slice(half * block, half * block + half), slice(step * j, step * j + step))
        v2 = v * v
        h = 0.5 * jnp.tanh(v * (k0 + (0.044715 * k0) * v2)) + 0.5
        act[at] = (v * h).astype(BF16)
        w = v * (2.0 * k0 + (6.0 * 0.044715 * k0) * v2)
        dg[at] = (h + h * (1.0 - h) * w).astype(BF16)

    def bottom(block):
        at = slice(half * block, half * block + half)
        out[at, :] = (resid[at, :] + dot(act[at, :], ffn_out[...])).astype(BF16)

    top(0)
    held = None
    for n in range(2 * chunks + 1):
        now = None
        if n < 2 * chunks:
            now = inner(n // chunks, n % chunks)
        if held is not None:
            gelu(*held)
        if n == chunks + 1:
            bottom(0)
        held = (n // chunks, n % chunks, now)
    bottom(1)
    out_own[...] = out[part(place, half, True), :]


def write_body(
    place, out, wqs, mem, memory_cotangent, recv, write_pair, write_out, write_gate, write_gain, nall,
    send, keep, dwpair, dwquery, dblend, own_new, newmem, gain_out,
):
    c, ks = place[1], (send, keep)
    slots, width = wqs.shape
    o = out[...]
    wk = dot(o, write_pair[:, :width]).astype(BF16)
    wv = dot(o, write_pair[:, width:]).astype(BF16)
    mask = head_mask(slots, width)
    qbd = block_diagonal(wqs[...], mask)
    s = dot(qbd, wk, 1, 1)
    e = jnp.exp(s - jnp.max(s, -1, keepdims=True))
    pf = e * (1.0 / jnp.sum(e, -1, keepdims=True))
    pb = pf.astype(BF16)
    wmixed = diagonal_blocks(dot(pb, wv), mask).astype(BF16)
    update = dot(wmixed, write_out[...])
    update_low = update.astype(BF16)
    gate = jax.nn.sigmoid(dot(update_low, write_gate[...]))
    blended = mem[...].astype(F32) + gate * update
    bhat, br = norm_parts(blended)
    gain = write_gain[...]
    newmem[...] = (bhat * gain).astype(BF16)
    mhalf = slots // 2
    own_new[...] = newmem[part(place, mhalf, True), :]
    mc = whole_rows(place, memory_cotangent, recv, recv.shape[0] - mhalf, mhalf).astype(F32)
    d_blend, d_gain = norm_back(mc, bhat, br, gain)
    gain_out[...] = d_gain
    dblend[...] = d_blend
    d_gate_pre = (d_blend * update * gate * (1.0 - gate)).astype(BF16)
    d_update = (d_blend * gate + dot(d_gate_pre, write_gate[...], 1, 1)).astype(BF16)
    d_wmixed = dot(d_update, write_out[...], 1, 1).astype(BF16)
    emit_rows(dot(update_low, d_gate_pre, 0, 0), 32, ks, 128, c)
    emit_rows(dot(wmixed, d_update, 0, 0), 32, ks, 96, c)
    dbd = block_diagonal(d_wmixed, mask)
    dp = dot(dbd, wv, 1, 1)
    row = jnp.sum(pf * dp, -1, keepdims=True)
    ds = (pf * (dp - row)).astype(BF16)
    d_wquery = (diagonal_blocks(dot(ds, wk), mask) * 0.125).astype(BF16)
    dwquery[...] = d_wquery
    dwk = dot(ds, qbd, 0, 0).astype(BF16)
    dwv = dot(pb, dbd, 0, 0).astype(BF16)
    dwpair[:, :width] = dwk
    dwpair[:, width:] = dwv
    emit_rows(dot(nall[0:slots, :], d_wquery, 0, 0), 32, ks, 0, c)
    emit_rows(dot(o, dwk, 0, 0), 32, ks, 32, c)
    emit_rows(dot(o, dwv, 0, 0), 32, ks, 64, c)


def ffn_back_body(
    place, dwpair, write_pair, out_cotangent, recv, ffn_out, dg, act,
    send, keep, dout_out, dinner,
):
    c, ks = place[1], (send, keep)
    ff, width = ffn_out.shape
    deep = ff // GROUPS
    cot = whole_rows(place, out_cotangent, recv, 0, out_cotangent.shape[1])
    d_out = cot.astype(F32) + dot(dwpair[...], write_pair[...], 1, 1)
    dout_out[...] = d_out
    d_branch = d_out.astype(BF16)
    for j in range(ff // 512):
        cols = slice(512 * j, 512 * j + 512)
        d_act = dot(d_branch, ffn_out[cols, :], 1, 1).astype(BF16)
        dinner[:, cols] = (d_act.astype(F32) * dg[:, cols].astype(F32)).astype(BF16)
        emit_rows(
            dot(act[:, cols], d_branch, 0, 0), deep, ks, 0, c, 512 // (2 * deep) * j,
        )


def inner_back_body(
    place, dinner, n2, ffn_in,
    send, keep, total,
):
    rows = ffn_in.shape[0] // GROUPS
    for j in range(ffn_in.shape[1] // 512):
        cols = slice(512 * j, 512 * j + 512)
        emit_rows(dot(n2[...], dinner[:, cols], 0, 0), rows, (send, keep), rows * j, place[1])
    total[...] = dot(dinner[...], ffn_in[...], 1, 1)


def resid_back_body(
    place, total, dout, resid, ffn_gain, mixed,
    send, keep, dresid, gain_out,
):
    rhat, rr = norm_parts(resid[...])
    d_norm, d_gain = norm_back(total[...], rhat, rr, ffn_gain[...])
    gain_out[...] = d_gain
    d = dout[...] + d_norm
    dresid[...] = d
    d_attn = d.astype(BF16)
    emit_rows(dot(mixed[...], d_attn), 32, (send, keep), 0, place[1])


def attn_back_body(
    place, qs, dresid, out_weight, vall, p3, kall, p2, p1, p0,
    dq_out, dk_out, dv_out, dk_ref, dv_ref, dqt_ref, dm, kt,
):
    dm[...] = dot(dresid[...].astype(BF16), out_weight[...], 1, 1).astype(BF16)
    kt[...] = kall[...].T
    probs = (p0, p1, p2, p3)

    def first(i, p):
        w, lanes = 128 * (i + 2), slice(128 * p, 128 * p + 128)
        dm01 = stacked_heads(dm[128 * i : 128 * i + 128, lanes])
        dv = dot(probs[i][p], dm01)
        if i == 3:
            dv_ref[0:w, lanes] = dv
        else:
            dv_ref[0:w, lanes] += dv
        return dot(vall[0:w, lanes], dm01, 1, 1)

    def second(i, p, dp):
        pf = probs[i][p].astype(F32)
        t = pf * dp
        return (t - pf * jnp.sum(t, 0, keepdims=True)).astype(BF16)

    def third(i, p, ds):
        w, lanes = 128 * (i + 2), slice(128 * p, 128 * p + 128)
        rows = slice(128 * i, 128 * i + 128)
        q01 = stacked_heads(qs[rows, lanes])
        dqt = (dot(kt[lanes, 0:w], ds) * 0.125).astype(BF16)
        dqt_ref[128 * p : 128 * p + 64, rows] = dqt[:64, :128]
        dqt_ref[128 * p + 64 : 128 * p + 128, rows] = dqt[64:, 128:]
        dk = dot(ds, q01)
        if i == 3:
            dk_ref[0:w, lanes] = dk
        else:
            dk_ref[0:w, lanes] += dk

    in_steps(
        [(i, p) for p in range(H // 2) for i in (3, 2, 1, 0)], (first, second, third)
    )
    dq_out[...] = dqt_ref[...].T
    dk_out[...] = dk_ref[...].astype(BF16)
    dv_out[...] = dv_ref[...].astype(BF16)


def input_back_body(
    place, nall, dq, dk, dv, pair_weight, query_weight, dwquery, write_query, x, mem, attn_gain,
    dresid, dblend, gain2, gain3, newmem, out,
    qsend, qkeep, ksend, kkeep, vsend, vkeep, gsend, gkeep, own_tok, own_mem, swap, gtok, gmem,
):
    c = place[1]
    rows, width = x.shape
    slots = mem.shape[0]
    half, mhalf = rows // 2, slots // 2
    na = nall[...]
    dqv = dq[...]
    emit_rows(dot(na[128:], dqv, 0, 0), 32, (qsend, qkeep), 0, c)
    emit_rows(dot(na, dk[...], 0, 0), 32, (ksend, kkeep), 0, c)
    emit_rows(dot(na, dv[...], 0, 0), 32, (vsend, vkeep), 0, c)
    d_all = dot(dk[...], pair_weight[:, :width], 1, 1)
    d_all = d_all + dot(dv[...], pair_weight[:, width:], 1, 1)
    d_nx = d_all[128:] + dot(dqv, query_weight[...], 1, 1)
    d_nm = d_all[:slots] + dot(dwquery[...], write_query[...], 1, 1)
    gain = attn_gain[...]
    xhat, xr = norm_parts(x[...].astype(F32))
    d_x, g_x = norm_back(d_nx, xhat, xr, gain)
    mhat, mr = norm_parts(mem[...].astype(F32))
    d_m, g_m = norm_back(d_nm, mhat, mr, gain)
    gains = jnp.concatenate(
        [g_x + g_m, gain2[...], gain3[...], jnp.zeros((13, width), F32)], 0
    ).astype(BF16)
    for one in (gsend, gkeep):
        one[...] = jnp.broadcast_to(gains, (GROUPS // 2, 16, width))
    gtok[...] = dresid[...] + d_x
    gmem[...] = dblend[...] + d_m
    own_tok[...] = gtok[part(place, half, True), :]
    own_mem[...] = gmem[part(place, mhalf, True), :]
    other = part(place, half, False)
    mother = part(place, mhalf, False)
    swap[0:half, :] = gtok[other, :].astype(BF16)
    swap[half : half + mhalf, :] = newmem[mother, :]
    swap[half + mhalf : half + 2 * mhalf, :] = gmem[mother, :].astype(BF16)
    swap[half + 2 * mhalf :, :] = out[other, :]


BIT = {"y": 0, "x": 2, "z": 3, "h": 4}


def other_of(axis, bit):
    return [(i, i ^ bit) for i in range(lax.axis_size(axis))]


def exchanged(send, label):
    if label == "y":
        return lax.ppermute(send, "seq", other_of("seq", 1))
    return lax.ppermute(send, "seg", other_of("seg", {"x": 2, "z": 4, "h": 8, "c": 1}[label]))


class Stream:
    def __init__(self, keep, recv, dims, start, rows):
        self.keep, self.recv, self.dims, self.start, self.rows = keep, recv, dims, start, rows


def stage(streams, labels, joined=False, deps=(), tail=False):
    ins = []
    index = {}
    for s in streams:
        for arr in (s.keep, s.recv):
            if id(arr) not in index:
                index[id(arr)] = len(ins)
                ins.append(("v", arr))
    n_arrays = len(ins)
    ins += [("d", d) for d in deps]
    width = streams[0].keep.shape[-1]
    shapes, new_dims, new_rows = [], [], []
    for s, label in zip(streams, labels):
        rows = s.rows // 2 if label == "y" else s.rows
        dims = s.dims.replace(label, "")
        new_dims.append(dims)
        new_rows.append(rows)
        shapes.append((2,) * len(dims) + (rows, width))
    if joined:
        shapes = [(sum(new_rows), width)]
    if tail:
        shapes = shapes[:-2] + [shapes[-2][:-2] + (new_rows[-2] + new_rows[-1], width)]
    outs = []
    for shape in shapes:
        outs += [(shape, BF16)] * 2

    def body(place, *refs):
        given, made = refs[:n_arrays], refs[n_arrays:]

        def value(s, label, own, arr):
            bit = place[BIT[label]]
            bit = bit if own else 1 - bit
            where = []
            for d in s.dims:
                where.append(bit if d == label else slice(None))
            if label == "y":
                half = s.rows // 2
                where.append(pl.ds(pl.multiple_of(s.start + bit * half, 16), half))
            else:
                where.append(slice(s.start, s.start + s.rows))
            return given[index[id(arr)]][tuple(where) + (slice(None),)].astype(F32)

        for own in (False, True):
            at = 0
            for k, (s, label) in enumerate(zip(streams, labels)):
                total = (value(s, label, own, s.keep) + value(s, label, own, s.recv)).astype(BF16)
                last = tail and k == len(streams) - 1
                target = made[(0 if joined else 2 * (k - last)) + (0 if own else 1)]
                if joined:
                    target[at : at + new_rows[k], :] = total
                    at += new_rows[k]
                elif last:
                    target[..., new_rows[k - 1] :, :] = total
                elif tail and k == len(streams) - 2:
                    target[..., : new_rows[k], :] = total
                else:
                    target[...] = total

    results = call(body, ins, outs, flops=10**6, nbytes=10**6)
    if joined:
        return results[0], results[1]
    if tail:
        new_rows = new_rows[:-2] + [new_rows[-2] + new_rows[-1]]
    return [
        (results[2 * k], results[2 * k + 1], new_dims[k], n) for k, n in enumerate(new_rows)
    ]


def added(keep, recv, deps=()):
    def body(place, keep, recv, total):
        total[...] = (keep[...].astype(F32) + recv[...].astype(F32)).astype(BF16)

    (total,) = call(
        body,
        [("v", keep), ("v", recv)] + [("d", d) for d in deps],
        [(keep.shape, BF16)],
        flops=10**6, nbytes=10**6,
    )
    return total


class Late:
    def __init__(self, pairs, order):
        flat = lambda a: a.reshape(-1, a.shape[2])
        self.arrays = [(flat(keep), flat(recv), [keep.shape[1]]) for keep, recv in pairs]
        self.order, self.dims = order, "hzx"

    def joined(self, other):
        self.arrays = self.arrays + other.arrays
        return self

    def next(self, deps=()):
        label = self.order[3 - len(self.dims)]
        at = self.dims.index(label)
        count = 1 << at
        plan, target = [], 0
        for array, (_, _, pieces) in enumerate(self.arrays):
            source = 0
            for rows in pieces:
                size = rows << (len(self.dims) - 1 - at)
                for b in range(count):
                    plan.append((array, source + 2 * b * size, target + b * size, size))
                source += 2 * count * size
                target += count * size

        def body(place, *refs):
            bit = place[BIT[label]]
            for out, b in ((refs[-1], 1 - bit), (refs[-2], bit)):
                for array, start, to, size in plan:
                    rows = pl.ds(pl.multiple_of(start + b * size, 16), size)
                    out[to : to + size, :] = (
                        refs[2 * array][rows, :].astype(F32)
                        + refs[2 * array + 1][rows, :].astype(F32)
                    ).astype(BF16)

        ins = [("v", a) for keep, recv, _ in self.arrays for a in (keep, recv)]
        ins += [("d", d) for d in deps]
        width = self.arrays[0][0].shape[1]
        keep, send = call(body, ins, [((target, width), BF16)] * 2, flops=10**6, nbytes=10**6)
        pieces = sum([p for _, _, p in self.arrays], [])
        self.arrays = [(keep, exchanged(send, label), pieces)]
        self.dims = self.dims.replace(label, "")


def in_hbm(a):
    return pltpu.with_memory_space_constraint(a, pltpu.HBM)


def packed(body_rows, extra_rows):
    half, width = body_rows.shape[1:]
    extra = extra_rows.shape[1]

    def kernel(a, b, o, sem):
        other = 1 - lax.axis_index("seq")
        copies = [
            pltpu.make_async_copy(a.at[other], o.at[0:half], sem.at[0]),
            pltpu.make_async_copy(b.at[other], o.at[half:], sem.at[1]),
        ]
        for copy in copies:
            copy.start()
        for copy in copies:
            copy.wait()

    return pl.pallas_call(
        kernel,
        out_shape=pltpu.VMEM((half + extra, width), body_rows.dtype),
        in_specs=[pl.BlockSpec(memory_space=pltpu.HBM)] * 2,
        out_specs=pl.BlockSpec(memory_space=pltpu.VMEM),
        scratch_shapes=[pltpu.SemaphoreType.DMA((2,))],
        compiler_params=pltpu.CompilerParams(vmem_limit_bytes=4 * 1024 * 1024),
    )(in_hbm(body_rows), in_hbm(extra_rows))


def assembled(own, recv, dtypes, deps=()):
    width = own[0].shape[1]

    def body(place, *refs):
        n = len(own)
        start = 0
        for mine, out in zip(refs[:n], refs[n + 1 :]):
            rows = mine.shape[0]
            out[place[0]] = mine[...].astype(out.dtype)
            out[1 - place[0]] = refs[n][start : start + rows, :].astype(out.dtype)
            start += rows

    return call(
        body,
        [("v", a) for a in own] + [("v", recv)] + [("d", d) for d in deps],
        [((2,) + a.shape, d) for a, d in zip(own, dtypes)],
        flops=10**6, nbytes=10**6, home=False,
    )


def fetched_weights(weights, tokens, gain):
    half, width = tokens.shape[1:]
    n = len(weights)

    def kernel(tokens, gain, *refs):
        y = lax.axis_index("seq")
        own, sem = refs[-2], refs[-1]
        copies = [pltpu.make_async_copy(tokens.at[y], own, sem.at[n])]
        order = [n - 2, n - 1] + list(range(n - 2))
        waits = {k: pltpu.make_async_copy(refs[k], refs[n + k], sem.at[k]) for k in order}
        copies[0].start()
        for k in order:
            waits[k].start()
        x_ref, n_ref, q_ref, k_ref, v_ref = refs[2 * n : 2 * n + 5]
        copies[0].wait()
        x_ref[...] = own[...]
        xhat, _ = norm_parts(own[...].astype(F32))
        nx = (xhat * gain[...]).astype(BF16)
        n_ref[...] = nx
        waits[n - 2].wait()
        q_ref[...] = (dot(nx, refs[2 * n - 2][...]) * 0.125).astype(BF16)
        waits[n - 1].wait()
        k_ref[...] = dot(nx, refs[2 * n - 1][:, :width]).astype(BF16)
        v_ref[...] = dot(nx, refs[2 * n - 1][:, width:]).astype(BF16)
        for k in order[2:]:
            waits[k].wait()

    one = pltpu.VMEM((half, width), BF16)
    results = pl.pallas_call(
        kernel,
        out_shape=[pltpu.VMEM(a.shape, a.dtype) for a in weights] + [one] * 5,
        in_specs=[pl.BlockSpec(memory_space=pltpu.HBM), pl.BlockSpec(memory_space=pltpu.VMEM)]
        + [pl.BlockSpec(memory_space=pltpu.HBM)] * n,
        out_specs=[pl.BlockSpec(memory_space=pltpu.VMEM)] * (n + 5),
        scratch_shapes=[pltpu.VMEM((half, width), BF16), pltpu.SemaphoreType.DMA((n + 1,))],
        compiler_params=pltpu.CompilerParams(vmem_limit_bytes=8 * 1024 * 1024),
        cost_estimate=pl.CostEstimate(flops=10**9, bytes_accessed=10**7, transcendentals=0),
    )(in_hbm(tokens), gain, *[in_hbm(a) for a in weights])
    return results[:n], results[n:]


def reduced_any(keep, send, pieces):
    groups = lax.axis_size("seg")
    c = lax.axis_index("seg") % 2
    first = jnp.where(c == 0, keep, send)
    second = jnp.where(c == 0, send, keep)
    total = jnp.stack([first, second], 1)
    total = total.reshape((GROUPS,) + keep.shape[1:])
    fine = groups // GROUPS
    parts = []
    at = 0
    for rows, shared in pieces:
        piece = total[:, at : at + rows]
        if shared:
            piece = jnp.broadcast_to(piece[:, None], (GROUPS, fine) + piece.shape[1:])
        else:
            piece = piece.reshape(GROUPS, fine, rows // fine, piece.shape[2])
        parts.append(piece.reshape(groups, -1, piece.shape[-1]))
        at += rows
    total = jnp.concatenate(parts, 1)
    total = lax.psum_scatter(total.astype(F32), "seg", scatter_dimension=0, tiled=True)[0]
    return lax.psum(total, "seq")


def final_parts(one, two, ff):
    ours, theirs, split = one
    t2, o2 = two
    width = t2.shape[-1]
    r = width // GROUPS
    n = ff // 512
    count = len(ours)
    shapes = [
        (r, width), (r, 2 * width), (r, width), (r, ff), (ff // GROUPS, width),
        (r, width), (r, 2 * width), (r, width), (r, width), (r,), (r,), (r,),
    ]

    def body(place, *refs):
        t2, o2, gq, gp, go, gfi, gfo, gwq, gwp, gwo, gwg, g0, g1, g2, full = refs[2 * count :]
        y = place[0]
        at = start = 0
        for rows in split:
            half = rows // 2
            for ref, index in ((refs[0], y), (refs[1], 1 - y)):
                full[pl.ds(pl.multiple_of(start + index * half, 16), half), :] = ref[
                    at : at + half, :
                ].astype(F32)
            at += half
            start += rows
        total = (t2[...].astype(F32) + o2[...].astype(F32))
        gq[...] = total[0:r, :]
        gp[:, :width] = total[r : 2 * r, :]
        gp[:, width:] = total[2 * r : 3 * r, :]
        seg = lax.axis_index("seg")
        gains = pltpu.roll(total[3 * r : 3 * r + 8, :], (width - seg * r) % width, 1)
        for k, ref in enumerate((g0, g1, g2)):
            ref[...] = gains[k, :r]
        gwq[...] = full[0:r, :]
        gwp[:, :width] = full[r : 2 * r, :]
        gwp[:, width:] = full[2 * r : 3 * r, :]
        gwo[...] = full[3 * r : 4 * r, :]
        gwg[...] = full[4 * r : 5 * r, :]
        for j in range(n):
            gfi[:, 512 * j : 512 * j + 512] = full[(5 + j) * r : (6 + j) * r, :]
        gfo[...] = full[(5 + n) * r : (5 + n) * r + ff // GROUPS, :]
        go[...] = full[(5 + n) * r + ff // GROUPS :, :]

    return call(
        body, [("v", a) for a in (*ours, *theirs, t2, o2)], [(s, F32) for s in shapes],
        scratch=[((sum(split), width), F32)], flops=10**6, nbytes=10**6, home=False,
    )


def shards(
    tokens, memory, lengths, attn_gain, query_weight, pair_weight, out_weight, ffn_gain, ffn_in,
    ffn_out, write_query, write_pair, write_out, write_gate, write_gain, out_cotangent,
    memory_cotangent,
):
    half, width = tokens.shape[1:]
    mhalf = memory.shape[1]
    rows, slots, ff = 2 * half, 2 * mhalf, ffn_in.shape[1]
    padded = rows + 128
    groups = lax.axis_size("seg")
    recv_a = exchanged(packed(tokens, memory), "y")
    recv_b = exchanged(packed(out_cotangent, memory_cotangent), "y")
    (
        memory, out_cotangent, memory_cotangent, out_weight, ffn_in, ffn_out, write_query,
        write_pair, write_out, write_gate, query_weight, pair_weight,
    ), own_rows = fetched_weights(
        (
            memory, out_cotangent, memory_cotangent, out_weight, ffn_in, ffn_out, write_query,
            write_pair, write_out, write_gate, query_weight, pair_weight,
        ),
        tokens, attn_gain[None],
    )
    ag, fg, wg = attn_gain[None], ffn_gain[None], write_gain[None]
    v = lambda *arrs: [("v", a) for a in arrs]
    h = lambda *arrs: [("h", a) for a in arrs]
    deps = lambda *arrs: [("d", a) for a in arrs]
    big = ((rows, width), BF16)
    wide = ((padded, width), BF16)
    deep = ((rows, ff), BF16)
    half_b = ((half, width), BF16)
    keep_send = lambda n: [((GROUPS // 2, n, width), BF16)] * 2
    small = ((slots, width), BF16)
    full_f = ((rows, width), F32)
    gain_row = ((1, width), F32)
    (
        x, mem, nall, qs, kall, vall, p0, p1, p2, p3, mixed, resid, n2, act, dg,
        out_own, out, wqs,
    ) = call(
        forward_body,
        [("s", lengths)] + v(*own_rows, memory, recv_a, ag, query_weight, pair_weight)
        + v(write_query, out_weight, fg, ffn_in, ffn_out),
        [big, small, wide, big, wide, wide]
        + [((H // 2, 128 * (i + 2), 256), BF16) for i in range(4)]
        + [big, full_f, big, deep, deep, half_b, big, small],
        scratch=[((width, padded), BF16)],
        flops=2 * 6 * 10**9, nbytes=20 * 10**6, limit=16,
    )
    send0, keep0, dwpair, dwquery, dblend, own_new, newmem, gain3 = call(
        write_body,
        v(out, wqs, mem, memory_cotangent, recv_b, write_pair, write_out, write_gate, wg, nall),
        [
            *keep_send(160), ((rows, 2 * width), BF16), small,
            ((slots, width), F32), ((mhalf, width), BF16), small, gain_row,
        ],
        flops=2 * 3 * 10**9, nbytes=10 * 10**6,
    )
    small_mesh = groups == GROUPS
    cube = lambda a: a.reshape((2, 2, 2) + a.shape[1:])
    pair = lambda keep, send: (cube(keep), cube(exchanged(send, "c")))
    deps0 = deps1 = []
    send1, keep1, dout, dinner = call(
        ffn_back_body,
        v(dwpair, write_pair, out_cotangent, recv_b, ffn_out, dg, act),
        [*keep_send(128), full_f, deep],
        flops=2 * 5 * 10**9, nbytes=20 * 10**6,
    )
    if small_mesh:
        k0, r0 = pair(keep0, send0)
        deps0 = deps(r0)
    send4, keep4, total = call(
        inner_back_body, v(dinner, n2, ffn_in) + deps0, [*keep_send(128), full_f],
        flops=10**9, nbytes=20 * 10**6,
    )
    if small_mesh:
        k1, r1 = pair(keep1, send1)
        deps0 = deps(r1)
    send3, keep3, dresid, gain2 = call(
        resid_back_body, v(total, dout, resid, fg, mixed) + deps0,
        [*keep_send(32), full_f, gain_row],
        flops=10**8, nbytes=10**6,
    )
    orders = ("xyz", "yzx", "zxy")
    late_orders = ("xz", "zx")

    def moved(parts, labels):
        return [
            Stream(keep, exchanged(send, label), dims, 0, r)
            for label, (keep, send, dims, r) in zip(labels, parts)
        ]

    nth = lambda these, step: [o[step] for o in these]
    if small_mesh:
        k4, r4 = pair(keep4, send4)
        k3, r3 = pair(keep3, send3)
        streams = [
            Stream(k0, r0, "hzx", 0, 160), Stream(k4, r4, "hzx", 0, 128),
            Stream(k1, r1, "hzx", 0, 128), Stream(k3, r3, "hzx", 0, 32),
        ]
        parts = stage_joined(streams, nth(orders, 0), [])
        deps1 = deps(parts[0][0])
        first = moved(parts, nth(orders, 0))
    dq, dk, dv = call(
        attn_back_body,
        v(qs, dresid, out_weight, vall, p3, kall, p2, p1, p0) + deps1,
        [big, wide, wide],
        scratch=[((padded, width), F32)] * 2 + [big, big, ((width, padded), BF16)],
        flops=2 * 6 * 10**9, nbytes=20 * 10**6,
    )
    *grads2, own_tok, own_mem, swap = call(
        input_back_body,
        v(
            nall, dq, dk, dv, pair_weight, query_weight, dwquery, write_query, x, mem, ag, dresid,
            dblend, gain2, gain3, newmem, out,
        ),
        [
            *keep_send(32), *keep_send(32), *keep_send(32), *keep_send(16), ((half, width), F32), ((mhalf, width), F32),
            ((2 * half + 2 * mhalf, width), BF16),
        ],
        scratch=[((rows, width), F32), ((slots, width), F32)],
        flops=2 * 3 * 10**9, nbytes=20 * 10**6,
    )
    r = width // groups
    if small_mesh:
        def each(streams, labels, deps=()):
            results = []
            for stream, label in zip(streams, labels):
                results += stage([stream], [label], deps=list(deps))
            return moved(results, labels)

        second = each(first, nth(orders, 1), [swap])
        pieces = [(grads2[k + 1], exchanged(grads2[k], "c")) for k in range(0, 8, 2)]
        by_x, by_z = Late(pieces[:2], "xzh"), Late(pieces[2:], "zxh")
        by_x.next()
        by_z.next()
        third = each(second, nth(orders, 2))
        behind = [stream.keep for stream in third]
        by_x.next(behind)
        by_z.next(behind)
        keep, send = stage(third, "hhh", joined=True)
        swapped = exchanged(swap, "y")
        by_x.joined(by_z).next([keep])
        t1 = added(keep, exchanged(send, "h"))
        one, two = [t1], [exchanged(t1, "y")]
        t2 = added(*by_x.arrays[0][:2])
        o2 = exchanged(t2, "y")
        gq, gp, go, gfi, gfo, gwq, gwp, gwo, gwg, *gains = final_parts(
            (one, two, (160, 128, 160)), (t2, o2), ff
        )
    else:
        w = width // GROUPS
        w0 = reduced_any(keep0, send0, [(w, False)] * 5)
        gfo = reduced_any(keep1, send1, [(ff // GROUPS, False)])
        w1 = reduced_any(keep4, send4, [(w, False)] * (ff // 512))
        w2 = jnp.concatenate(
            [
                reduced_any(grads2[k + 1], grads2[k], [(w, False)] if k < 6 else [(16, True)])
                for k in range(0, 8, 2)
            ],
            0,
        )
        go = reduced_any(keep3, send3, [(w, False)])
        cut = lambda a, at, n: jnp.concatenate(
            [a[(at + i) * r : (at + i + 1) * r] for i in range(n)], 1
        )
        gq, gp = cut(w2, 0, 1), cut(w2, 1, 2)
        gfi = cut(w1, 0, ff // 512)
        gwq, gwp, gwo, gwg = cut(w0, 0, 1), cut(w0, 1, 2), cut(w0, 3, 1), cut(w0, 4, 1)
        at = lax.axis_index("seg") * r
        gains = [lax.dynamic_slice_in_dim(w2[3 * r + i], at, r, 0) for i in range(3)]
    if not small_mesh:
        swapped = exchanged(swap, "y")
    tok_both, new_both, mem_both, out_both = assembled(
        [own_tok, own_new, own_mem, out_own], swapped, [F32, BF16, F32, BF16]
    )
    return (
        out_both, new_both, tok_both, mem_both,
        gains[0], gq, gp, go, gains[1], gfi, gfo, gwq, gwp, gwo, gwg, gains[2],
    )


def stage_joined(streams, labels, deps):
    return stage(streams, list(labels) + [labels[-1]], tail=True, deps=deps)


def solution(mesh):
    row = P("seg", "seq", None)
    grad = P("seg", None)
    in_specs = (row, row, P("seg", None)) + (P(),) * 12 + (row, row)
    out_specs = (row, row, row, row, P("seg"), grad, grad, grad, P("seg")) + (grad,) * 6 + (P("seg"),)
    return jax.shard_map(shards, mesh=mesh, in_specs=in_specs, out_specs=out_specs, check_vma=False)
```

```python
import jax
import jax.numpy as jnp
from jax import lax
from jax.experimental import pallas as pl
from jax.experimental.pallas import tpu as pltpu
from jax.sharding import PartitionSpec as P

H = 8
GROUPS = 16
EPSILON = 1e-05
MASKED = -1e30
F32 = jnp.float32
BF16 = jnp.bfloat16
VMEM_LIMIT = 56 * 1024 * 1024


def part(place, half, own):
    index = place[0] if own else 1 - place[0]
    return pl.ds(pl.multiple_of(index * half, half), half)


class Fetched:
    def __init__(self, source, ref, sem):
        self.ref, self.copy, self.waited = ref, pltpu.make_async_copy(source, ref, sem), False

    def __call__(self):
        if not self.waited:
            self.copy.wait()
            self.waited = True
        return self.ref


def position():
    seg = lax.axis_index("seg")
    return [lax.axis_index("seq")] + [(seg >> k) & 1 for k in range(4)]


def call(body, ins, outs, scratch=(), flops=0, nbytes=0, limit=16, home=True):
    kinds = [kind for kind, _ in ins]
    arrays = [
        pltpu.with_memory_space_constraint(a, pltpu.VMEM) if kind == "v" else a for kind, a in ins
    ]
    spaces = {"s": pltpu.SMEM, "v": pltpu.VMEM, "d": pl.ANY, "h": pl.ANY}
    fetched = [pltpu.VMEM(a.shape, a.dtype) for kind, a in ins if kind == "h"]
    n_io = len(ins) + len(outs)

    def kernel(*refs):
        given, at = [], 0
        for kind, r in zip(kinds, refs):
            if kind == "h":
                r = Fetched(r, refs[n_io + at], refs[-1].at[at])
                r.copy.start()
                at += 1
            if kind != "d":
                given.append(r)
        end = -1 if fetched else len(refs)
        body(position(), *given, *refs[len(ins) : n_io], *refs[n_io + at : end])
        for r in given:
            if isinstance(r, Fetched):
                r()

    shape = (lambda s, d: pltpu.VMEM(s, d)) if home else jax.ShapeDtypeStruct
    sems = [pltpu.SemaphoreType.DMA((len(fetched),))] if fetched else []
    return pl.pallas_call(
        kernel,
        out_shape=[shape(s, d) for s, d in outs],
        in_specs=[pl.BlockSpec(memory_space=spaces[kind]) for kind in kinds],
        out_specs=[pl.BlockSpec(memory_space=pltpu.VMEM)] * len(outs),
        scratch_shapes=fetched + [pltpu.VMEM(s, d) for s, d in scratch] + sems,
        compiler_params=pltpu.CompilerParams(vmem_limit_bytes=limit * 1024 * 1024),
        cost_estimate=pl.CostEstimate(flops=flops, bytes_accessed=nbytes, transcendentals=0),
    )(*arrays)


def dot(a, b, ca=1, cb=0):
    return lax.dot_general(a, b, (((ca,), (cb,)), ((), ())), preferred_element_type=F32)


def norm_parts(v):
    centred = v - jnp.mean(v, -1, keepdims=True)
    r = lax.rsqrt(jnp.mean(centred * centred, -1, keepdims=True) + EPSILON)
    return centred * r, r


def norm_back(dy, xhat, r, gain):
    dx = dy * gain
    m1 = jnp.mean(dx, -1, keepdims=True)
    m2 = jnp.mean(dx * xhat, -1, keepdims=True)
    return r * (dx - m1 - xhat * m2), jnp.sum(dy * xhat, 0, keepdims=True)


def emit_rows(grad, rows, ks_ref, offset, c, first=0):
    pairs = grad.shape[0] // (2 * rows)
    g = grad.astype(BF16).reshape(pairs, 2, rows, grad.shape[1])
    where = (slice(first, first + pairs), slice(offset, offset + rows), slice(None))
    even, odd = g[:, 0], g[:, 1]
    send_ref, keep_ref = ks_ref
    keep_ref[where] = jnp.where(c == 0, even, odd)
    send_ref[where] = jnp.where(c == 0, odd, even)


def whole_rows(place, pair_ref, recv_ref, start, half):
    own, other = pair_ref[place[0]], recv_ref[start : start + half, :]
    first = place[0] == 0
    return jnp.concatenate([jnp.where(first, own, other), jnp.where(first, other, own)], 0)


def lane_low(shape):
    return lax.broadcasted_iota(jnp.int32, shape, 1) < 64


def stacked_heads(block):
    low = lane_low(block.shape)
    zero = jnp.zeros_like(block)
    return jnp.concatenate([jnp.where(low, block, zero), jnp.where(low, zero, block)], 0)


def unstacked_heads(block):
    rows = block.shape[0] // 2
    top, bottom = block[:rows], block[rows:]
    return jnp.where(lane_low(top.shape), top, bottom)


def head_mask(rows_per, width):
    shape = (H * rows_per, width)
    row_head = lax.broadcasted_iota(jnp.int32, shape, 0) // rows_per
    col_head = lax.broadcasted_iota(jnp.int32, shape, 1) // (width // H)
    return row_head == col_head


def block_diagonal(v, mask):
    return jnp.where(mask, jnp.concatenate([v] * H, 0), jnp.zeros((), v.dtype))


def diagonal_blocks(v, mask):
    rows = v.shape[0] // H
    v = jnp.where(mask, v, 0.0)
    return jnp.sum(v.reshape(H, rows, v.shape[1]), 0)


def in_steps(items, stages):
    held = {}
    for step in range(len(items) + len(stages) - 1):
        for k, stage_of in enumerate(stages):
            n = step - k
            if 0 <= n < len(items):
                given = () if k == 0 else (held.pop((n, k - 1)),)
                held[n, k] = stage_of(*items[n], *given)


def forward_body(
    place, lengths, x_own, n_own, q_own, k_own, v_own, memory, recv, attn_gain, query_weight, pair_weight, write_query, out_weight,
    ffn_gain, ffn_in, ffn_out,
    x, mem, nall, qs, kall, vall, p0, p1, p2, p3, mixed, resid, n2, act, dg,
    out_own, out, wqs, vt,
):
    y = place[0]
    width = pair_weight.shape[0]
    rows = x.shape[0]
    slots = mem.shape[0]
    half = rows // 2
    own, other = part(place, half, True), part(place, half, False)
    x[own, :] = x_own[...]
    x_other = recv[0:half, :]
    x[other, :] = x_other
    mem[...] = whole_rows(place, memory, recv, half, slots // 2)
    gain = attn_gain[...]
    xhat, _ = norm_parts(x_other.astype(F32))
    nx = (xhat * gain).astype(BF16)
    mhat, _ = norm_parts(mem[...].astype(F32))
    nm = (mhat * gain).astype(BF16)
    some = jnp.concatenate([nm, jnp.zeros((128 - slots, width), BF16), nx], 0)
    own_at = pl.ds(pl.multiple_of(128 + place[0] * half, 128), half)
    other_at = pl.ds(pl.multiple_of(128 + (1 - place[0]) * half, 128), half)
    qs[own, :] = q_own[...]
    qs[other, :] = (dot(nx, query_weight[...]) * 0.125).astype(BF16)
    for ref, mine, value in (
        (nall, n_own, some),
        (kall, k_own, dot(some, pair_weight[:, :width]).astype(BF16)),
        (vall, v_own, dot(some, pair_weight[:, width:]).astype(BF16)),
    ):
        ref[0:128, :] = value[:128]
        ref[own_at, :] = mine[...]
        ref[other_at, :] = value[128:]
    wqs[...] = (dot(nm, write_query[...]) * 0.125).astype(BF16)
    bounds = []
    total = 0
    for k in range(lengths.shape[1]):
        total = total + lengths[y, k]
        bounds.append(total)
    pos_k = lax.broadcasted_iota(jnp.int32, (rows, 1), 0)
    doc_k = sum([(pos_k >= b).astype(jnp.int32) for b in bounds])
    mem_bias = jnp.where(
        lax.broadcasted_iota(jnp.int32, (128, 128), 0) < slots, 0.0, MASKED
    ).astype(F32)
    vt[...] = vall[...].T
    biases = []
    for i in range(4):
        cols = 128 * (i + 1)
        pos_q = lax.broadcasted_iota(jnp.int32, (1, 128), 1) + 128 * i
        doc_q = sum([(pos_q >= b).astype(jnp.int32) for b in bounds])
        ok = (doc_k[:cols] == doc_q) & (pos_k[:cols] <= pos_q)
        bias = jnp.concatenate([mem_bias, jnp.where(ok, 0.0, MASKED).astype(F32)], 0)
        biases.append(jnp.concatenate([bias, bias], 1))

    def score(i, p):
        w, lanes = 128 * (i + 2), slice(128 * p, 128 * p + 128)
        q01 = stacked_heads(qs[128 * i : 128 * i + 128, lanes])
        return dot(kall[0:w, lanes], q01, 1, 1)

    def soften(i, p, s):
        s = s + biases[i]
        e = jnp.exp(s - jnp.max(s, 0, keepdims=True))
        pr = (e * (1.0 / jnp.sum(e, 0, keepdims=True))).astype(BF16)
        (p0, p1, p2, p3)[i][p] = pr
        return pr

    def mix(i, p, pr):
        w, lanes = 128 * (i + 2), slice(128 * p, 128 * p + 128)
        queries = slice(128 * i, 128 * i + 128)
        o = dot(vt[lanes, 0:w], pr).astype(BF16)
        mixed[128 * p : 128 * p + 64, queries] = o[:64, :128]
        mixed[128 * p + 64 : 128 * p + 128, queries] = o[64:, 128:]

    in_steps(
        [(i, p) for i in range(4) for p in range(H // 2)], (score, soften, mix)
    )
    ff = ffn_in.shape[1]
    k0 = 0.7978845608028654
    step = 512
    chunks = ff // step

    def top(block):
        at = slice(half * block, half * block + half)
        r = x[at, :].astype(F32) + dot(mixed[:, at], out_weight[...], 0, 0)
        resid[at, :] = r
        rhat, _ = norm_parts(r)
        n2[at, :] = (rhat * ffn_gain[...]).astype(BF16)

    def inner(block, j):
        if block == 0 and j == 1:
            top(1)
        return dot(n2[half * block : half * block + half, :], ffn_in[:, step * j : step * j + step])

    def gelu(block, j, v):
        at = (slice(half * block, half * block + half), slice(step * j, step * j + step))
        v2 = v * v
        h = 0.5 * jnp.tanh(v * (k0 + (0.044715 * k0) * v2)) + 0.5
        act[at] = (v * h).astype(BF16)
        w = v * (2.0 * k0 + (6.0 * 0.044715 * k0) * v2)
        dg[at] = (h + h * (1.0 - h) * w).astype(BF16)

    def bottom(block):
        at = slice(half * block, half * block + half)
        out[at, :] = (resid[at, :] + dot(act[at, :], ffn_out[...])).astype(BF16)

    top(0)
    held = None
    for n in range(2 * chunks + 1):
        now = None
        if n < 2 * chunks:
            now = inner(n // chunks, n % chunks)
        if held is not None:
            gelu(*held)
        if n == chunks + 1:
            bottom(0)
        held = (n // chunks, n % chunks, now)
    bottom(1)
    out_own[...] = out[part(place, half, True), :]


def write_body(
    place, out, wqs, mem, memory_cotangent, recv, write_pair, write_out, write_gate, write_gain, nall,
    send, keep, dwpair, dwquery, dblend, own_new, newmem, gain_out,
):
    c, ks = place[1], (send, keep)
    slots, width = wqs.shape
    o = out[...]
    wk = dot(o, write_pair[:, :width]).astype(BF16)
    wv = dot(o, write_pair[:, width:]).astype(BF16)
    mask = head_mask(slots, width)
    qbd = block_diagonal(wqs[...], mask)
    s = dot(qbd, wk, 1, 1)
    e = jnp.exp(s - jnp.max(s, -1, keepdims=True))
    pf = e * (1.0 / jnp.sum(e, -1, keepdims=True))
    pb = pf.astype(BF16)
    wmixed = diagonal_blocks(dot(pb, wv), mask).astype(BF16)
    update = dot(wmixed, write_out[...])
    update_low = update.astype(BF16)
    gate = jax.nn.sigmoid(dot(update_low, write_gate[...]))
    blended = mem[...].astype(F32) + gate * update
    bhat, br = norm_parts(blended)
    gain = write_gain[...]
    newmem[...] = (bhat * gain).astype(BF16)
    mhalf = slots // 2
    own_new[...] = newmem[part(place, mhalf, True), :]
    mc = whole_rows(place, memory_cotangent, recv, recv.shape[0] - mhalf, mhalf).astype(F32)
    d_blend, d_gain = norm_back(mc, bhat, br, gain)
    gain_out[...] = d_gain
    dblend[...] = d_blend
    d_gate_pre = (d_blend * update * gate * (1.0 - gate)).astype(BF16)
    d_update = (d_blend * gate + dot(d_gate_pre, write_gate[...], 1, 1)).astype(BF16)
    d_wmixed = dot(d_update, write_out[...], 1, 1).astype(BF16)
    emit_rows(dot(update_low, d_gate_pre, 0, 0), 32, ks, 128, c)
    emit_rows(dot(wmixed, d_update, 0, 0), 32, ks, 96, c)
    dbd = block_diagonal(d_wmixed, mask)
    dp = dot(dbd, wv, 1, 1)
    row = jnp.sum(pf * dp, -1, keepdims=True)
    ds = (pf * (dp - row)).astype(BF16)
    d_wquery = (diagonal_blocks(dot(ds, wk), mask) * 0.125).astype(BF16)
    dwquery[...] = d_wquery
    dwk = dot(ds, qbd, 0, 0).astype(BF16)
    dwv = dot(pb, dbd, 0, 0).astype(BF16)
    dwpair[:, :width] = dwk
    dwpair[:, width:] = dwv
    emit_rows(dot(nall[0:slots, :], d_wquery, 0, 0), 32, ks, 0, c)
    emit_rows(dot(o, dwk, 0, 0), 32, ks, 32, c)
    emit_rows(dot(o, dwv, 0, 0), 32, ks, 64, c)


def ffn_back_body(
    place, dwpair, write_pair, out_cotangent, recv, ffn_out, dg, act,
    send, keep, dout_out, dinner,
):
    c, ks = place[1], (send, keep)
    ff, width = ffn_out.shape
    deep = ff // GROUPS
    cot = whole_rows(place, out_cotangent, recv, 0, out_cotangent.shape[1])
    d_out = cot.astype(F32) + dot(dwpair[...], write_pair[...], 1, 1)
    dout_out[...] = d_out
    d_branch = d_out.astype(BF16)
    for j in range(ff // 512):
        cols = slice(512 * j, 512 * j + 512)
        d_act = dot(d_branch, ffn_out[cols, :], 1, 1).astype(BF16)
        dinner[:, cols] = (d_act.astype(F32) * dg[:, cols].astype(F32)).astype(BF16)
        emit_rows(
            dot(act[:, cols], d_branch, 0, 0), deep, ks, 0, c, 512 // (2 * deep) * j,
        )


def inner_back_body(
    place, dinner, n2, ffn_in,
    send, keep, total,
):
    rows = ffn_in.shape[0] // GROUPS
    for j in range(ffn_in.shape[1] // 512):
        cols = slice(512 * j, 512 * j + 512)
        emit_rows(dot(n2[...], dinner[:, cols], 0, 0), rows, (send, keep), rows * j, place[1])
    total[...] = dot(dinner[...], ffn_in[...], 1, 1)


def resid_back_body(
    place, total, dout, resid, ffn_gain, mixed,
    send, keep, dresid, gain_out,
):
    rhat, rr = norm_parts(resid[...])
    d_norm, d_gain = norm_back(total[...], rhat, rr, ffn_gain[...])
    gain_out[...] = d_gain
    d = dout[...] + d_norm
    dresid[...] = d
    d_attn = d.astype(BF16)
    emit_rows(dot(mixed[...], d_attn), 32, (send, keep), 0, place[1])


def attn_back_body(
    place, qs, dresid, out_weight, vall, p3, kall, p2, p1, p0,
    dq_out, dk_out, dv_out, dk_ref, dv_ref, dqt_ref, dm, kt,
):
    dm[...] = dot(dresid[...].astype(BF16), out_weight[...], 1, 1).astype(BF16)
    kt[...] = kall[...].T
    probs = (p0, p1, p2, p3)

    def first(i, p):
        w, lanes = 128 * (i + 2), slice(128 * p, 128 * p + 128)
        dm01 = stacked_heads(dm[128 * i : 128 * i + 128, lanes])
        dv = dot(probs[i][p], dm01)
        if i == 3:
            dv_ref[0:w, lanes] = dv
        else:
            dv_ref[0:w, lanes] += dv
        return dot(vall[0:w, lanes], dm01, 1, 1)

    def second(i, p, dp):
        pf = probs[i][p].astype(F32)
        t = pf * dp
        return (t - pf * jnp.sum(t, 0, keepdims=True)).astype(BF16)

    def third(i, p, ds):
        w, lanes = 128 * (i + 2), slice(128 * p, 128 * p + 128)
        rows = slice(128 * i, 128 * i + 128)
        q01 = stacked_heads(qs[rows, lanes])
        dqt = (dot(kt[lanes, 0:w], ds) * 0.125).astype(BF16)
        dqt_ref[128 * p : 128 * p + 64, rows] = dqt[:64, :128]
        dqt_ref[128 * p + 64 : 128 * p + 128, rows] = dqt[64:, 128:]
        dk = dot(ds, q01)
        if i == 3:
            dk_ref[0:w, lanes] = dk
        else:
            dk_ref[0:w, lanes] += dk

    in_steps(
        [(i, p) for p in range(H // 2) for i in (3, 2, 1, 0)], (first, second, third)
    )
    dq_out[...] = dqt_ref[...].T
    dk_out[...] = dk_ref[...].astype(BF16)
    dv_out[...] = dv_ref[...].astype(BF16)


def input_back_body(
    place, nall, dq, dk, dv, pair_weight, query_weight, dwquery, write_query, x, mem, attn_gain,
    dresid, dblend, gain2, gain3, newmem, out,
    qsend, qkeep, ksend, kkeep, vsend, vkeep, gsend, gkeep, own_tok, own_mem, swap, gtok, gmem,
):
    c = place[1]
    rows, width = x.shape
    slots = mem.shape[0]
    half, mhalf = rows // 2, slots // 2
    na = nall[...]
    dqv = dq[...]
    emit_rows(dot(na[128:], dqv, 0, 0), 32, (qsend, qkeep), 0, c)
    emit_rows(dot(na, dk[...], 0, 0), 32, (ksend, kkeep), 0, c)
    emit_rows(dot(na, dv[...], 0, 0), 32, (vsend, vkeep), 0, c)
    d_all = dot(dk[...], pair_weight[:, :width], 1, 1)
    d_all = d_all + dot(dv[...], pair_weight[:, width:], 1, 1)
    d_nx = d_all[128:] + dot(dqv, query_weight[...], 1, 1)
    d_nm = d_all[:slots] + dot(dwquery[...], write_query[...], 1, 1)
    gain = attn_gain[...]
    xhat, xr = norm_parts(x[...].astype(F32))
    d_x, g_x = norm_back(d_nx, xhat, xr, gain)
    mhat, mr = norm_parts(mem[...].astype(F32))
    d_m, g_m = norm_back(d_nm, mhat, mr, gain)
    gains = jnp.concatenate(
        [g_x + g_m, gain2[...], gain3[...], jnp.zeros((13, width), F32)], 0
    ).astype(BF16)
    for one in (gsend, gkeep):
        one[...] = jnp.broadcast_to(gains, (GROUPS // 2, 16, width))
    gtok[...] = dresid[...] + d_x
    gmem[...] = dblend[...] + d_m
    own_tok[...] = gtok[part(place, half, True), :]
    own_mem[...] = gmem[part(place, mhalf, True), :]
    other = part(place, half, False)
    mother = part(place, mhalf, False)
    swap[0:half, :] = gtok[other, :].astype(BF16)
    swap[half : half + mhalf, :] = newmem[mother, :]
    swap[half + mhalf : half + 2 * mhalf, :] = gmem[mother, :].astype(BF16)
    swap[half + 2 * mhalf :, :] = out[other, :]


BIT = {"y": 0, "x": 2, "z": 3, "h": 4}


def other_of(axis, bit):
    return [(i, i ^ bit) for i in range(lax.axis_size(axis))]


def exchanged(send, label):
    if label == "y":
        return lax.ppermute(send, "seq", other_of("seq", 1))
    return lax.ppermute(send, "seg", other_of("seg", {"x": 2, "z": 4, "h": 8, "c": 1}[label]))


class Stream:
    def __init__(self, keep, recv, dims, start, rows):
        self.keep, self.recv, self.dims, self.start, self.rows = keep, recv, dims, start, rows


def stage(streams, labels, joined=False, deps=(), tail=False):
    ins = []
    index = {}
    for s in streams:
        for arr in (s.keep, s.recv):
            if id(arr) not in index:
                index[id(arr)] = len(ins)
                ins.append(("v", arr))
    n_arrays = len(ins)
    ins += [("d", d) for d in deps]
    width = streams[0].keep.shape[-1]
    shapes, new_dims, new_rows = [], [], []
    for s, label in zip(streams, labels):
        rows = s.rows // 2 if label == "y" else s.rows
        dims = s.dims.replace(label, "")
        new_dims.append(dims)
        new_rows.append(rows)
        shapes.append((2,) * len(dims) + (rows, width))
    if joined:
        shapes = [(sum(new_rows), width)]
    if tail:
        shapes = shapes[:-2] + [shapes[-2][:-2] + (new_rows[-2] + new_rows[-1], width)]
    outs = []
    for shape in shapes:
        outs += [(shape, BF16)] * 2

    def body(place, *refs):
        given, made = refs[:n_arrays], refs[n_arrays:]

        def value(s, label, own, arr):
            bit = place[BIT[label]]
            bit = bit if own else 1 - bit
            where = []
            for d in s.dims:
                where.append(bit if d == label else slice(None))
            if label == "y":
                half = s.rows // 2
                where.append(pl.ds(pl.multiple_of(s.start + bit * half, 16), half))
            else:
                where.append(slice(s.start, s.start + s.rows))
            return given[index[id(arr)]][tuple(where) + (slice(None),)].astype(F32)

        for own in (False, True):
            at = 0
            for k, (s, label) in enumerate(zip(streams, labels)):
                total = (value(s, label, own, s.keep) + value(s, label, own, s.recv)).astype(BF16)
                last = tail and k == len(streams) - 1
                target = made[(0 if joined else 2 * (k - last)) + (0 if own else 1)]
                if joined:
                    target[at : at + new_rows[k], :] = total
                    at += new_rows[k]
                elif last:
                    target[..., new_rows[k - 1] :, :] = total
                elif tail and k == len(streams) - 2:
                    target[..., : new_rows[k], :] = total
                else:
                    target[...] = total

    results = call(body, ins, outs, flops=10**6, nbytes=10**6)
    if joined:
        return results[0], results[1]
    if tail:
        new_rows = new_rows[:-2] + [new_rows[-2] + new_rows[-1]]
    return [
        (results[2 * k], results[2 * k + 1], new_dims[k], n) for k, n in enumerate(new_rows)
    ]


def added(keep, recv, deps=()):
    def body(place, keep, recv, total):
        total[...] = (keep[...].astype(F32) + recv[...].astype(F32)).astype(BF16)

    (total,) = call(
        body,
        [("v", keep), ("v", recv)] + [("d", d) for d in deps],
        [(keep.shape, BF16)],
        flops=10**6, nbytes=10**6,
    )
    return total


class Late:
    def __init__(self, pairs, order):
        flat = lambda a: a.reshape(-1, a.shape[2])
        self.arrays = [(flat(keep), flat(recv), [keep.shape[1]]) for keep, recv in pairs]
        self.order, self.dims = order, "hzx"

    def joined(self, other):
        self.arrays = self.arrays + other.arrays
        return self

    def next(self, deps=()):
        label = self.order[3 - len(self.dims)]
        at = self.dims.index(label)
        count = 1 << at
        plan, target = [], 0
        for array, (_, _, pieces) in enumerate(self.arrays):
            source = 0
            for rows in pieces:
                size = rows << (len(self.dims) - 1 - at)
                for b in range(count):
                    plan.append((array, source + 2 * b * size, target + b * size, size))
                source += 2 * count * size
                target += count * size

        def body(place, *refs):
            bit = place[BIT[label]]
            for out, b in ((refs[-1], 1 - bit), (refs[-2], bit)):
                for array, start, to, size in plan:
                    rows = pl.ds(pl.multiple_of(start + b * size, 16), size)
                    out[to : to + size, :] = (
                        refs[2 * array][rows, :].astype(F32)
                        + refs[2 * array + 1][rows, :].astype(F32)
                    ).astype(BF16)

        ins = [("v", a) for keep, recv, _ in self.arrays for a in (keep, recv)]
        ins += [("d", d) for d in deps]
        width = self.arrays[0][0].shape[1]
        keep, send = call(body, ins, [((target, width), BF16)] * 2, flops=10**6, nbytes=10**6)
        pieces = sum([p for _, _, p in self.arrays], [])
        self.arrays = [(keep, exchanged(send, label), pieces)]
        self.dims = self.dims.replace(label, "")


def in_hbm(a):
    return pltpu.with_memory_space_constraint(a, pltpu.HBM)


def packed(body_rows, extra_rows):
    half, width = body_rows.shape[1:]
    extra = extra_rows.shape[1]

    def kernel(a, b, o, sem):
        other = 1 - lax.axis_index("seq")
        copies = [
            pltpu.make_async_copy(a.at[other], o.at[0:half], sem.at[0]),
            pltpu.make_async_copy(b.at[other], o.at[half:], sem.at[1]),
        ]
        for copy in copies:
            copy.start()
        for copy in copies:
            copy.wait()

    return pl.pallas_call(
        kernel,
        out_shape=pltpu.VMEM((half + extra, width), body_rows.dtype),
        in_specs=[pl.BlockSpec(memory_space=pltpu.HBM)] * 2,
        out_specs=pl.BlockSpec(memory_space=pltpu.VMEM),
        scratch_shapes=[pltpu.SemaphoreType.DMA((2,))],
        compiler_params=pltpu.CompilerParams(vmem_limit_bytes=4 * 1024 * 1024),
    )(in_hbm(body_rows), in_hbm(extra_rows))


def assembled(own, recv, dtypes, deps=()):
    width = own[0].shape[1]

    def body(place, *refs):
        n = len(own)
        start = 0
        for mine, out in zip(refs[:n], refs[n + 1 :]):
            rows = mine.shape[0]
            out[place[0]] = mine[...].astype(out.dtype)
            out[1 - place[0]] = refs[n][start : start + rows, :].astype(out.dtype)
            start += rows

    return call(
        body,
        [("v", a) for a in own] + [("v", recv)] + [("d", d) for d in deps],
        [((2,) + a.shape, d) for a, d in zip(own, dtypes)],
        flops=10**6, nbytes=10**6, home=False,
    )


def fetched_weights(weights, tokens, gain):
    half, width = tokens.shape[1:]
    n = len(weights)

    def kernel(tokens, gain, *refs):
        y = lax.axis_index("seq")
        own, sem = refs[-2], refs[-1]
        copies = [pltpu.make_async_copy(tokens.at[y], own, sem.at[n])]
        order = [n - 2, n - 1] + list(range(n - 2))
        waits = {k: pltpu.make_async_copy(refs[k], refs[n + k], sem.at[k]) for k in order}
        copies[0].start()
        for k in order:
            waits[k].start()
        x_ref, n_ref, q_ref, k_ref, v_ref = refs[2 * n : 2 * n + 5]
        copies[0].wait()
        x_ref[...] = own[...]
        xhat, _ = norm_parts(own[...].astype(F32))
        nx = (xhat * gain[...]).astype(BF16)
        n_ref[...] = nx
        waits[n - 2].wait()
        q_ref[...] = (dot(nx, refs[2 * n - 2][...]) * 0.125).astype(BF16)
        waits[n - 1].wait()
        k_ref[...] = dot(nx, refs[2 * n - 1][:, :width]).astype(BF16)
        v_ref[...] = dot(nx, refs[2 * n - 1][:, width:]).astype(BF16)
        for k in order[2:]:
            waits[k].wait()

    one = pltpu.VMEM((half, width), BF16)
    results = pl.pallas_call(
        kernel,
        out_shape=[pltpu.VMEM(a.shape, a.dtype) for a in weights] + [one] * 5,
        in_specs=[pl.BlockSpec(memory_space=pltpu.HBM), pl.BlockSpec(memory_space=pltpu.VMEM)]
        + [pl.BlockSpec(memory_space=pltpu.HBM)] * n,
        out_specs=[pl.BlockSpec(memory_space=pltpu.VMEM)] * (n + 5),
        scratch_shapes=[pltpu.VMEM((half, width), BF16), pltpu.SemaphoreType.DMA((n + 1,))],
        compiler_params=pltpu.CompilerParams(vmem_limit_bytes=8 * 1024 * 1024),
        cost_estimate=pl.CostEstimate(flops=10**9, bytes_accessed=10**7, transcendentals=0),
    )(in_hbm(tokens), gain, *[in_hbm(a) for a in weights])
    return results[:n], results[n:]


def reduced_any(keep, send, pieces):
    groups = lax.axis_size("seg")
    c = lax.axis_index("seg") % 2
    first = jnp.where(c == 0, keep, send)
    second = jnp.where(c == 0, send, keep)
    total = jnp.stack([first, second], 1)
    total = total.reshape((GROUPS,) + keep.shape[1:])
    fine = groups // GROUPS
    parts = []
    at = 0
    for rows, shared in pieces:
        piece = total[:, at : at + rows]
        if shared:
            piece = jnp.broadcast_to(piece[:, None], (GROUPS, fine) + piece.shape[1:])
        else:
            piece = piece.reshape(GROUPS, fine, rows // fine, piece.shape[2])
        parts.append(piece.reshape(groups, -1, piece.shape[-1]))
        at += rows
    total = jnp.concatenate(parts, 1)
    total = lax.psum_scatter(total.astype(F32), "seg", scatter_dimension=0, tiled=True)[0]
    return lax.psum(total, "seq")


def final_parts(one, two, ff):
    ours, theirs, split = one
    t2, o2 = two
    width = t2.shape[-1]
    r = width // GROUPS
    n = ff // 512
    count = len(ours)
    shapes = [
        (r, width), (r, 2 * width), (r, width), (r, ff), (ff // GROUPS, width),
        (r, width), (r, 2 * width), (r, width), (r, width), (r,), (r,), (r,),
    ]

    def body(place, *refs):
        t2, o2, gq, gp, go, gfi, gfo, gwq, gwp, gwo, gwg, g0, g1, g2, full = refs[2 * count :]
        y = place[0]
        at = start = 0
        for rows in split:
            half = rows // 2
            for ref, index in ((refs[0], y), (refs[1], 1 - y)):
                full[pl.ds(pl.multiple_of(start + index * half, 16), half), :] = ref[
                    at : at + half, :
                ].astype(F32)
            at += half
            start += rows
        total = (t2[...].astype(F32) + o2[...].astype(F32))
        gq[...] = total[0:r, :]
        gp[:, :width] = total[r : 2 * r, :]
        gp[:, width:] = total[2 * r : 3 * r, :]
        seg = lax.axis_index("seg")
        gains = pltpu.roll(total[3 * r : 3 * r + 8, :], (width - seg * r) % width, 1)
        for k, ref in enumerate((g0, g1, g2)):
            ref[...] = gains[k, :r]
        gwq[...] = full[0:r, :]
        gwp[:, :width] = full[r : 2 * r, :]
        gwp[:, width:] = full[2 * r : 3 * r, :]
        gwo[...] = full[3 * r : 4 * r, :]
        gwg[...] = full[4 * r : 5 * r, :]
        for j in range(n):
            gfi[:, 512 * j : 512 * j + 512] = full[(5 + j) * r : (6 + j) * r, :]
        gfo[...] = full[(5 + n) * r : (5 + n) * r + ff // GROUPS, :]
        go[...] = full[(5 + n) * r + ff // GROUPS :, :]

    return call(
        body, [("v", a) for a in (*ours, *theirs, t2, o2)], [(s, F32) for s in shapes],
        scratch=[((sum(split), width), F32)], flops=10**6, nbytes=10**6, home=False,
    )


def shards(
    tokens, memory, lengths, attn_gain, query_weight, pair_weight, out_weight, ffn_gain, ffn_in,
    ffn_out, write_query, write_pair, write_out, write_gate, write_gain, out_cotangent,
    memory_cotangent,
):
    half, width = tokens.shape[1:]
    mhalf = memory.shape[1]
    rows, slots, ff = 2 * half, 2 * mhalf, ffn_in.shape[1]
    padded = rows + 128
    groups = lax.axis_size("seg")
    recv_a = exchanged(packed(tokens, memory), "y")
    (
        memory, out_cotangent, memory_cotangent, out_weight, ffn_in, ffn_out, write_query,
        write_pair, write_out, write_gate, query_weight, pair_weight,
    ), own_rows = fetched_weights(
        (
            memory, out_cotangent, memory_cotangent, out_weight, ffn_in, ffn_out, write_query,
            write_pair, write_out, write_gate, query_weight, pair_weight,
        ),
        tokens, attn_gain[None],
    )
    ag, fg, wg = attn_gain[None], ffn_gain[None], write_gain[None]
    v = lambda *arrs: [("v", a) for a in arrs]

    def half_pack(place, a, b, pack):
        pack[0:half, :] = a[1 - place[0]]
        pack[half:, :] = b[1 - place[0]]

    (pack,) = call(
        half_pack, v(out_cotangent, memory_cotangent), [((half + mhalf, width), BF16)],
        flops=10**6, nbytes=10**6,
    )
    recv_b = exchanged(pack, "y")
    deps = lambda *arrs: [("d", a) for a in arrs]
    big = ((rows, width), BF16)
    wide = ((padded, width), BF16)
    deep = ((rows, ff), BF16)
    half_b = ((half, width), BF16)
    keep_send = lambda n: [((GROUPS // 2, n, width), BF16)] * 2
    small = ((slots, width), BF16)
    full_f = ((rows, width), F32)
    gain_row = ((1, width), F32)
    (
        x, mem, nall, qs, kall, vall, p0, p1, p2, p3, mixed, resid, n2, act, dg,
        out_own, out, wqs,
    ) = call(
        forward_body,
        [("s", lengths)] + v(*own_rows, memory, recv_a, ag, query_weight, pair_weight)
        + v(write_query, out_weight, fg, ffn_in, ffn_out),
        [big, small, wide, big, wide, wide]
        + [((H // 2, 128 * (i + 2), 256), BF16) for i in range(4)]
        + [big, full_f, big, deep, deep, half_b, big, small],
        scratch=[((width, padded), BF16)],
        flops=2 * 6 * 10**9, nbytes=20 * 10**6, limit=16,
    )
    send0, keep0, dwpair, dwquery, dblend, own_new, newmem, gain3 = call(
        write_body,
        v(out, wqs, mem, memory_cotangent, recv_b, write_pair, write_out, write_gate, wg, nall),
        [
            *keep_send(160), ((rows, 2 * width), BF16), small,
            ((slots, width), F32), ((mhalf, width), BF16), small, gain_row,
        ],
        flops=2 * 3 * 10**9, nbytes=10 * 10**6,
    )
    small_mesh = groups == GROUPS
    cube = lambda a: a.reshape((2, 2, 2) + a.shape[1:])
    pair = lambda keep, send: (cube(keep), cube(exchanged(send, "c")))
    deps0 = deps1 = []
    send1, keep1, dout, dinner = call(
        ffn_back_body,
        v(dwpair, write_pair, out_cotangent, recv_b, ffn_out, dg, act),
        [*keep_send(128), full_f, deep],
        flops=2 * 5 * 10**9, nbytes=20 * 10**6,
    )
    if small_mesh:
        k0, r0 = pair(keep0, send0)
        deps0 = deps(r0)
    send4, keep4, total = call(
        inner_back_body, v(dinner, n2, ffn_in) + deps0, [*keep_send(128), full_f],
        flops=10**9, nbytes=20 * 10**6,
    )
    if small_mesh:
        k1, r1 = pair(keep1, send1)
        deps0 = deps(r1)
    send3, keep3, dresid, gain2 = call(
        resid_back_body, v(total, dout, resid, fg, mixed) + deps0,
        [*keep_send(32), full_f, gain_row],
        flops=10**8, nbytes=10**6,
    )
    orders = ("xyz", "yzx", "zxy")
    late_orders = ("xz", "zx")

    def moved(parts, labels):
        return [
            Stream(keep, exchanged(send, label), dims, 0, r)
            for label, (keep, send, dims, r) in zip(labels, parts)
        ]

    nth = lambda these, step: [o[step] for o in these]
    if small_mesh:
        k4, r4 = pair(keep4, send4)
        k3, r3 = pair(keep3, send3)
        streams = [
            Stream(k0, r0, "hzx", 0, 160), Stream(k4, r4, "hzx", 0, 128),
            Stream(k1, r1, "hzx", 0, 128), Stream(k3, r3, "hzx", 0, 32),
        ]
        parts = stage_joined(streams, nth(orders, 0), [])
        deps1 = deps(parts[0][0])
        first = moved(parts, nth(orders, 0))
    dq, dk, dv = call(
        attn_back_body,
        v(qs, dresid, out_weight, vall, p3, kall, p2, p1, p0) + deps1,
        [big, wide, wide],
        scratch=[((padded, width), F32)] * 2 + [big, big, ((width, padded), BF16)],
        flops=2 * 6 * 10**9, nbytes=20 * 10**6,
    )
    *grads2, own_tok, own_mem, swap = call(
        input_back_body,
        v(
            nall, dq, dk, dv, pair_weight, query_weight, dwquery, write_query, x, mem, ag, dresid,
            dblend, gain2, gain3, newmem, out,
        ),
        [
            *keep_send(32), *keep_send(32), *keep_send(32), *keep_send(16), ((half, width), F32), ((mhalf, width), F32),
            ((2 * half + 2 * mhalf, width), BF16),
        ],
        scratch=[((rows, width), F32), ((slots, width), F32)],
        flops=2 * 3 * 10**9, nbytes=20 * 10**6,
    )
    r = width // groups
    if small_mesh:
        def each(streams, labels, deps=()):
            results = []
            for stream, label in zip(streams, labels):
                results += stage([stream], [label], deps=list(deps))
            return moved(results, labels)

        second = each(first, nth(orders, 1), [swap])
        pieces = [(grads2[k + 1], exchanged(grads2[k], "c")) for k in range(0, 8, 2)]
        by_x, by_z = Late(pieces[:2], "xzh"), Late(pieces[2:], "zxh")
        by_x.next()
        by_z.next()
        third = each(second, nth(orders, 2))
        behind = [stream.keep for stream in third]
        by_x.next(behind)
        by_z.next(behind)
        keep, send = stage(third, "hhh", joined=True)
        swapped = exchanged(swap, "y")
        by_x.joined(by_z).next([keep])
        t1 = added(keep, exchanged(send, "h"))
        one, two = [t1], [exchanged(t1, "y")]
        t2 = added(*by_x.arrays[0][:2])
        o2 = exchanged(t2, "y")
        gq, gp, go, gfi, gfo, gwq, gwp, gwo, gwg, *gains = final_parts(
            (one, two, (160, 128, 160)), (t2, o2), ff
        )
    else:
        w = width // GROUPS
        w0 = reduced_any(keep0, send0, [(w, False)] * 5)
        gfo = reduced_any(keep1, send1, [(ff // GROUPS, False)])
        w1 = reduced_any(keep4, send4, [(w, False)] * (ff // 512))
        w2 = jnp.concatenate(
            [
                reduced_any(grads2[k + 1], grads2[k], [(w, False)] if k < 6 else [(16, True)])
                for k in range(0, 8, 2)
            ],
            0,
        )
        go = reduced_any(keep3, send3, [(w, False)])
        cut = lambda a, at, n: jnp.concatenate(
            [a[(at + i) * r : (at + i + 1) * r] for i in range(n)], 1
        )
        gq, gp = cut(w2, 0, 1), cut(w2, 1, 2)
        gfi = cut(w1, 0, ff // 512)
        gwq, gwp, gwo, gwg = cut(w0, 0, 1), cut(w0, 1, 2), cut(w0, 3, 1), cut(w0, 4, 1)
        at = lax.axis_index("seg") * r
        gains = [lax.dynamic_slice_in_dim(w2[3 * r + i], at, r, 0) for i in range(3)]
    if not small_mesh:
        swapped = exchanged(swap, "y")
    tok_both, new_both, mem_both, out_both = assembled(
        [own_tok, own_new, own_mem, out_own], swapped, [F32, BF16, F32, BF16]
    )
    return (
        out_both, new_both, tok_both, mem_both,
        gains[0], gq, gp, go, gains[1], gfi, gfo, gwq, gwp, gwo, gwg, gains[2],
    )


def stage_joined(streams, labels, deps):
    return stage(streams, list(labels) + [labels[-1]], tail=True, deps=deps)


def solution(mesh):
    row = P("seg", "seq", None)
    grad = P("seg", None)
    in_specs = (row, row, P("seg", None)) + (P(),) * 12 + (row, row)
    out_specs = (row, row, row, row, P("seg"), grad, grad, grad, P("seg")) + (grad,) * 6 + (P("seg"),)
    return jax.shard_map(shards, mesh=mesh, in_specs=in_specs, out_specs=out_specs, check_vma=False)
```
